256 devices in a mesh: gx: 8 (over x, core), gy: 32 (over y, z).
Axes of the slice: x: 4, y: 4, z: 8, core: 2. Of those that a mesh axis runs over, the one named last changes fastest.
Arguments:
- salinity: float32 [4, 2048, 8192], P(None, 'gx', 'gy'), may hold values from -8 to 8, as said below
Outputs:
- decomposed: float32 [4, 2048, 8192], P(None, 'gx', 'gy')
The draws below stay inside these ranges and needn't reach their ends.
Inputs may be any that keep to these rules, and one draw needn't show every extreme that they name: salinity anomaly of a cell, in practical salinity units.
All inputs are finite; a program needn't handle non-finite values.
Results may differ from the reference program's by a relative error of at most 0.0003.
Values sent between devices are 32-bit elements; how exact they have to be, the bound alone decides.
A program may use at most 128 MiB of HBM per device.

```python
import jax
import jax.numpy as jnp
import numpy as np
from jax import lax

DEPTH = 4
LEVELS = 3
NX = 2048
NY = 8192


def draw_salinity(key, part):
    key = jax.random.fold_in(key, 11)
    key_noise = jax.random.fold_in(key, 0)
    noise = jax.random.normal(key_noise, (DEPTH, NX, NY), jnp.float32)
    return jnp.clip(noise, -6.0, 6.0)


def setup_inputs(seed: int = 0) -> dict:
    seeds = jax.random.split(jax.random.key(seed), 2)
    salinity = draw_salinity(jax.random.fold_in(seeds[1], 71), 0)
    return {"salinity": salinity}


smooth_length = 64.0


def line_constants():
    square = smooth_length * smooth_length
    off_size = square - 1.0 / 3.0
    inner_diag = (4.0 / 3.0 + 2.0 * square) / off_size
    end_diag = (2.0 / 3.0 + square) / off_size
    return inner_diag, end_diag, square / (off_size * off_size)


def pivots(count):
    inner_diag, end_diag, _ = line_constants()
    entries = [end_diag]
    for position in range(1, count):
        diagonal = end_diag if position == count - 1 else inner_diag
        entries.append(diagonal - 1.0 / entries[-1])
    return np.array(entries)


def checker(row_ids, col_ids):
    parity = (row_ids[:, None] + col_ids[None, :]) % 2
    return 1.0 - 2.0 * parity.astype(jnp.float32)


def shaped(vector, axis, rank_count):
    target = [1] * rank_count
    target[axis] = -1
    return vector.reshape(target)


def interpolate(field, axis, count, start, total):
    middle = lax.slice_in_dim(field, 1, count + 2, axis=axis)
    before = lax.slice_in_dim(field, 0, count + 1, axis=axis)
    after = lax.slice_in_dim(field, 2, count + 3, axis=axis)
    places = jnp.arange(1, count + 2, dtype=jnp.int32)
    global_ids = start + places - 2
    last_node = global_ids == total - 1
    w_left = jnp.where(last_node, 1.0, 0.5).astype(jnp.float32)
    w_right = jnp.where(last_node, 0.0, 0.5).astype(jnp.float32)
    is_odd = (places % 2) == 1
    blended = shaped(w_left, axis, field.ndim) * before + shaped(w_right, axis, field.ndim) * after
    inner = jnp.where(shaped(is_odd, axis, field.ndim), blended, middle)
    head = lax.slice_in_dim(field, 0, 1, axis=axis)
    tail = lax.slice_in_dim(field, count + 2, count + 3, axis=axis)
    return jnp.concatenate([head, inner, tail], axis=axis)


def valid_mask(count, start, total):
    global_ids = start + jnp.arange(count + 3, dtype=jnp.int32) - 2
    return ((global_ids >= 0) & (global_ids < total)).astype(jnp.float32)


def restrict(field, axis, count, start, total):
    global_ids = start + jnp.arange(count + 1, dtype=jnp.int32) - 1
    weight = jnp.where((global_ids == 0) | (global_ids == total - 1), 2.0, 4.0).astype(jnp.float32)
    mass = (lax.slice_in_dim(field, 0, count + 1, axis=axis)
            + shaped(weight, axis, field.ndim) * lax.slice_in_dim(field, 1, count + 2, axis=axis)
            + lax.slice_in_dim(field, 2, count + 3, axis=axis)) / 6.0
    centre = lax.slice_in_dim(mass, 1, count + 1, 2, axis=axis)
    lower = lax.slice_in_dim(mass, 0, count, 2, axis=axis)
    upper = lax.slice_in_dim(mass, 2, count + 1, 2, axis=axis)
    coarse_ids = start // 2 + jnp.arange(count // 2, dtype=jnp.int32)
    w_lower = jnp.where(coarse_ids == 0, 0.0, 0.5).astype(jnp.float32)
    w_upper = jnp.where(2 * coarse_ids + 1 == total - 1, 1.0, 0.5).astype(jnp.float32)
    return centre + shaped(w_lower, axis, field.ndim) * lower + shaped(w_upper, axis, field.ndim) * upper


def level_terms(halo_field, ax_rows, ax_cols, row_count, col_count, row_start, col_start, row_total, col_total):
    window = lax.slice_in_dim(halo_field, 0, row_count + 3, axis=ax_rows)
    window = lax.slice_in_dim(window, 0, col_count + 3, axis=ax_cols)
    along_cols = interpolate(window, ax_cols, col_count, col_start, col_total)
    interpolant = interpolate(along_cols, ax_rows, row_count, row_start, row_total)
    masking = (shaped(valid_mask(row_count, row_start, row_total), ax_rows, window.ndim)
               * shaped(valid_mask(col_count, col_start, col_total), ax_cols, window.ndim))
    detail = (window - interpolant) * masking
    load = restrict(detail, ax_rows, row_count, row_start, row_total)
    load = restrict(load, ax_cols, col_count, col_start, col_total)
    own = lax.slice_in_dim(detail, 2, row_count + 2, axis=ax_rows)
    own = lax.slice_in_dim(own, 2, col_count + 2, axis=ax_cols)
    coarse = lax.slice_in_dim(halo_field, 2, row_count + 2, 2, axis=ax_rows)
    coarse = lax.slice_in_dim(coarse, 2, col_count + 2, 2, axis=ax_cols)
    return own, coarse, load


def thomas(rhs_field, pivot_table, axis):
    moved = jnp.moveaxis(rhs_field, axis, 0)
    pivot_vals = jnp.asarray(pivot_table, jnp.float32)
    pivot_prev = jnp.concatenate([jnp.ones((1,), jnp.float32), pivot_vals[:-1]])

    def forward(previous, entries):
        line_row, divisor = entries
        result = line_row - previous / divisor
        return result, result

    _, upward = lax.scan(forward, jnp.zeros_like(moved[0]), (moved, pivot_prev))

    def backward(following, entries):
        line_row, pivot_one = entries
        result = (line_row - following) / pivot_one
        return result, result

    _, solved = lax.scan(backward, jnp.zeros_like(moved[0]), (upward, pivot_vals), reverse=True)
    return jnp.moveaxis(solved, 0, axis)


def reference(salinity):
    _, _, line_factor = line_constants()

    def one_layer(layer):
        field = layer
        for level_step in range(LEVELS):
            stride = 2 ** level_step
            nodes = field[::stride, ::stride]
            row_count, col_count = nodes.shape
            padded = jnp.pad(nodes, 2)
            own, coarse, load = level_terms(padded, 0, 1, row_count, col_count, 0, 0, row_count, col_count)
            signs = checker(jnp.arange(row_count // 2, dtype=jnp.int32), jnp.arange(col_count // 2, dtype=jnp.int32))
            solved = thomas(line_factor * signs * load, pivots(row_count // 2), 0)
            solved = thomas(solved, pivots(col_count // 2), 1)
            solved = signs * solved
            updated = own.at[::2, ::2].set(coarse + solved)
            field = field.at[::stride, ::stride].set(updated)
        return field

    return lax.map(one_layer, salinity)
```

```python
import functools

import jax
import jax.numpy as jnp
import numpy as np
from jax import lax
from jax.experimental import pallas as pl
from jax.experimental.pallas import tpu as pltpu
from jax.sharding import PartitionSpec as P

LEVELS = 3
DEPTH = 4
LENGTH = 64.0
MESH = pl.DeviceIdType.MESH
TABLE_LANES = 384


def padded_rows(count):
    return count + 8


def padded_lanes(count):
    return (count // 128 + 1) * 128 if count >= 128 else 128


def solver_line(count):
    off = 1.0 / (3.0 * LENGTH) - LENGTH
    inner = 4.0 / (3.0 * LENGTH) + 2.0 * LENGTH
    end = 2.0 / (3.0 * LENGTH) + LENGTH
    diag = np.full(count, inner)
    diag[0] = diag[-1] = end
    q = np.ones(count)
    p = np.ones(count)
    q[1] = -diag[0] / off
    p[-2] = -diag[-1] / off
    for i in range(1, count - 1):
        q[i + 1] = -(diag[i] * q[i]) / off - q[i - 1]
        j = count - 1 - i
        p[j - 1] = -(diag[j] * p[j]) / off - p[j + 1]
    return q, p, diag[0] * p[0] + off * p[1]


def load_block(total, coarse_ids, fine_ids):
    out = np.zeros((len(coarse_ids), len(fine_ids)))

    def mass(i, j):
        if i < 0 or i >= total or j < 0 or j >= total:
            return 0.0
        if i == j:
            return (2.0 if i in (0, total - 1) else 4.0) / 6.0
        return 1.0 / 6.0 if abs(i - j) == 1 else 0.0

    for a, k in enumerate(coarse_ids):
        if k < 0 or k >= total // 2:
            continue
        upper = 1.0 if 2 * k + 1 == total - 1 else 0.5
        for b in range(max(0, 2 * k - 2 - fine_ids[0]), min(len(fine_ids), 2 * k + 3 - fine_ids[0])):
            j = fine_ids[b]
            out[a, b] = mass(2 * k, j) + 0.5 * mass(2 * k - 1, j) + upper * mass(2 * k + 1, j)
    return out


def line_tables(total, tiles):
    n = total // tiles
    h = n // 2
    coarse = total // 2
    q, p, w = solver_line(coarse)
    local, functional, carry, weight, select = [], [], [], [], []
    for t in range(tiles):
        first = t * h
        last_tile = t == tiles - 1
        ids = np.arange(first, first + h + 1)
        if last_tile:
            ids[h] = ids[h - 2]
        window = np.arange(first - 1, first + h + 2)
        load = load_block(total, window, np.arange(t * n, t * n + n + 1))
        inside = (window >= 0) & (window < coarse)
        safe = np.clip(window, 0, coarse - 1)
        low = np.minimum(ids[:, None], safe[None, :])
        high = np.maximum(ids[:, None], safe[None, :])
        green = np.where(inside[None, :], q[low] * p[high] / w, 0.0)
        local.append(green @ load)
        q_end = q[min(first + h, coarse - 1)]
        to_right = (np.where(inside, q[safe] / q_end, 0.0)) @ load
        to_left = (np.where(inside, p[safe] / p[first], 0.0)) @ load
        to_right[n] = 0.0
        to_left[0] = 0.0
        functional.append(np.stack([to_right, to_left]))
        carry.append(np.stack([p[ids] / p[first], q[ids] / q_end]))
        weights = np.zeros((2, tiles))
        for k in range(1, tiles):
            s = (t - k) % tiles
            if s < t:
                weights[0, k] = q[(s + 1) * h] * p[first] / w
            else:
                weights[1, k] = q_end * p[s * h] / w
        weight.append(weights)
        pick = np.zeros((n + 1, h + 1))
        pick[2 * np.arange(h), np.arange(h)] = 1.0
        pick[n - 4 if last_tile else n, h] = 1.0
        select.append(pick)
    return [np.stack(item) for item in (local, functional, carry, weight, select)]


def fit(array, shape):
    out = np.zeros(array.shape[: array.ndim - len(shape)] + tuple(shape))
    out[tuple(slice(0, size) for size in array.shape)] = array
    return out


@functools.lru_cache(maxsize=None)
def tables(nx, ny, gx, gy):
    row_mats, col_mats, selects = [], [], []
    row_vecs = np.zeros((gx, LEVELS, 8, TABLE_LANES))
    col_vecs = np.zeros((gy, LEVELS, 8, TABLE_LANES))
    row_w = np.zeros((gx, LEVELS, 2, gx))
    col_w = np.zeros((gy, LEVELS, 2, gy))
    for level in range(LEVELS):
        for vecs, ws, total, tiles in ((row_vecs, row_w, nx >> level, gx), (col_vecs, col_w, ny >> level, gy)):
            n = total // tiles
            h = n // 2
            local, functional, carry, weight, select = line_tables(total, tiles)
            vecs[:, level, 0:2, : n + 1] = functional
            vecs[:, level, 2:4, : h + 1] = carry
            ws[:, level] = weight
            if vecs is row_vecs:
                row_mats.append(fit(local, (padded_rows(h), padded_rows(n))))
            else:
                joined = np.concatenate([local, functional], axis=1).transpose(0, 2, 1)
                shape = (padded_lanes(n), padded_lanes(h))
                col_mats.append(fit(joined, shape))
                selects.append(fit(select[[0, -1]], shape))
    as32 = lambda item: np.ascontiguousarray(item, np.float32)
    return (
        [as32(m) for m in row_mats],
        [as32(m) for m in col_mats],
        [as32(m) for m in selects],
        as32(row_vecs),
        as32(col_vecs),
        as32(row_w.reshape(-1)),
        as32(col_w.reshape(-1)),
    )


def dot(a, b, dims=((1,), (0,))):
    return lax.dot_general(
        a, b, (dims, ((), ())), precision=lax.Precision.HIGHEST, preferred_element_type=jnp.float32
    )


def iota(shape, dim):
    return lax.broadcasted_iota(jnp.int32, shape, dim)


def detail(u):
    rows, lanes = u.shape
    odd_lane = iota(u.shape, 1) % 2 == 1
    odd_row = iota(u.shape, 0) % 2 == 1
    along = jnp.where(odd_lane, 0.5 * (pltpu.roll(u, 1, 1) + pltpu.roll(u, lanes - 1, 1)), u)
    both = jnp.where(odd_row, 0.5 * (pltpu.roll(along, 1, 0) + pltpu.roll(along, rows - 1, 0)), along)
    return u - both


def spread_matrix(count, lanes, stride, width):
    shape = (lanes, width)
    row = iota(shape, 0)
    return jnp.where((iota(shape, 1) == stride * row) & (row < count), 1.0, 0.0).astype(jnp.float32)


def kernel(gx_n, gy_n, n0, *refs):
    (sal, rm0, rm1, rm2, cm0, cm1, cm2, se0, se1, se2, row_vecs, col_vecs, row_w, col_w, out) = refs[:15]
    (u0, u1, u2, w0, w1, w2, out_v, tall_v, rmv0, rmv1, rmv2, cmv0, cmv1, cmv2, sev0, sev1, sev2, rv, cv,
     hrow, hcol, hcorner, hrow_in, hcol_in, hcorner_in,
     xs0, xs1, xs2, xr0, xr1, xr2, ys0, ys1, ys2, yr0, yr1, yr2,
     load_sem, halo_send, halo_recv, x_send, x_recv, y_send, y_recv, out_sem) = refs[15:]
    us, ws = (u0, u1, u2), (w0, w1, w2)
    row_mats, col_mats, selects = (rmv0, rmv1, rmv2), (cmv0, cmv1, cmv2), (sev0, sev1, sev2)
    xs, xr, ys, yr = (xs0, xs1, xs2), (xr0, xr1, xr2), (ys0, ys1, ys2), (yr0, yr1, yr2)
    gx, gy = lax.axis_index("gx"), lax.axis_index("gy")
    last_x, last_y = gx == gx_n - 1, gy == gy_n - 1
    is_last_col = (gy + 1) // gy_n

    loads = [pltpu.make_async_copy(sal, u0.at[:, pl.ds(0, n0), pl.ds(0, n0)], load_sem.at[0])]
    later = [(rv, row_vecs.at[gx]), (cv, col_vecs.at[gy])]
    for src, dst in zip((rm0, rm1, rm2), row_mats):
        later.append((dst, src.at[gx]))
    for src, dst in zip((cm0, cm1, cm2), col_mats):
        later.append((dst, src.at[gy]))
    for src, dst in zip((se0, se1, se2), selects):
        later.append((dst, src.at[is_last_col]))
    for i, (dst, src) in enumerate(later):
        loads.append(pltpu.make_async_copy(src, dst, load_sem.at[1 + i]))
    for copy in loads:
        copy.start()

    barrier = pltpu.get_barrier_semaphore()
    x_peers = [(lax.rem(gx + k, gx_n), gy) for k in range(1, gx_n)]
    y_peers = [(gx, lax.rem(gy + k, gy_n)) for k in range(1, gy_n)]
    up, left = lax.rem(gx + gx_n - 1, gx_n), lax.rem(gy + gy_n - 1, gy_n)
    greeted = x_peers + y_peers + [(lax.rem(gx + 1, gx_n), lax.rem(gy + 1, gy_n))]
    for peer in greeted:
        pl.semaphore_signal(barrier, inc=1, device_id=peer, device_id_type=MESH)

    loads[0].wait()
    edge = jnp.where(iota((DEPTH, n0), 1) == 0, 1.0, 0.0)
    depth_row = iota((DEPTH, n0), 0)
    hrow[...] = u0[:, 0, 0:n0]
    hcorner[...] = u0[:, 0, 0:128]
    first_cols = jnp.zeros((DEPTH, n0), jnp.float32)
    for d in range(DEPTH):
        first_cols += dot(jnp.where(depth_row == d, edge, 0.0), u0[d, 0:n0, 0:n0], ((1,), (1,)))
    hcol[...] = first_cols
    pl.semaphore_wait(barrier, len(greeted))
    halos = []
    for i, (src, dst, peer) in enumerate(
        ((hrow, hrow_in, (up, gy)), (hcol, hcol_in, (gx, left)), (hcorner, hcorner_in, (up, left)))
    ):
        copy = pltpu.make_async_remote_copy(
            src_ref=src, dst_ref=dst, send_sem=halo_send.at[i], recv_sem=halo_recv.at[i],
            device_id=peer, device_id_type=MESH,
        )
        copy.start()
        halos.append(copy)
    for copy in loads[1:]:
        copy.wait()
    for copy in halos:
        copy.wait_recv()
    lane0 = iota((n0, 128), 1) == 0
    first_row = iota((8, 1), 0) == 0
    cols_in = jnp.concatenate([hcol_in[...], jnp.zeros((4, n0), jnp.float32)], axis=0).T
    for d in range(DEPTH):
        own_alias = u0[d, 0:n0, n0 - 2 : n0 - 1]
        column = jnp.where(last_y, own_alias, cols_in[:, d : d + 1])
        u0[d, 0:n0, n0 : n0 + 128] = jnp.where(lane0, column, 0.0)
        row = jnp.where(last_x, u0[d, n0 - 2 : n0 - 1, 0:n0], hrow_in[d : d + 1, :])
        corner = jnp.where(
            last_y,
            row[:, n0 - 2 : n0 - 1],
            jnp.where(last_x, u0[d, n0 - 2 : n0 - 1, n0 : n0 + 1], hcorner_in[d : d + 1, 0:1]),
        )
        u0[d, n0 : n0 + 8, 0:n0] = jnp.where(first_row, row, 0.0)
        u0[d, n0 : n0 + 8, n0 : n0 + 128] = jnp.where(first_row & (iota((8, 128), 1) == 0), corner, 0.0)

    def send_all(peers, me, count, src, dst, send, recv):
        for k, peer in enumerate(peers):
            pltpu.make_async_remote_copy(
                src_ref=src.at[(me + k + 1) // count], dst_ref=dst.at[k], send_sem=send, recv_sem=recv,
                device_id=peer, device_id_type=MESH,
            ).start()

    def gather(buf, weights, base, count):
        right = jnp.zeros(buf.shape[1:], jnp.float32)
        left_sum = jnp.zeros(buf.shape[1:], jnp.float32)
        for k in range(1, count):
            part = buf[k - 1]
            right += weights[base + k] * part
            left_sum += weights[base + count + k] * part
        return right, left_sum

    for level in range(LEVELS):
        n = n0 >> level
        h = n // 2
        rows, lanes = padded_rows(n), padded_lanes(n)
        rows_c, lanes_c = padded_rows(h), padded_lanes(h)
        tall = padded_lanes(h)
        u, w = us[level], ws[level]
        col_mat, row_mat, select = col_mats[level][...], row_mats[level][...], selects[level][...]
        q_cols = rv[level, :, 0:rows if rows % 128 == 0 else padded_lanes(n)].T
        right_rows, left_rows = [], []
        for d in range(DEPTH):
            value = detail(u[d])
            w[d] = value
            right_rows.append(jnp.sum(value * q_cols[0:rows, 0:1], axis=0, keepdims=True))
            left_rows.append(jnp.sum(value * q_cols[0:rows, 1:2], axis=0, keepdims=True))
        xs[level][0] = jnp.concatenate(right_rows, axis=0)
        xs[level][1] = jnp.concatenate(left_rows, axis=0)
        send_all(x_peers, gx, gx_n, xs[level], xr[level], x_send.at[level], x_recv.at[level])

        base, cols_local = [], jnp.zeros((8, rows_c), jnp.float32)
        row8 = iota((8, lanes_c), 0)
        lane8 = iota((8, lanes_c), 1)
        is_tail = iota((rows_c, lanes_c), 0) == h
        for d in range(DEPTH):
            z = dot(row_mat, dot(w[d], col_mat))
            pick = ((row8 == d) & (lane8 == h + 1)) | ((row8 == 4 + d) & (lane8 == h + 2))
            cols_local += dot(jnp.where(pick, 1.0, 0.0), z, ((1,), (1,)))
            even = even_rows(tall_v, dot(u[d], select), rows_c)
            even = jnp.where(is_tail & last_x, even[h - 2 : h - 1, :], even)
            base.append(jnp.where(iota((rows_c, lanes_c), 1) <= h, z, 0.0) + even)
        if rows_c < tall:
            cols_local = jnp.concatenate([cols_local, jnp.zeros((8, tall - rows_c), jnp.float32)], axis=1)

        if level == 0:
            for d in range(DEPTH):
                for j in range(out_v.shape[1]):
                    out_v[d, j] = w0[d, 0:n0, 128 * j : 128 * j + 128]
        else:
            mat = spread_matrix(n, lanes, 1 << level, n0)
            for d in range(DEPTH):
                add_rows(out_v, d, dot(w[d, 0:n, :], mat), 1 << level)

        pltpu.make_async_copy(xr[level], xr[level], x_recv.at[level]).wait()
        a_right, a_left = gather(xr[level], row_w, (gx * LEVELS + level) * 2 * gx_n, gx_n)
        q_r, q_l = cv[level, 0:1, 0:lanes], cv[level, 1:2, 0:lanes]
        p_r, p_l = rv[level, 2:3, 0:tall], rv[level, 3:4, 0:tall]

        def line(value, functional):
            return jnp.sum(value * functional, axis=1, keepdims=True)

        ys[level][0] = cols_local[0:4] + line(a_right, q_r) * p_r + line(a_left, q_r) * p_l
        ys[level][1] = cols_local[4:8] + line(a_right, q_l) * p_r + line(a_left, q_l) * p_l
        send_all(y_peers, gy, gy_n, ys[level], yr[level], y_send.at[level], y_recv.at[level])

        carried = dot(jnp.concatenate([a_right, a_left], axis=0), col_mat)
        carried = jnp.where(iota((8, lanes_c), 1) <= h, carried, 0.0)
        py_r, py_l = cv[level, 2:3, 0:lanes_c], cv[level, 3:4, 0:lanes_c]
        shapes = jnp.concatenate([jnp.broadcast_to(py_r, (4, lanes_c)), jnp.broadcast_to(py_l, (4, lanes_c))], axis=0)
        own = jnp.concatenate([jnp.broadcast_to(p_r, (4, tall)), jnp.broadcast_to(p_l, (4, tall))], axis=0)
        other = jnp.concatenate([carried, shapes], axis=0)

        pltpu.make_async_copy(yr[level], yr[level], y_recv.at[level]).wait()
        c_right, c_left = gather(yr[level], col_w, (gy * LEVELS + level) * 2 * gy_n, gy_n)
        lhs = jnp.concatenate([own, c_right, c_left], axis=0).T[0:rows_c]
        for d in range(DEPTH):
            chosen = jnp.where(iota((16, lanes_c), 0) % 4 == d, other, 0.0)
            new = base[d] + dot(lhs, chosen)
            if level + 1 < LEVELS:
                us[level + 1][d] = new
            else:
                mat = spread_matrix(h, lanes_c, 2 << level, n0)
                add_rows(out_v, d, dot(new[0:h], mat), 2 << level)

    results = []
    for j in range(out_v.shape[1]):
        results.append(pltpu.make_async_copy(out_v.at[:, j], out.at[:, :, pl.ds(128 * j, 128)], out_sem.at[j]))
        results[-1].start()
    for i, copy in enumerate(halos):
        copy.wait_send()
    for level in range(LEVELS):
        pltpu.make_async_copy(xr[level], xr[level], x_send.at[level]).wait()
        pltpu.make_async_copy(yr[level], yr[level], y_send.at[level]).wait()
    for copy in results:
        copy.wait()


def even_rows(tall_v, value, rows_c):
    rows, lanes = value.shape
    half = rows // 2
    parts = []
    for j in range(lanes // 128):
        tall_v[j, 0:rows] = value[:, 128 * j : 128 * j + 128]
        part = tall_v[j, pl.ds(0, half, stride=2), :]
        parts.append(jnp.concatenate([part, jnp.zeros((rows_c - half, 128), jnp.float32)], axis=0))
    return jnp.concatenate(parts, axis=1)


def add_rows(ref, d, value, stride):
    place = pl.ds(0, value.shape[0], stride=stride)
    for j in range(ref.shape[1]):
        ref[d, j, place, :] = ref[d, j, place, :] + value[:, 128 * j : 128 * j + 128]


def shards(salinity):
    gx_n, gy_n = lax.axis_size("gx"), lax.axis_size("gy")
    _, nx, ny = salinity.shape
    n0 = nx
    row_mats, col_mats, selects, row_vecs, col_vecs, row_w, col_w = tables(nx * gx_n, ny * gy_n, gx_n, gy_n)
    scratch = []
    vmem = lambda *shape: pltpu.VMEM(shape, jnp.float32)
    sizes = [n0 >> level for level in range(LEVELS)]
    scratch += [vmem(DEPTH, padded_rows(n), padded_lanes(n)) for n in sizes]
    scratch += [vmem(DEPTH, padded_rows(n), padded_lanes(n)) for n in sizes]
    scratch += [vmem(DEPTH, n0 // 128, n0, 128), vmem(2, padded_rows(n0), 128)]
    for group in (row_mats, col_mats, selects):
        scratch += [vmem(*m.shape[1:]) for m in group]
    scratch += [vmem(*row_vecs.shape[1:]), vmem(*col_vecs.shape[1:])]
    scratch += [vmem(DEPTH, n0), vmem(DEPTH, n0), vmem(DEPTH, 128)] * 2
    scratch += [vmem(2, DEPTH, padded_lanes(n)) for n in sizes]
    scratch += [vmem(gx_n - 1, DEPTH, padded_lanes(n)) for n in sizes]
    scratch += [vmem(2, DEPTH, padded_lanes(n // 2)) for n in sizes]
    scratch += [vmem(gy_n - 1, DEPTH, padded_lanes(n // 2)) for n in sizes]
    scratch += [pltpu.SemaphoreType.DMA((12,)), pltpu.SemaphoreType.DMA((3,)), pltpu.SemaphoreType.DMA((3,))]
    scratch += [pltpu.SemaphoreType.DMA((LEVELS,))] * 4
    scratch += [pltpu.SemaphoreType.DMA((n0 // 128,))]
    anywhere = pl.BlockSpec(memory_space=pl.ANY)
    scalars = pl.BlockSpec(memory_space=pltpu.SMEM)
    return pl.pallas_call(
        functools.partial(kernel, gx_n, gy_n, n0),
        out_shape=jax.ShapeDtypeStruct(salinity.shape, jnp.float32),
        in_specs=[anywhere] * 12 + [scalars] * 2,
        out_specs=anywhere,
        scratch_shapes=scratch,
        compiler_params=pltpu.CompilerParams(
            collective_id=0, has_side_effects=True, vmem_limit_bytes=48 * 1024 * 1024
        ),
    )(salinity, *row_mats, *col_mats, *selects, row_vecs, col_vecs, row_w, col_w)


def solution(mesh):
    placed = P(None, "gx", "gy")
    return jax.shard_map(shards, mesh=mesh, in_specs=(placed,), out_specs=placed, check_vma=False)
```

```python
import functools

import jax
import jax.numpy as jnp
import numpy as np
from jax import lax
from jax.experimental import pallas as pl
from jax.experimental.pallas import tpu as pltpu
from jax.sharding import PartitionSpec as P

LEVELS = 3
DEPTH = 4
LENGTH = 64.0
MESH = pl.DeviceIdType.MESH
TABLE_LANES = 384


def padded_rows(count):
    return count + 8


def padded_lanes(count):
    return (count // 128 + 1) * 128 if count >= 128 else 128


def solver_line(count):
    off = 1.0 / (3.0 * LENGTH) - LENGTH
    inner = 4.0 / (3.0 * LENGTH) + 2.0 * LENGTH
    end = 2.0 / (3.0 * LENGTH) + LENGTH
    diag = np.full(count, inner)
    diag[0] = diag[-1] = end
    q = np.ones(count)
    p = np.ones(count)
    q[1] = -diag[0] / off
    p[-2] = -diag[-1] / off
    for i in range(1, count - 1):
        q[i + 1] = -(diag[i] * q[i]) / off - q[i - 1]
        j = count - 1 - i
        p[j - 1] = -(diag[j] * p[j]) / off - p[j + 1]
    return q, p, diag[0] * p[0] + off * p[1]


def load_block(total, coarse_ids, fine_ids):
    out = np.zeros((len(coarse_ids), len(fine_ids)))

    def mass(i, j):
        if i < 0 or i >= total or j < 0 or j >= total:
            return 0.0
        if i == j:
            return (2.0 if i in (0, total - 1) else 4.0) / 6.0
        return 1.0 / 6.0 if abs(i - j) == 1 else 0.0

    for a, k in enumerate(coarse_ids):
        if k < 0 or k >= total // 2:
            continue
        upper = 1.0 if 2 * k + 1 == total - 1 else 0.5
        for b in range(max(0, 2 * k - 2 - fine_ids[0]), min(len(fine_ids), 2 * k + 3 - fine_ids[0])):
            j = fine_ids[b]
            out[a, b] = mass(2 * k, j) + 0.5 * mass(2 * k - 1, j) + upper * mass(2 * k + 1, j)
    return out


def line_tables(total, tiles):
    n = total // tiles
    h = n // 2
    coarse = total // 2
    q, p, w = solver_line(coarse)
    local, functional, carry, weight, select = [], [], [], [], []
    for t in range(tiles):
        first = t * h
        last_tile = t == tiles - 1
        ids = np.arange(first, first + h + 1)
        if last_tile:
            ids[h] = ids[h - 2]
        window = np.arange(first - 1, first + h + 2)
        load = load_block(total, window, np.arange(t * n, t * n + n + 1))
        inside = (window >= 0) & (window < coarse)
        safe = np.clip(window, 0, coarse - 1)
        low = np.minimum(ids[:, None], safe[None, :])
        high = np.maximum(ids[:, None], safe[None, :])
        green = np.where(inside[None, :], q[low] * p[high] / w, 0.0)
        local.append(green @ load)
        q_end = q[min(first + h, coarse - 1)]
        to_right = (np.where(inside, q[safe] / q_end, 0.0)) @ load
        to_left = (np.where(inside, p[safe] / p[first], 0.0)) @ load
        to_right[n] = 0.0
        to_left[0] = 0.0
        functional.append(np.stack([to_right, to_left]))
        carry.append(np.stack([p[ids] / p[first], q[ids] / q_end]))
        weights = np.zeros((2, tiles))
        for k in range(1, tiles):
            s = (t - k) % tiles
            if s < t:
                weights[0, k] = q[(s + 1) * h] * p[first] / w
            else:
                weights[1, k] = q_end * p[s * h] / w
        weight.append(weights)
        pick = np.zeros((n + 1, h + 1))
        pick[2 * np.arange(h), np.arange(h)] = 1.0
        pick[n - 4 if last_tile else n, h] = 1.0
        select.append(pick)
    return [np.stack(item) for item in (local, functional, carry, weight, select)]


def fit(array, shape):
    out = np.zeros(array.shape[: array.ndim - len(shape)] + tuple(shape))
    out[tuple(slice(0, size) for size in array.shape)] = array
    return out


def interpolation(nodes):
    out = np.eye(nodes)
    for i in range(1, nodes, 2):
        out[i] = 0.0
        out[i, i - 1] = out[i, i + 1] = 0.5
    return out


def pair_weights(weight):
    tiles = weight.shape[0]
    out = np.zeros((tiles, tiles, 2, 2))
    for t in range(tiles):
        for k in range(1, tiles):
            for way in range(2):
                out[t, (t - k) % tiles, way, way] = weight[t, way, k]
    return out


def joined_weights(first, couplings, second):
    tiles = first.shape[0]
    blocks = [first]
    blocks += [np.einsum("tsab,sbc,sucd->tuad", second, k, first) for k in couplings]
    blocks.append(second)
    out = np.zeros((tiles, 4, 2, DEPTH, tiles, 2, DEPTH))
    for t in range(tiles):
        for slot in range(tiles):
            for d in range(DEPTH):
                for i, block in enumerate(blocks):
                    out[t, i, :, d, slot, :, d] = block[t, (t - slot) % tiles]
    return out.reshape(tiles, 32, tiles * 8)


@functools.lru_cache(maxsize=None)
def tables(nx, ny, gx, gy):
    row_vecs = np.zeros((gx, LEVELS, 8, TABLE_LANES))
    col_vecs = np.zeros((gy, LEVELS, 8, TABLE_LANES))
    mats, sides = ([], [], []), []
    weights = []
    for vecs, size, tiles in ((row_vecs, nx, gx), (col_vecs, ny, gy)):
        lines = [line_tables(size >> level, tiles) for level in range(LEVELS)]
        sides.append(lines)
        for level, (local, functional, carry, weight, select) in enumerate(lines):
            n = (size >> level) // tiles
            h = n // 2
            vecs[:, level, 0:2, : n + 1] = functional
            vecs[:, level, 2:4, : h + 1] = carry
            if vecs is row_vecs:
                mats[0].append(fit(local, (padded_rows(h), padded_rows(n))))
            else:
                shape = (padded_lanes(n), padded_lanes(h))
                joined = np.concatenate([local, functional], axis=1).transpose(0, 2, 1)
                mats[1].append(fit(joined, shape))
                mats[2].append(fit(select[[0, -1]], shape))
        weights.append(lines[0][3])
    nodes = (nx // gx >> 2) + 1
    inter = interpolation(nodes)
    rest = np.eye(nodes) - inter
    (_, _, carry_a, weight_a, _), (local_b, func_b, carry_b, weight_b, _) = sides[0][1:]
    row_k = [np.einsum("tbi,ij,taj->tba", func_b, op, carry_a) for op in (rest, inter)]
    row_join = joined_weights(pair_weights(weight_a), row_k, pair_weights(weight_b))
    row_after = np.zeros((gx, 256, 128))
    half = carry_b.shape[2]
    for i, op in enumerate((rest, inter)):
        row_vecs[:, 1, 4 + 2 * i : 6 + 2 * i, :nodes] = func_b @ op
        row_vecs[:, 2, 4 + 2 * i : 6 + 2 * i, :half] = np.einsum("tij,taj->tai", local_b @ op, carry_a)
        row_after[:, 128 * i : 128 * i + nodes, :half] = (local_b @ op).transpose(0, 2, 1)
        row_after[:, 128 * i + nodes + 2 * i : 128 * i + nodes + 2 * i + 2, :half] = carry_b
    (_, _, carry_a, weight_a, _), (local_b, func_b, _, weight_b, _) = sides[1][1:]
    col_k = [np.einsum("tbi,ij,taj->tba", func_b, op, carry_a) for op in (np.eye(nodes), rest)]
    col_join = joined_weights(pair_weights(weight_a), col_k, pair_weights(weight_b))
    col_after = np.zeros((gy, 256, 128))
    col_vecs[:, 1, 4:6, :nodes] = func_b @ rest
    both = np.concatenate([local_b, func_b], axis=1)
    for i, op in enumerate((np.eye(nodes), rest)):
        col_vecs[:, 2, 4 + 2 * i : 6 + 2 * i, :half] = np.einsum("tij,taj->tai", local_b @ op, carry_a)
        col_after[:, 128 * i : 128 * i + nodes, : both.shape[1]] = (both @ op).transpose(0, 2, 1)
    as32 = lambda item: np.ascontiguousarray(item, np.float32)
    grids = mats[0] + mats[1] + mats[2] + [row_join, row_after, col_join, col_after, row_vecs, col_vecs]
    return [as32(m) for m in grids], [as32(w.reshape(-1)) for w in weights]


def parts(value, count):
    out = []
    for _ in range(count):
        out.append(value.astype(jnp.bfloat16))
        value = value - out[-1].astype(jnp.float32)
    return out


def dot(a, b, dims=((1,), (0,))):
    return lax.dot_general(
        a, b, (dims, ((), ())), precision=lax.Precision.HIGHEST, preferred_element_type=jnp.float32
    )


def pick_dot(a, b, count=3, dims=((1,), (0,)), ones=1):
    total = None
    for part in reversed(parts(b if ones == 0 else a, count)):
        x, y = (a.astype(jnp.bfloat16), part) if ones == 0 else (part, b.astype(jnp.bfloat16))
        term = lax.dot_general(x, y, (dims, ((), ())), preferred_element_type=jnp.float32)
        total = term if total is None else total + term
    return total


def iota(shape, dim):
    return lax.broadcasted_iota(jnp.int32, shape, dim)


def detail(u):
    rows, lanes = u.shape
    odd_lane = iota(u.shape, 1) % 2 == 1
    odd_row = iota(u.shape, 0) % 2 == 1
    along = jnp.where(odd_lane, 0.5 * (pltpu.roll(u, 1, 1) + pltpu.roll(u, lanes - 1, 1)), u)
    both = jnp.where(odd_row, 0.5 * (pltpu.roll(along, 1, 0) + pltpu.roll(along, rows - 1, 0)), along)
    return u - both


def spread_matrix(count, lanes, stride, width):
    shape = (lanes, width)
    row = iota(shape, 0)
    return jnp.where((iota(shape, 1) == stride * row) & (row < count), 1.0, 0.0).astype(jnp.float32)


def kernel(gx_n, gy_n, n0, *refs):
    sal, out = refs[0], refs[18]
    tables_in, (row_w, col_w) = refs[1:16], refs[16:18]
    (u0, u1, w0, w1, out_v, tall_v) = refs[19:25]
    tables_v = refs[25:40]
    (hrow, hcol, hcorner, hrow_in, hcol_in, hcorner_in, xs0, xr0, ys0, yr0, xs1, xr1, ys1, yr1,
     load_sem, halo_send, halo_recv, x_send, x_recv, y_send, y_recv, out_sem) = refs[40:]
    row_mats, col_mats, selects = tables_v[0:3], tables_v[3:6], tables_v[6:9]
    row_join, row_after, col_join, col_after, rv, cv = tables_v[9:15]
    gx, gy = lax.axis_index("gx"), lax.axis_index("gy")
    last_x, last_y = gx == gx_n - 1, gy == gy_n - 1
    is_last_col = (gy + 1) // gy_n

    loads = [pltpu.make_async_copy(sal, u0.at[:, pl.ds(0, n0), pl.ds(0, n0)], load_sem.at[0])]
    places = [gx] * 3 + [gy] * 3 + [is_last_col] * 3 + [gx, gx, gy, gy, gx, gy]
    later = [(dst, src.at[place]) for dst, src, place in zip(tables_v, tables_in, places)]
    for i, (dst, src) in enumerate(later):
        loads.append(pltpu.make_async_copy(src, dst, load_sem.at[1 + i]))
    for copy in loads:
        copy.start()

    barrier = pltpu.get_barrier_semaphore()
    x_peers = [(lax.rem(gx + k, gx_n), gy) for k in range(1, gx_n)]
    y_peers = [(gx, lax.rem(gy + k, gy_n)) for k in range(1, gy_n)]
    up, left = lax.rem(gx + gx_n - 1, gx_n), lax.rem(gy + gy_n - 1, gy_n)
    greeted = x_peers + y_peers + [(lax.rem(gx + 1, gx_n), lax.rem(gy + 1, gy_n))]
    for peer in greeted:
        pl.semaphore_signal(barrier, inc=1, device_id=peer, device_id_type=MESH)

    loads[0].wait()
    edge = jnp.where(iota((DEPTH, n0), 1) == 0, 1.0, 0.0)
    depth_row = iota((DEPTH, n0), 0)
    hrow[...] = u0[:, 0, 0:n0]
    hcorner[...] = u0[:, 0, 0:128]
    first_cols = jnp.zeros((DEPTH, n0), jnp.float32)
    for d in range(DEPTH):
        first_cols += pick_dot(jnp.where(depth_row == d, edge, 0.0), u0[d, 0:n0, 0:n0], 3, ((1,), (1,)), 0)
    hcol[...] = first_cols
    pl.semaphore_wait(barrier, len(greeted))
    halos = []
    for i, (src, dst, peer) in enumerate(
        ((hrow, hrow_in, (up, gy)), (hcol, hcol_in, (gx, left)), (hcorner, hcorner_in, (up, left)))
    ):
        copy = pltpu.make_async_remote_copy(
            src_ref=src, dst_ref=dst, send_sem=halo_send.at[i], recv_sem=halo_recv.at[i],
            device_id=peer, device_id_type=MESH,
        )
        copy.start()
        halos.append(copy)
    for copy in loads[1:]:
        copy.wait()
    for copy in halos:
        copy.wait_recv()
    lane0 = iota((n0, 128), 1) == 0
    first_row = iota((8, 1), 0) == 0
    cols_in = jnp.concatenate([hcol_in[...], jnp.zeros((4, n0), jnp.float32)], axis=0).T
    for d in range(DEPTH):
        own_alias = u0[d, 0:n0, n0 - 2 : n0 - 1]
        column = jnp.where(last_y, own_alias, cols_in[:, d : d + 1])
        u0[d, 0:n0, n0 : n0 + 128] = jnp.where(lane0, column, 0.0)
        row = jnp.where(last_x, u0[d, n0 - 2 : n0 - 1, 0:n0], hrow_in[d : d + 1, :])
        corner = jnp.where(
            last_y,
            row[:, n0 - 2 : n0 - 1],
            jnp.where(last_x, u0[d, n0 - 2 : n0 - 1, n0 : n0 + 1], hcorner_in[d : d + 1, 0:1]),
        )
        u0[d, n0 : n0 + 8, 0:n0] = jnp.where(first_row, row, 0.0)
        u0[d, n0 : n0 + 8, n0 : n0 + 128] = jnp.where(first_row & (iota((8, 128), 1) == 0), corner, 0.0)

    def send_all(peers, me, count, src, dst, send, recv):
        for k, peer in enumerate(peers):
            pltpu.make_async_remote_copy(
                src_ref=src.at[(me + k + 1) // count], dst_ref=dst.at[k], send_sem=send, recv_sem=recv,
                device_id=peer, device_id_type=MESH,
            ).start()

    def send_same(peers, src, dst, send, recv):
        for k, peer in enumerate(peers):
            pltpu.make_async_remote_copy(
                src_ref=src, dst_ref=dst.at[k + 1], send_sem=send, recv_sem=recv, device_id=peer, device_id_type=MESH
            ).start()

    def gather(buf, weights, base, count):
        right = jnp.zeros(buf.shape[1:], jnp.float32)
        left_sum = jnp.zeros(buf.shape[1:], jnp.float32)
        for k in range(1, count):
            part = buf[k - 1]
            right += weights[base + k] * part
            left_sum += weights[base + count + k] * part
        return right, left_sum

    def local_level(level, n, u, w):
        h = n // 2
        rows, rows_c, lanes_c = padded_rows(n), padded_rows(h), padded_lanes(h)
        col_mat, row_mat, select = col_mats[level][...], row_mats[level][...], selects[level][...]
        base, across, solved, cols_local = [], [], [], jnp.zeros((8, rows_c), jnp.float32)
        row8, lane8 = iota((8, lanes_c), 0), iota((8, lanes_c), 1)
        is_tail = iota((rows_c, lanes_c), 0) == h
        for d in range(DEPTH):
            q = dot(w[d], col_mat)
            z = dot(row_mat, q)
            pick = ((row8 == d) & (lane8 == h + 1)) | ((row8 == 4 + d) & (lane8 == h + 2))
            cols_local += pick_dot(jnp.where(pick, 1.0, 0.0), z, 3, ((1,), (1,)), 0)
            even = even_rows(tall_v, pick_dot(u[d], select), rows_c)
            even = jnp.where(is_tail & last_x, even[h - 2 : h - 1, :], even)
            base.append(jnp.where(iota((rows_c, lanes_c), 1) <= h, z, 0.0) + even)
            across.append(q)
            solved.append(z)
        tall = padded_lanes(h)
        if rows_c < tall:
            cols_local = jnp.concatenate([cols_local, jnp.zeros((8, tall - rows_c), jnp.float32)], axis=1)
        return base, across, solved, cols_local

    def row_sums(values, weights):
        sums = []
        for way in range(2):
            for d in range(DEPTH):
                rows = values[d].shape[0]
                sums.append(jnp.sum(values[d] * weights[0:rows, way : way + 1], axis=0, keepdims=True))
        return jnp.concatenate(sums, axis=0)

    def line(value, functional):
        return jnp.sum(value * functional, axis=1, keepdims=True)

    def twice(table, row, lanes):
        return jnp.concatenate(
            [jnp.broadcast_to(table[row + way : row + way + 1, 0:lanes], (4, lanes)) for way in range(2)], axis=0
        )

    def outer(column, table, row, lanes):
        return (
            column[0:4] * table[row : row + 1, 0:lanes] + column[4:8] * table[row + 1 : row + 2, 0:lanes]
        )

    def spread_out(values, count, lanes, stride, pieces):
        mat = spread_matrix(count, lanes, stride, n0)
        for d in range(DEPTH):
            add_rows(out_v, d, pick_dot(values[d][0:count], mat, pieces), stride)

    n, h = n0, n0 // 2
    lanes, rows_c, lanes_c = padded_lanes(n), padded_rows(h), padded_lanes(h)
    for d in range(DEPTH):
        w0[d] = detail(u0[d])
    sums = row_sums([w0[d] for d in range(DEPTH)], rv[0].T)
    xs0[0] = sums[0:4]
    xs0[1] = sums[4:8]
    send_all(x_peers, gx, gx_n, xs0, xr0, x_send.at[0], x_recv.at[0])
    base, _, _, cols_local = local_level(0, n, u0, w0)
    pltpu.make_async_copy(xr0, xr0, x_recv.at[0]).wait()
    a_right, a_left = gather(xr0, row_w, gx * 2 * gx_n, gx_n)
    q_r, q_l = cv[0, 0:1, 0:lanes], cv[0, 1:2, 0:lanes]
    p_r, p_l = rv[0, 2:3, 0:lanes_c], rv[0, 3:4, 0:lanes_c]
    ys0[0] = cols_local[0:4] + line(a_right, q_r) * p_r + line(a_left, q_r) * p_l
    ys0[1] = cols_local[4:8] + line(a_right, q_l) * p_r + line(a_left, q_l) * p_l
    send_all(y_peers, gy, gy_n, ys0, yr0, y_send.at[0], y_recv.at[0])
    for d in range(DEPTH):
        for j in range(out_v.shape[1]):
            out_v[d, j] = w0[d, 0:n0, 128 * j : 128 * j + 128]
    carried = dot(jnp.concatenate([a_right, a_left], axis=0), col_mats[0][...])
    carried = jnp.where(iota((8, lanes_c), 1) <= h, carried, 0.0)
    other = jnp.concatenate([carried, twice(cv[0], 2, lanes_c)], axis=0)
    own = twice(rv[0], 2, lanes_c)
    pltpu.make_async_copy(yr0, yr0, y_recv.at[0]).wait()
    c_right, c_left = gather(yr0, col_w, gy * 2 * gy_n, gy_n)
    lhs = jnp.concatenate([own, c_right, c_left], axis=0).T[0:rows_c]
    for d in range(DEPTH):
        u1[d] = base[d] + dot(lhs, jnp.where(iota((16, lanes_c), 0) % 4 == d, other, 0.0))

    n, h, g = n0 // 2, n0 // 4, n0 // 8
    for d in range(DEPTH):
        w1[d] = detail(u1[d])
    rv1 = rv[1, :, 0 : 2 * 128].T
    rv2 = rv[2, :, 0:128].T
    base1, across1, solved1, cols1 = local_level(1, n, u1, w1)
    base2_w = [detail(base1[d]) for d in range(DEPTH)]
    _, across2, _, cols2 = local_level(2, h, base1, base2_w)
    lane = iota((8, 128), 1)
    is_c = (lane == h + 1) | (lane == h + 2)
    sent = row_sums(across1, rv1) + pltpu.roll(row_sums(across2, rv2), h + 3, 1)
    for i in range(2):
        of_cols = row_sums(solved1, rv1[:, 4 + 2 * i : 6 + 2 * i])
        sent += pltpu.roll(jnp.where(is_c, of_cols, 0.0), g + 5 + 2 * i, 1)
    xs1[...] = sent
    xr1[0] = sent
    send_same(x_peers, xs1, xr1, x_send.at[1], x_recv.at[1])
    spread_out([w1[d] for d in range(DEPTH)], n, 256, 2, 2)
    others = xr1.at[pl.ds(1, gx_n - 1)]
    pltpu.make_async_copy(others, others, x_recv.at[1]).wait()
    got = dot(row_join[...], xr1[...].reshape(gx_n * 8, 128))
    a_1 = got[0:8]
    a_2 = pltpu.roll(got[24:32], 128 - (h + 3), 1) + dot(
        jnp.concatenate([got[8:16], got[16:24]], axis=1), col_after[...]
    )
    kappa = got[0:8]
    msg, msg2, hs = [], [], []
    for way in range(2):
        msg.append(cols1[4 * way : 4 * way + 4] + outer(kappa[:, h + 1 + way : h + 2 + way], rv[1], 2, 128))
        row = outer(line(a_1, cv[2, way : way + 1, 0:128]), rv[2], 4, 128)
        row += outer(line(a_1, cv[1, 4 + way : 5 + way, 0:128]), rv[2], 6, 128)
        row += outer(a_2[:, g + 1 + way : g + 2 + way], rv[2], 2, 128)
        msg2.append(cols2[4 * way : 4 * way + 4] + row)
        block = jnp.zeros((4, 128), jnp.float32)
        for i in range(2):
            at = h + g + 6 + 2 * i + way
            h_col = got[24:32, at : at + 1] + got[8 + 8 * i : 16 + 8 * i, h + 1 + way : h + 2 + way]
            for x_way in range(2):
                block += jnp.where(iota((4, 128), 1) == h + 1 + 2 * i + x_way, h_col[4 * x_way : 4 * x_way + 4], 0.0)
        hs.append(block)
    sent = jnp.concatenate(msg, axis=0) + pltpu.roll(jnp.concatenate(msg2, axis=0), h + 5, 1)
    sent += jnp.concatenate(hs, axis=0)
    ys1[...] = sent
    yr1[0] = sent
    send_same(y_peers, ys1, yr1, y_send.at[1], y_recv.at[1])
    lane = iota((8, 128), 1)
    carried1 = jnp.where(lane <= h, a_1, 0.0)
    other1 = jnp.concatenate([carried1, twice(cv[1], 2, 128)], axis=0)
    others = yr1.at[pl.ds(1, gy_n - 1)]
    pltpu.make_async_copy(others, others, y_recv.at[1]).wait()
    got = dot(col_join[...], yr1[...].reshape(gy_n * 8, 128))
    c_1 = jnp.where(lane <= h, got[0:8], 0.0)
    c_2 = pltpu.roll(got[24:32], 128 - (h + 5), 1) + dot(
        jnp.concatenate([got[8:16], got[16:24]], axis=1), row_after[...]
    )
    lhs = jnp.concatenate([twice(rv[1], 2, 128), c_1], axis=0).T[0 : padded_rows(h)]
    nodes, details = [], []
    for d in range(DEPTH):
        nodes.append(base1[d] + dot(lhs, jnp.where(iota((16, 128), 0) % 4 == d, other1, 0.0)))
        details.append(detail(nodes[d]))
    base2, _, _, _ = local_level(2, h, nodes, details)
    extra = []
    for x_way in range(2):
        part = jnp.zeros((4, 128), jnp.float32)
        for i in range(2):
            part += outer(got[0:8, h + 1 + 2 * i + x_way : h + 2 + 2 * i + x_way], cv[2], 4 + 2 * i, 128)
        extra.append(part)
    carried2 = jnp.where(lane <= g, a_2, 0.0) + jnp.concatenate(extra, axis=0)
    other2 = jnp.concatenate([carried2, twice(cv[2], 2, 128)], axis=0)
    c_2 = jnp.where(lane <= g, c_2, 0.0)
    lhs = jnp.concatenate([twice(rv[2], 2, 128), c_2], axis=0).T[0 : padded_rows(g)]
    last = []
    for d in range(DEPTH):
        last.append(base2[d] + dot(lhs, jnp.where(iota((16, 128), 0) % 4 == d, other2, 0.0)))
    spread_out(details, h, 128, 4, 2)
    spread_out(last, g, 128, 8, 3)

    results = []
    for j in range(out_v.shape[1]):
        results.append(pltpu.make_async_copy(out_v.at[:, j], out.at[:, :, pl.ds(128 * j, 128)], out_sem.at[j]))
        results[-1].start()
    for i, copy in enumerate(halos):
        copy.wait_send()
    pltpu.make_async_copy(xr0, xr0, x_send.at[0]).wait()
    pltpu.make_async_copy(yr0, yr0, y_send.at[0]).wait()
    others = xr1.at[pl.ds(1, gx_n - 1)]
    pltpu.make_async_copy(others, others, x_send.at[1]).wait()
    others = yr1.at[pl.ds(1, gy_n - 1)]
    pltpu.make_async_copy(others, others, y_send.at[1]).wait()
    for copy in results:
        copy.wait()


def even_rows(tall_v, value, rows_c):
    rows, lanes = value.shape
    half = rows // 2
    parts = []
    for j in range(lanes // 128):
        tall_v[j, 0:rows] = value[:, 128 * j : 128 * j + 128]
        part = tall_v[j, pl.ds(0, half, stride=2), :]
        parts.append(jnp.concatenate([part, jnp.zeros((rows_c - half, 128), jnp.float32)], axis=0))
    return jnp.concatenate(parts, axis=1)


def add_rows(ref, d, value, stride):
    place = pl.ds(0, value.shape[0], stride=stride)
    for j in range(ref.shape[1]):
        ref[d, j, place, :] = ref[d, j, place, :] + value[:, 128 * j : 128 * j + 128]


def shards(salinity):
    gx_n, gy_n = lax.axis_size("gx"), lax.axis_size("gy")
    _, nx, ny = salinity.shape
    n0 = nx
    grids, weights = tables(nx * gx_n, ny * gy_n, gx_n, gy_n)
    vmem = lambda *shape: pltpu.VMEM(shape, jnp.float32)
    dma = lambda count: pltpu.SemaphoreType.DMA((count,))
    wide, wide_c = padded_lanes(n0), padded_lanes(n0 // 2)
    levels = [vmem(DEPTH, padded_rows(n), padded_lanes(n)) for n in (n0, n0 // 2)]
    scratch = levels + levels + [vmem(DEPTH, n0 // 128, n0, 128), vmem(2, padded_rows(n0), 128)]
    scratch += [vmem(*m.shape[1:]) for m in grids]
    scratch += [vmem(DEPTH, n0), vmem(DEPTH, n0), vmem(DEPTH, 128)] * 2
    scratch += [vmem(2, DEPTH, wide), vmem(gx_n - 1, DEPTH, wide)]
    scratch += [vmem(2, DEPTH, wide_c), vmem(gy_n - 1, DEPTH, wide_c)]
    scratch += [vmem(8, 128), vmem(gx_n, 8, 128), vmem(8, 128), vmem(gy_n, 8, 128)]
    scratch += [dma(1 + len(grids)), dma(3), dma(3), dma(2), dma(2), dma(2), dma(2), dma(n0 // 128)]
    anywhere = pl.BlockSpec(memory_space=pl.ANY)
    scalars = pl.BlockSpec(memory_space=pltpu.SMEM)
    return pl.pallas_call(
        functools.partial(kernel, gx_n, gy_n, n0),
        out_shape=jax.ShapeDtypeStruct(salinity.shape, jnp.float32),
        in_specs=[anywhere] * (1 + len(grids)) + [scalars] * 2,
        out_specs=anywhere,
        scratch_shapes=scratch,
        compiler_params=pltpu.CompilerParams(
            collective_id=0, has_side_effects=True, vmem_limit_bytes=63 * 1024 * 1024
        ),
    )(salinity, *grids, *weights)


def solution(mesh):
    placed = P(None, "gx", "gy")
    return jax.shard_map(shards, mesh=mesh, in_specs=(placed,), out_specs=placed, check_vma=False)
```

```python
import functools

import jax
import jax.numpy as jnp
import numpy as np
from jax import lax
from jax.experimental import pallas as pl
from jax.experimental.pallas import tpu as pltpu
from jax.sharding import PartitionSpec as P

LEVELS = 3
DEPTH = 4
LENGTH = 64.0
MESH = pl.DeviceIdType.MESH
TABLE_LANES = 384
VMEM_LIMIT = 52 * 1024 * 1024


def padded_rows(count):
    return count + 8


def padded_lanes(count):
    return (count // 128 + 1) * 128 if count >= 128 else 128


def solver_line(count):
    off = 1.0 / (3.0 * LENGTH) - LENGTH
    inner = 4.0 / (3.0 * LENGTH) + 2.0 * LENGTH
    end = 2.0 / (3.0 * LENGTH) + LENGTH
    diag = np.full(count, inner)
    diag[0] = diag[-1] = end
    q = np.ones(count)
    p = np.ones(count)
    q[1] = -diag[0] / off
    p[-2] = -diag[-1] / off
    for i in range(1, count - 1):
        q[i + 1] = -(diag[i] * q[i]) / off - q[i - 1]
        j = count - 1 - i
        p[j - 1] = -(diag[j] * p[j]) / off - p[j + 1]
    return q, p, diag[0] * p[0] + off * p[1]


def load_block(total, coarse_ids, fine_ids):
    out = np.zeros((len(coarse_ids), len(fine_ids)))

    def mass(i, j):
        if i < 0 or i >= total or j < 0 or j >= total:
            return 0.0
        if i == j:
            return (2.0 if i in (0, total - 1) else 4.0) / 6.0
        return 1.0 / 6.0 if abs(i - j) == 1 else 0.0

    for a, k in enumerate(coarse_ids):
        if k < 0 or k >= total // 2:
            continue
        upper = 1.0 if 2 * k + 1 == total - 1 else 0.5
        for b in range(max(0, 2 * k - 2 - fine_ids[0]), min(len(fine_ids), 2 * k + 3 - fine_ids[0])):
            j = fine_ids[b]
            out[a, b] = mass(2 * k, j) + 0.5 * mass(2 * k - 1, j) + upper * mass(2 * k + 1, j)
    return out


def line_tables(total, tiles):
    n = total // tiles
    h = n // 2
    coarse = total // 2
    q, p, w = solver_line(coarse)
    local, functional, carry, weight, select = [], [], [], [], []
    for t in range(tiles):
        first = t * h
        last_tile = t == tiles - 1
        ids = np.arange(first, first + h + 1)
        if last_tile:
            ids[h] = ids[h - 2]
        window = np.arange(first - 1, first + h + 2)
        load = load_block(total, window, np.arange(t * n, t * n + n + 1))
        inside = (window >= 0) & (window < coarse)
        safe = np.clip(window, 0, coarse - 1)
        low = np.minimum(ids[:, None], safe[None, :])
        high = np.maximum(ids[:, None], safe[None, :])
        green = np.where(inside[None, :], q[low] * p[high] / w, 0.0)
        local.append(green @ load)
        q_end = q[min(first + h, coarse - 1)]
        to_right = (np.where(inside, q[safe] / q_end, 0.0)) @ load
        to_left = (np.where(inside, p[safe] / p[first], 0.0)) @ load
        to_right[n] = 0.0
        to_left[0] = 0.0
        functional.append(np.stack([to_right, to_left]))
        carry.append(np.stack([p[ids] / p[first], q[ids] / q_end]))
        weights = np.zeros((2, tiles))
        for k in range(1, tiles):
            s = (t - k) % tiles
            if s < t:
                weights[0, k] = q[(s + 1) * h] * p[first] / w
            else:
                weights[1, k] = q_end * p[s * h] / w
        weight.append(weights)
        pick = np.zeros((n + 1, h + 1))
        pick[2 * np.arange(h), np.arange(h)] = 1.0
        pick[n - 4 if last_tile else n, h] = 1.0
        select.append(pick)
    return [np.stack(item) for item in (local, functional, carry, weight, select)]


def fit(array, shape):
    out = np.zeros(array.shape[: array.ndim - len(shape)] + tuple(shape))
    out[tuple(slice(0, size) for size in array.shape)] = array
    return out


def interpolation(nodes):
    out = np.eye(nodes)
    for i in range(1, nodes, 2):
        out[i] = 0.0
        out[i, i - 1] = out[i, i + 1] = 0.5
    return out


def pair_weights(weight):
    tiles = weight.shape[0]
    out = np.zeros((tiles, tiles, 2, 2))
    for t in range(tiles):
        for k in range(1, tiles):
            for way in range(2):
                out[t, (t - k) % tiles, way, way] = weight[t, way, k]
    return out


def joined_weights(first, couplings, second):
    tiles = first.shape[0]
    blocks = [first]
    blocks += [np.einsum("tsab,sbc,sucd->tuad", second, k, first) for k in couplings]
    blocks.append(second)
    out = np.zeros((tiles, 4, 2, DEPTH, tiles, 2, DEPTH))
    for t in range(tiles):
        for slot in range(tiles):
            for d in range(DEPTH):
                for i, block in enumerate(blocks):
                    out[t, i, :, d, slot, :, d] = block[t, (t - slot) % tiles]
    return out.reshape(tiles, 32, tiles * 8)


def packed(tables):
    places, blocks, at = {}, [], 0
    for name, table in tables.items():
        rows, lanes = -(-table.shape[1] // 8) * 8, -(-table.shape[2] // 128) * 128
        table = fit(table, (rows, lanes))
        places[name] = (at, rows, lanes // 128)
        at += rows * (lanes // 128)
        blocks += [table[:, :, 128 * j : 128 * j + 128] for j in range(lanes // 128)]
    return np.ascontiguousarray(np.concatenate(blocks, axis=1), np.float32), places


@functools.lru_cache(maxsize=None)
def tables(nx, ny, gx, gy):
    row_vecs = np.zeros((gx, 8 * LEVELS + 8, TABLE_LANES))
    col_vecs = np.zeros((gy, 8 * LEVELS + 8, TABLE_LANES))
    row_out, col_out, sides = {}, {}, []
    for vecs, size, tiles, out in ((row_vecs, nx, gx, row_out), (col_vecs, ny, gy, col_out)):
        lines = [line_tables(size >> level, tiles) for level in range(LEVELS)]
        sides.append(lines)
        for level, (local, functional, carry, weight, select) in enumerate(lines):
            n = (size >> level) // tiles
            h = n // 2
            vecs[:, 8 * level : 8 * level + 2, : n + 1] = functional
            vecs[:, 8 * level + 2 : 8 * level + 4, : h + 1] = carry
            if vecs is row_vecs:
                out[f"mat{level}"] = fit(local, (padded_rows(h), padded_lanes(n)))
                if level == 0:
                    vecs[:, 4, : h + 1] = local[:, :, n - 1]
                    vecs[:, 5, : h + 1] = local[:, :, n]
            else:
                joined = np.concatenate([local, functional], axis=1).transpose(0, 2, 1)
                out[f"mat{level}"] = fit(joined, (padded_lanes(n), padded_lanes(h)))
        out["weight"] = np.repeat(lines[0][3].reshape(tiles, 2 * tiles, 1), 128, axis=2)
    nodes = (nx // gx >> 2) + 1
    inter = interpolation(nodes)
    rest = np.eye(nodes) - inter
    (local_a, _, carry_a, weight_a, select_a), (local_b, func_b, carry_b, weight_b, select_b) = sides[0][1:]
    row_k = [np.einsum("tbi,ij,taj->tba", func_b, op, carry_a) for op in (rest, inter)]
    row_out["join"] = joined_weights(pair_weights(weight_a), row_k, pair_weights(weight_b))
    after = np.zeros((gx, 384, 128))
    half = carry_b.shape[2]
    taken = np.zeros((gx, 8, TABLE_LANES))
    for i, op in enumerate((rest, inter)):
        func = func_b @ op
        row_vecs[:, 12 + 2 * i : 14 + 2 * i, : local_a.shape[2]] = np.einsum("tij,tjk->tik", func, local_a)
        taken[:, 2 * i : 2 * i + 2, : select_a.shape[1]] = np.einsum("tij,tkj->tik", func, select_a)
        row_vecs[:, 20 + 2 * i : 22 + 2 * i, :half] = np.einsum("tij,taj->tai", local_b @ op, carry_a)
        after[:, 128 * i : 128 * i + nodes, :half] = (local_b @ op).transpose(0, 2, 1)
        after[:, 128 * i + nodes + 2 * i : 128 * i + nodes + 2 * i + 2, :half] = carry_b
    after[:, 256 : 256 + nodes, :half] = select_b
    row_vecs[:, 24:26, :half] = carry_a @ select_b
    row_out.update(after=after, taken=taken, vecs=row_vecs)
    (_, _, carry_a, weight_a, _), (local_b, func_b, _, weight_b, select_b) = sides[1][1:]
    col_k = [np.einsum("tbi,ij,taj->tba", func_b, op, carry_a) for op in (np.eye(nodes), rest)]
    col_out["join"] = joined_weights(pair_weights(weight_a), col_k, pair_weights(weight_b))
    after = np.zeros((gy, 384, 128))
    col_vecs[:, 12:14, :nodes] = func_b @ rest
    both = np.concatenate([local_b, func_b], axis=1)
    for i, op in enumerate((np.eye(nodes), rest)):
        col_vecs[:, 20 + 2 * i : 22 + 2 * i, :half] = np.einsum("tij,taj->tai", local_b @ op, carry_a)
        after[:, 128 * i : 128 * i + nodes, : both.shape[1]] = (both @ op).transpose(0, 2, 1)
    after[:, 256 : 256 + nodes, :half] = select_b
    col_vecs[:, 24:26, :half] = carry_a @ select_b
    col_out.update(after=after, vecs=col_vecs)
    return packed(row_out), packed(col_out)


def parts(value, count):
    out = []
    for _ in range(count):
        out.append(value.astype(jnp.bfloat16))
        value = value - out[-1].astype(jnp.float32)
    return out


def dot(a, b, dims=((1,), (0,))):
    return lax.dot_general(
        a, b, (dims, ((), ())), precision=lax.Precision.HIGHEST, preferred_element_type=jnp.float32
    )


def pick_dot(a, b, count=3, dims=((1,), (0,)), ones=1):
    total = None
    for part in reversed(parts(b if ones == 0 else a, count)):
        x, y = (a.astype(jnp.bfloat16), part) if ones == 0 else (part, b.astype(jnp.bfloat16))
        term = lax.dot_general(x, y, (dims, ((), ())), preferred_element_type=jnp.float32)
        total = term if total is None else total + term
    return total


def iota(shape, dim):
    return lax.broadcasted_iota(jnp.int32, shape, dim)


def detail(u, alone=False):
    rows, lanes = u.shape
    lane, row = iota(u.shape, 1), iota(u.shape, 0)
    left, right = pltpu.roll(u, 1, 1), pltpu.roll(u, lanes - 1, 1)
    if alone:
        right = jnp.where(lane == lanes - 1, left, right)
    along = jnp.where(lane % 2 == 1, 0.5 * (left + right), u)
    above, below = pltpu.roll(along, 1, 0), pltpu.roll(along, rows - 1, 0)
    if alone:
        below = jnp.where(row == rows - 1, above, below)
    return u - jnp.where(row % 2 == 1, 0.5 * (above + below), along)


def spread_matrix(count, lanes, stride, width):
    shape = (lanes, width)
    row = iota(shape, 0)
    return jnp.where((iota(shape, 1) == stride * row) & (row < count), 1.0, 0.0).astype(jnp.float32)


def kernel(gx_n, gy_n, n0, row_places, col_places, *refs):
    (sal, row_in, col_in, out, out_v, u0, u1, w0, w1, tall_v, row_v, col_v,
     hrow, hcol, hcorner, hrow_in, hcol_in, hcorner_in, xs0, xr0, ys0, yr0, xs1, xr1, ys1, yr1,
     load_sem, halo_send, halo_recv, x_send, x_recv, y_send, y_recv) = refs

    def table(ref, places, name):
        at, rows, tiles = places[name]
        return jnp.concatenate([ref[at + j * rows : at + (j + 1) * rows] for j in range(tiles)], axis=1)

    row_table = functools.partial(table, row_v, row_places)
    col_table = functools.partial(table, col_v, col_places)
    gx, gy = lax.axis_index("gx"), lax.axis_index("gy")
    last_x, last_y = gx == gx_n - 1, gy == gy_n - 1

    loads = [
        pltpu.make_async_copy(sal.at[:, :, pl.ds(128 * j, 128)], u0.at[:, j], load_sem.at[j]) for j in range(2)
    ]
    loads.append(pltpu.make_async_copy(row_in.at[gx], row_v, load_sem.at[2]))
    loads.append(pltpu.make_async_copy(col_in.at[gy], col_v, load_sem.at[3]))
    for copy in loads:
        copy.start()

    barrier = pltpu.get_barrier_semaphore()
    x_peers = [(lax.rem(gx + k, gx_n), gy) for k in range(1, gx_n)]
    y_peers = [(gx, lax.rem(gy + k, gy_n)) for k in range(1, gy_n)]
    up, left = lax.rem(gx + gx_n - 1, gx_n), lax.rem(gy + gy_n - 1, gy_n)
    greeted = x_peers + y_peers + [(lax.rem(gx + 1, gx_n), lax.rem(gy + 1, gy_n))]
    for peer in greeted:
        pl.semaphore_signal(barrier, inc=1, device_id=peer, device_id_type=MESH)

    loads[0].wait()
    loads[1].wait()
    hrow[...] = jnp.concatenate([u0[:, 0, 0, :], u0[:, 1, 0, :]], axis=1)
    hcorner[...] = u0[:, 0, 0, :]
    lane = iota((n0, 128), 1)
    packed = jnp.zeros((n0, 128), jnp.float32)
    for d in range(DEPTH):
        packed = jnp.where(lane == d, u0[d, 0, :, 0:1], packed)
        packed = jnp.where(lane == 4 + d, u0[d, 1, :, 126:127], packed)
    packed = packed.T
    hcol[...] = packed[0:4]
    pl.semaphore_wait(barrier, len(greeted))
    halos = []
    for i, (src, dst, peer) in enumerate(
        ((hrow, hrow_in, (up, gy)), (hcol, hcol_in, (gx, left)), (hcorner, hcorner_in, (up, left)))
    ):
        copy = pltpu.make_async_remote_copy(
            src_ref=src, dst_ref=dst, send_sem=halo_send.at[i], recv_sem=halo_recv.at[i],
            device_id=peer, device_id_type=MESH,
        )
        copy.start()
        halos.append(copy)

    def send_all(peers, me, count, src, dst, send, recv):
        for k, peer in enumerate(peers):
            pltpu.make_async_remote_copy(
                src_ref=src.at[(me + k + 1) // count], dst_ref=dst.at[k], send_sem=send, recv_sem=recv,
                device_id=peer, device_id_type=MESH,
            ).start()

    def send_same(peers, src, dst, send, recv):
        for k, peer in enumerate(peers):
            pltpu.make_async_remote_copy(
                src_ref=src, dst_ref=dst.at[k + 1], send_sem=send, recv_sem=recv, device_id=peer, device_id_type=MESH
            ).start()

    def gather(buf, ref, places, count):
        at, _, _ = places["weight"]
        tiles = buf.shape[2] // 128
        sums = [jnp.zeros(buf.shape[1:], jnp.float32)] * 2
        for k in range(1, count):
            for way in range(2):
                weight = ref[at + way * count + k : at + way * count + k + 1, :]
                sums[way] = sums[way] + jnp.concatenate([weight] * tiles, axis=1) * buf[k - 1]
        return sums

    def selection(n, last):
        shape = (padded_lanes(n), padded_lanes(n // 2))
        row, lane = iota(shape, 0), iota(shape, 1)
        tail = jnp.where(last, n - 4, n)
        hit = ((lane < n // 2) & (row == 2 * lane)) | ((lane == n // 2) & (row == tail))
        return jnp.where(hit, 1.0, 0.0)

    def local_level(level, n, u, w):
        h = n // 2
        rows, rows_c, lanes_c = padded_rows(n), padded_rows(h), padded_lanes(h)
        col_mat, row_mat = col_table(f"mat{level}"), row_table(f"mat{level}")[:, 0:rows]
        select = selection(n, last_y)
        base, cols_local = [], jnp.zeros((8, rows_c), jnp.float32)
        row8, lane8 = iota((8, lanes_c), 0), iota((8, lanes_c), 1)
        is_tail = iota((rows_c, lanes_c), 0) == h
        for d in range(DEPTH):
            q = dot(w[d], col_mat)
            z = dot(row_mat, q)
            pick = ((row8 == d) & (lane8 == h + 1)) | ((row8 == 4 + d) & (lane8 == h + 2))
            cols_local += pick_dot(jnp.where(pick, 1.0, 0.0), z, 3, ((1,), (1,)), 0)
            even = even_rows(tall_v, pick_dot(u[d], select), rows_c)
            even = jnp.where(is_tail & last_x, even[h - 2 : h - 1, :], even)
            base.append(jnp.where(iota((rows_c, lanes_c), 1) <= h, z, 0.0) + even)
        tall = padded_lanes(h)
        if rows_c < tall:
            cols_local = jnp.concatenate([cols_local, jnp.zeros((8, tall - rows_c), jnp.float32)], axis=1)
        return base, cols_local

    def row_sums(values, weights, count=2):
        sums = []
        for way in range(count):
            for d in range(DEPTH):
                rows = values[d].shape[0]
                sums.append(jnp.sum(values[d] * weights[0:rows, way : way + 1], axis=0, keepdims=True))
        return jnp.concatenate(sums, axis=0)

    def line(value, functional):
        return jnp.sum(value * functional, axis=1, keepdims=True)

    def twice(table, row, lanes):
        return jnp.concatenate(
            [jnp.broadcast_to(table[row + way : row + way + 1, 0:lanes], (4, lanes)) for way in range(2)], axis=0
        )

    def outer(column, table, row, lanes):
        return (
            column[0:4] * table[row : row + 1, 0:lanes] + column[4:8] * table[row + 1 : row + 2, 0:lanes]
        )

    def spread_out(values, count, lanes, stride, pieces):
        mat = spread_matrix(count, lanes, stride, n0)
        for d in range(DEPTH):
            add_rows(out_v, d, pick_dot(values[d][0:count], mat, pieces), stride)

    n, h = n0, n0 // 2
    wide, rows_c, lanes_c = padded_lanes(n), padded_rows(h), padded_lanes(h)
    for copy in loads[2:]:
        copy.wait()
    rv, cv = row_table("vecs"), col_table("vecs")
    col_q = cv[0:2, 0:n]
    own_cols = jnp.zeros((n, 128), jnp.float32)
    for d in range(DEPTH):
        value = detail(jnp.concatenate([u0[d, 0], u0[d, 1]], axis=1), True)
        w0[d] = value
        for way in range(2):
            own_cols = jnp.where(lane == 4 * way + d, line(value, col_q[way : way + 1]), own_cols)
    own_rows = row_sums([w0[d] for d in range(DEPTH)], rv[0:8, 0:n].T)
    own_cols = own_cols.T[0:8]
    none = jnp.zeros((8, 128), jnp.float32)
    own_rows = jnp.concatenate([own_rows, none], axis=1)
    own_cols = jnp.concatenate([own_cols, none], axis=1)

    for copy in halos:
        copy.wait_recv()
    at = iota((4, wide), 1)
    own_254 = jnp.concatenate([u0[:, 0, n - 2, :], u0[:, 1, n - 2, :]], axis=1)
    next_row = jnp.where(last_x, own_254, hrow_in[...])
    next_col = jnp.where(last_y, packed[4:8], hcol_in[...])
    corner = jnp.where(
        last_y, next_row[:, n - 2 : n - 1], jnp.where(last_x, next_col[:, n - 2 : n - 1], hcorner_in[:, 0:1])
    )
    alias = packed[4:8, n - 2 : n - 1]
    wider = lambda value, end: jnp.where(at == n, end, jnp.concatenate([value, none[0:4]], axis=1))
    row_change, col_change = wider(next_row - own_254, 0.0), wider(next_col - packed[4:8], corner - alias)
    next_row, next_col = wider(next_row, alias), wider(next_col, corner)

    def between(value):
        mean = 0.5 * (pltpu.roll(value, 1, 1) + pltpu.roll(value, wide - 1, 1))
        return jnp.where(at > n, 0.0, jnp.where(at % 2 == 1, mean, value))

    row_255, row_256 = -0.5 * between(row_change), next_row - between(next_row)
    col_255, col_256 = -0.5 * between(col_change), next_col - between(next_col)
    for way in range(2):
        q = rv[way : way + 1, 0:wide]
        xs0[way] = (
            own_rows[4 * way : 4 * way + 4]
            + q[:, n - 1 : n] * row_255
            + q[:, n : n + 1] * row_256
            + jnp.where(at == n - 1, line(col_255, q), 0.0)
            + jnp.where(at == n, line(col_256, q), 0.0)
        )
    send_all(x_peers, gx, gx_n, xs0, xr0, x_send.at[0], x_recv.at[0])
    cols = []
    for way in range(2):
        q = cv[way : way + 1, 0:wide]
        cols.append(
            own_cols[4 * way : 4 * way + 4]
            + q[:, n - 1 : n] * col_255
            + q[:, n : n + 1] * col_256
            + jnp.where(at == n - 1, line(row_255, q), 0.0)
            + jnp.where(at == n, line(row_256, q), 0.0)
        )
    down_x = dot(jnp.concatenate(cols + [col_255, col_256], axis=0), row_table("mat0"), ((1,), (1,)))
    down_x = jnp.concatenate([down_x, jnp.zeros((16, lanes_c - rows_c), jnp.float32)], axis=1)
    select = selection(n, last_y)[0:n]
    next_even = pick_dot(next_row[:, 0:n], select)
    next_col_even = jnp.where(last_y, 0.0, pick_dot(next_col, selection(n, last_x)))
    evens = []
    for d in range(DEPTH):
        even = jnp.concatenate([u0[d, j, pl.ds(0, h, stride=2), :] for j in range(2)], axis=1)
        even = pick_dot(even, select)
        tail = jnp.where(last_x, even[h - 2 : h - 1], next_even[d : d + 1])
        tail = jnp.where(iota((8, lanes_c), 0) == 0, tail, 0.0)
        evens.append(jnp.concatenate([even, tail], axis=0))

    pltpu.make_async_copy(xr0, xr0, x_recv.at[0]).wait()
    a_right, a_left = gather(xr0, row_v, row_places, gx_n)
    q_r, q_l = cv[0:1, 0:wide], cv[1:2, 0:wide]
    p_r, p_l = rv[2:3, 0:lanes_c], rv[3:4, 0:lanes_c]
    ys0[0] = down_x[0:4] + line(a_right, q_r) * p_r + line(a_left, q_r) * p_l
    ys0[1] = down_x[4:8] + line(a_right, q_l) * p_r + line(a_left, q_l) * p_l
    send_all(y_peers, gy, gy_n, ys0, yr0, y_send.at[0], y_recv.at[0])
    col_mat, row_mat = col_table("mat0"), row_table("mat0")
    is_node = iota((1, lanes_c), 1) <= h
    base = []
    for d in range(DEPTH):
        z = dot(row_mat[:, 0:n], dot(w0[d], col_mat[0:n]))
        base.append(jnp.where(is_node, z, 0.0) + evens[d])
    down_turned = jnp.concatenate([col_255, col_255], axis=0).T[0:n]
    is_last = iota((n, 128), 1) == 127
    for d in range(DEPTH):
        out_v[d, 0] = w0[d, :, 0:128]
        out_v[d, 1] = w0[d, :, 128:256] + jnp.where(is_last, down_turned[:, d : d + 1], 0.0)
        for j in range(2):
            tail = iota((8, 128), 0) == 7
            fix = row_255[d : d + 1, 128 * j : 128 * j + 128]
            out_v[d, j, n - 8 : n, :] = out_v[d, j, n - 8 : n, :] + jnp.where(tail, fix, 0.0)
    carried = dot(jnp.concatenate([a_right, a_left, row_255, row_256], axis=0), col_mat)
    four = lambda row: jnp.broadcast_to(row, (4, lanes_c))
    other = jnp.concatenate(
        [jnp.where(is_node, carried, 0.0), twice(cv, 2, lanes_c)]
        + [four(jnp.where(is_node, col_mat[n - 1 + i : n + i, :], 0.0)) for i in range(2)]
        + [four(jnp.where(iota((1, lanes_c), 1) == h, 1.0, 0.0)), jnp.zeros((4, lanes_c), jnp.float32)],
        axis=0,
    )
    own = jnp.concatenate([twice(rv, 2, lanes_c), twice(rv, 4, lanes_c)], axis=0)
    rest = jnp.concatenate([down_x[8:16], next_col_even, jnp.zeros((4, lanes_c), jnp.float32)], axis=0)
    pltpu.make_async_copy(yr0, yr0, y_recv.at[0]).wait()
    c_right, c_left = gather(yr0, col_v, col_places, gy_n)
    lhs = jnp.concatenate([own, c_right, c_left, rest], axis=0).T[0:rows_c]
    for d in range(DEPTH):
        u1[d] = base[d] + dot(lhs, jnp.where(iota((40, lanes_c), 0) % 4 == d, other, 0.0))

    n, h, g = n0 // 2, n0 // 4, n0 // 8
    lane = iota((8, 128), 1)
    for d in range(DEPTH):
        w1[d] = detail(u1[d])
    ways = jnp.concatenate([rv[8:16, 0:256], row_table("taken")[:, 0:256]], axis=0).T
    functionals = jnp.concatenate([ways[:, 0:2], ways[:, 4:8]], axis=1)
    of_w = dot(row_sums([w1[d] for d in range(DEPTH)], functionals, 6), col_table("mat1"))
    taken = row_sums([u1[d] for d in range(DEPTH)], ways[:, 8:12], 4)
    of_next = of_w[8:24] + pick_dot(taken, selection(n, last_y))
    after = col_table("after")
    of_second = dot(jnp.concatenate([of_next[0:8], of_next[8:16]], axis=1), after[0:256])
    is_c = (lane == h + 1) | (lane == h + 2)
    sent = of_w[0:8] + pltpu.roll(of_second, h + 3, 1)
    for i in range(2):
        sent += pltpu.roll(jnp.where(is_c, of_w[8 + 8 * i : 16 + 8 * i], 0.0), g + 5 + 2 * i, 1)
    xs1[...] = sent
    xr1[0] = sent
    send_same(x_peers, xs1, xr1, x_send.at[1], x_recv.at[1])
    base1, cols1 = local_level(1, n, u1, w1)
    base2, cols2 = local_level(2, h, base1, [detail(base1[d]) for d in range(DEPTH)])
    others = xr1.at[pl.ds(1, gx_n - 1)]
    pltpu.make_async_copy(others, others, x_recv.at[1]).wait()
    got = dot(row_table("join")[:, 0 : gx_n * 8], xr1[...].reshape(gx_n * 8, 128))
    a_1 = got[0:8]
    a_2 = pltpu.roll(got[24:32], 128 - (h + 3), 1) + dot(
        jnp.concatenate([got[8:16], got[16:24]], axis=1), after[0:256]
    )
    msg, msg2, hs = [], [], []
    for way in range(2):
        msg.append(cols1[4 * way : 4 * way + 4] + outer(a_1[:, h + 1 + way : h + 2 + way], rv, 10, 128))
        row = outer(line(a_1, cv[16 + way : 17 + way, 0:128]), rv, 20, 128)
        row += outer(line(a_1, cv[12 + way : 13 + way, 0:128]), rv, 22, 128)
        row += outer(a_2[:, g + 1 + way : g + 2 + way], rv, 18, 128)
        msg2.append(cols2[4 * way : 4 * way + 4] + row)
        block = jnp.zeros((4, 128), jnp.float32)
        for i in range(2):
            at = h + g + 6 + 2 * i + way
            h_col = got[24:32, at : at + 1] + got[8 + 8 * i : 16 + 8 * i, h + 1 + way : h + 2 + way]
            for x_way in range(2):
                block += jnp.where(iota((4, 128), 1) == h + 1 + 2 * i + x_way, h_col[4 * x_way : 4 * x_way + 4], 0.0)
        hs.append(block)
    sent = jnp.concatenate(msg, axis=0) + pltpu.roll(jnp.concatenate(msg2, axis=0), h + 5, 1)
    sent += jnp.concatenate(hs, axis=0)
    ys1[...] = sent
    yr1[0] = sent
    send_same(y_peers, ys1, yr1, y_send.at[1], y_recv.at[1])
    spread_out([w1[d] for d in range(DEPTH)], n, 256, 2, 2)
    beside = lambda value: jnp.concatenate([value[128 * i : 128 * i + 128] for i in range(3)], axis=1)
    nodes_1 = lambda value: jnp.where(lane <= h, value, 0.0)
    nodes_2 = lambda value: jnp.where(lane <= g, value, 0.0)
    other1 = jnp.concatenate([nodes_1(a_1), twice(cv, 10, 128)], axis=0)
    across = dot(a_1, beside(after))
    other2 = jnp.concatenate(
        [nodes_2(across[:, 256:384]), nodes_2(across[:, 0:128]), nodes_2(across[:, 128:256]), nodes_2(a_2)]
        + [twice(cv, row, 128) for row in (24, 20, 22, 18)],
        axis=0,
    )
    own = jnp.concatenate([twice(rv, row, 128) for row in (24, 20, 22, 18)], axis=0)
    row_after = beside(row_table("after"))
    others = yr1.at[pl.ds(1, gy_n - 1)]
    pltpu.make_async_copy(others, others, y_recv.at[1]).wait()
    got = dot(col_table("join"), yr1[...].reshape(gy_n * 8, 128))
    down = dot(got[0:24], row_after)
    c_2 = nodes_2(pltpu.roll(got[24:32], 128 - (h + 5), 1) + down[8:16, 0:128] + down[16:24, 128:256])
    lhs = jnp.concatenate([own, down[0:8, 256:384], down[0:8, 0:128], down[0:8, 128:256], c_2], axis=0)
    lhs = jnp.concatenate([lhs, jnp.zeros_like(lhs)], axis=0).T[0 : padded_rows(g), 0:64]
    lhs1 = jnp.concatenate([twice(rv, 10, 128), nodes_1(got[0:8])], axis=0).T[0 : padded_rows(h)]
    details, last = [], []
    for d in range(DEPTH):
        last.append(base2[d] + dot(lhs, jnp.where(iota((64, 128), 0) % 4 == d, other2, 0.0)))
        nodes = base1[d] + dot(lhs1, jnp.where(iota((16, 128), 0) % 4 == d, other1, 0.0))
        details.append(detail(nodes))
    spread_out(details, h, 128, 4, 2)
    spread_out(last, g, 128, 8, 3)
    for d in range(DEPTH):
        out[d] = jnp.concatenate([out_v[d, j] for j in range(n0 // 128)], axis=1)

    for i, copy in enumerate(halos):
        copy.wait_send()
    pltpu.make_async_copy(xr0, xr0, x_send.at[0]).wait()
    pltpu.make_async_copy(yr0, yr0, y_send.at[0]).wait()
    others = xr1.at[pl.ds(1, gx_n - 1)]
    pltpu.make_async_copy(others, others, x_send.at[1]).wait()
    others = yr1.at[pl.ds(1, gy_n - 1)]
    pltpu.make_async_copy(others, others, y_send.at[1]).wait()


def even_rows(tall_v, value, rows_c):
    rows, lanes = value.shape
    half = rows // 2
    parts = []
    for j in range(lanes // 128):
        tall_v[j, 0:rows] = value[:, 128 * j : 128 * j + 128]
        part = tall_v[j, pl.ds(0, half, stride=2), :]
        parts.append(jnp.concatenate([part, jnp.zeros((rows_c - half, 128), jnp.float32)], axis=0))
    return jnp.concatenate(parts, axis=1)


def add_rows(ref, d, value, stride):
    place = pl.ds(0, value.shape[0], stride=stride)
    for j in range(ref.shape[1]):
        ref[d, j, place, :] = ref[d, j, place, :] + value[:, 128 * j : 128 * j + 128]


def shards(salinity):
    gx_n, gy_n = lax.axis_size("gx"), lax.axis_size("gy")
    _, nx, ny = salinity.shape
    n0 = nx
    (row_tab, row_places), (col_tab, col_places) = tables(nx * gx_n, ny * gy_n, gx_n, gy_n)
    vmem = lambda *shape: pltpu.VMEM(shape, jnp.float32)
    dma = lambda count: pltpu.SemaphoreType.DMA((count,))
    wide, wide_c = padded_lanes(n0), padded_lanes(n0 // 2)
    second = vmem(DEPTH, padded_rows(n0 // 2), padded_lanes(n0 // 2))
    scratch = [vmem(DEPTH, n0 // 128, n0, 128), vmem(DEPTH, 2, n0, 128), second, vmem(DEPTH, n0, n0), second, vmem(2, padded_rows(n0), 128)]
    scratch += [vmem(*row_tab.shape[1:]), vmem(*col_tab.shape[1:])]
    scratch += [vmem(DEPTH, n0), vmem(DEPTH, n0), vmem(DEPTH, 128)] * 2
    scratch += [vmem(2, DEPTH, wide), vmem(gx_n - 1, DEPTH, wide)]
    scratch += [vmem(2, DEPTH, wide_c), vmem(gy_n - 1, DEPTH, wide_c)]
    scratch += [vmem(8, 128), vmem(gx_n, 8, 128), vmem(8, 128), vmem(gy_n, 8, 128)]
    scratch += [dma(4), dma(3), dma(3), dma(2), dma(2), dma(2), dma(2)]
    anywhere = pl.BlockSpec(memory_space=pl.ANY)
    out = pl.pallas_call(
        functools.partial(kernel, gx_n, gy_n, n0, row_places, col_places),
        out_shape=jax.ShapeDtypeStruct(salinity.shape, jnp.float32),
        in_specs=[anywhere] * 3,
        out_specs=pl.BlockSpec(memory_space=pltpu.VMEM),
        scratch_shapes=scratch,
        compiler_params=pltpu.CompilerParams(
            collective_id=0, has_side_effects=True, vmem_limit_bytes=VMEM_LIMIT
        ),
    )(salinity, row_tab, col_tab)
    return out


def solution(mesh):
    placed = P(None, "gx", "gy")
    return jax.shard_map(shards, mesh=mesh, in_specs=(placed,), out_specs=placed, check_vma=False)
```

```python
import functools

import jax
import jax.numpy as jnp
import numpy as np
from jax import lax
from jax.experimental import pallas as pl
from jax.experimental.pallas import tpu as pltpu
from jax.sharding import PartitionSpec as P

LEVELS = 3
DEPTH = 4
LENGTH = 64.0
MESH = pl.DeviceIdType.MESH
TABLE_LANES = 384
INNER = {8: 2, 32: 8}
VMEM_LIMIT = 52 * 1024 * 1024


def padded_rows(count):
    return count + 8


def padded_lanes(count):
    return (count // 128 + 1) * 128 if count >= 128 else 128


def partner(me, slot, tiles, sign):
    inner = INNER.get(tiles, 1)
    outer = tiles // inner
    far = (me // inner + outer + sign * (slot // inner)) % outer
    return far * inner + (me % inner + inner + sign * (slot % inner)) % inner


def farthest_first(tiles):
    inner = INNER.get(tiles, 1)
    outer = tiles // inner
    hops = lambda k: min(k // inner, outer - k // inner) + min(k % inner, inner - k % inner)
    return sorted(range(1, tiles), key=lambda k: -hops(k))


def solver_line(count):
    off = 1.0 / (3.0 * LENGTH) - LENGTH
    inner = 4.0 / (3.0 * LENGTH) + 2.0 * LENGTH
    end = 2.0 / (3.0 * LENGTH) + LENGTH
    diag = np.full(count, inner)
    diag[0] = diag[-1] = end
    q = np.ones(count)
    p = np.ones(count)
    q[1] = -diag[0] / off
    p[-2] = -diag[-1] / off
    for i in range(1, count - 1):
        q[i + 1] = -(diag[i] * q[i]) / off - q[i - 1]
        j = count - 1 - i
        p[j - 1] = -(diag[j] * p[j]) / off - p[j + 1]
    return q, p, diag[0] * p[0] + off * p[1]


def load_block(total, coarse_ids, fine_ids):
    out = np.zeros((len(coarse_ids), len(fine_ids)))

    def mass(i, j):
        if i < 0 or i >= total or j < 0 or j >= total:
            return 0.0
        if i == j:
            return (2.0 if i in (0, total - 1) else 4.0) / 6.0
        return 1.0 / 6.0 if abs(i - j) == 1 else 0.0

    for a, k in enumerate(coarse_ids):
        if k < 0 or k >= total // 2:
            continue
        upper = 1.0 if 2 * k + 1 == total - 1 else 0.5
        for b in range(max(0, 2 * k - 2 - fine_ids[0]), min(len(fine_ids), 2 * k + 3 - fine_ids[0])):
            j = fine_ids[b]
            out[a, b] = mass(2 * k, j) + 0.5 * mass(2 * k - 1, j) + upper * mass(2 * k + 1, j)
    return out


def line_tables(total, tiles):
    n = total // tiles
    h = n // 2
    coarse = total // 2
    q, p, w = solver_line(coarse)
    local, functional, carry, weight, select = [], [], [], [], []
    for t in range(tiles):
        first = t * h
        last_tile = t == tiles - 1
        ids = np.arange(first, first + h + 1)
        if last_tile:
            ids[h] = ids[h - 2]
        window = np.arange(first - 1, first + h + 2)
        load = load_block(total, window, np.arange(t * n, t * n + n + 1))
        inside = (window >= 0) & (window < coarse)
        safe = np.clip(window, 0, coarse - 1)
        low = np.minimum(ids[:, None], safe[None, :])
        high = np.maximum(ids[:, None], safe[None, :])
        green = np.where(inside[None, :], q[low] * p[high] / w, 0.0)
        local.append(green @ load)
        q_end = q[min(first + h, coarse - 1)]
        to_right = (np.where(inside, q[safe] / q_end, 0.0)) @ load
        to_left = (np.where(inside, p[safe] / p[first], 0.0)) @ load
        to_right[n] = 0.0
        to_left[0] = 0.0
        functional.append(np.stack([to_right, to_left]))
        carry.append(np.stack([p[ids] / p[first], q[ids] / q_end]))
        weights = np.zeros((2, tiles))
        for k in range(1, tiles):
            s = partner(t, k, tiles, -1)
            if s < t:
                weights[0, k] = q[(s + 1) * h] * p[first] / w
            else:
                weights[1, k] = q_end * p[s * h] / w
        weight.append(weights)
        pick = np.zeros((n + 1, h + 1))
        pick[2 * np.arange(h), np.arange(h)] = 1.0
        pick[n - 4 if last_tile else n, h] = 1.0
        select.append(pick)
    return [np.stack(item) for item in (local, functional, carry, weight, select)]


def fit(array, shape):
    out = np.zeros(array.shape[: array.ndim - len(shape)] + tuple(shape))
    out[tuple(slice(0, size) for size in array.shape)] = array
    return out


def interpolation(nodes):
    out = np.eye(nodes)
    for i in range(1, nodes, 2):
        out[i] = 0.0
        out[i, i - 1] = out[i, i + 1] = 0.5
    return out


def pair_weights(weight):
    tiles = weight.shape[0]
    out = np.zeros((tiles, tiles, 2, 2))
    for t in range(tiles):
        for k in range(1, tiles):
            for way in range(2):
                out[t, partner(t, k, tiles, -1), way, way] = weight[t, way, k]
    return out


def joined_weights(first, couplings, second):
    tiles = first.shape[0]
    blocks = [first]
    blocks += [np.einsum("tsab,sbc,sucd->tuad", second, k, first) for k in couplings]
    blocks.append(second)
    out = np.zeros((tiles, 4, 2, DEPTH, tiles, 2, DEPTH))
    for t in range(tiles):
        for slot in range(tiles):
            for d in range(DEPTH):
                for i, block in enumerate(blocks):
                    out[t, i, :, d, slot, :, d] = block[t, partner(t, slot, tiles, -1)]
    return out.reshape(tiles, 32, tiles * 8)


def packed(tables):
    places, blocks, at = {}, [], 0
    for name, table in tables.items():
        rows, lanes = -(-table.shape[1] // 8) * 8, -(-table.shape[2] // 128) * 128
        table = fit(table, (rows, lanes))
        places[name] = (at, rows, lanes // 128)
        at += rows * (lanes // 128)
        blocks += [table[:, :, 128 * j : 128 * j + 128] for j in range(lanes // 128)]
    return np.ascontiguousarray(np.concatenate(blocks, axis=1), np.float32), places


@functools.lru_cache(maxsize=None)
def tables(nx, ny, gx, gy):
    row_vecs = np.zeros((gx, 8 * LEVELS + 8, TABLE_LANES))
    col_vecs = np.zeros((gy, 8 * LEVELS + 8, TABLE_LANES))
    row_out, col_out, sides = {}, {}, []
    for vecs, size, tiles, out in ((row_vecs, nx, gx, row_out), (col_vecs, ny, gy, col_out)):
        lines = [line_tables(size >> level, tiles) for level in range(LEVELS)]
        sides.append(lines)
        for level, (local, functional, carry, weight, select) in enumerate(lines):
            n = (size >> level) // tiles
            h = n // 2
            vecs[:, 8 * level : 8 * level + 2, : n + 1] = functional
            vecs[:, 8 * level + 2 : 8 * level + 4, : h + 1] = carry
            if vecs is row_vecs:
                out[f"mat{level}"] = fit(local, (padded_rows(h), padded_lanes(n)))
                if level == 0:
                    vecs[:, 4, : h + 1] = local[:, :, n - 1]
                    vecs[:, 5, : h + 1] = local[:, :, n]
            else:
                joined = np.concatenate([local, functional], axis=1).transpose(0, 2, 1)
                out[f"mat{level}"] = fit(joined, (padded_lanes(n), padded_lanes(h)))
        out["weight"] = np.repeat(lines[0][3].reshape(tiles, 2 * tiles, 1), 128, axis=2)
    nodes = (nx // gx >> 2) + 1
    inter = interpolation(nodes)
    rest = np.eye(nodes) - inter
    (local_a, _, carry_a, weight_a, select_a), (local_b, func_b, carry_b, weight_b, select_b) = sides[0][1:]
    row_k = [np.einsum("tbi,ij,taj->tba", func_b, op, carry_a) for op in (rest, inter)]
    row_out["join"] = joined_weights(pair_weights(weight_a), row_k, pair_weights(weight_b))
    after = np.zeros((gx, 384, 128))
    half = carry_b.shape[2]
    taken = np.zeros((gx, 8, TABLE_LANES))
    for i, op in enumerate((rest, inter)):
        func = func_b @ op
        row_vecs[:, 12 + 2 * i : 14 + 2 * i, : local_a.shape[2]] = np.einsum("tij,tjk->tik", func, local_a)
        taken[:, 2 * i : 2 * i + 2, : select_a.shape[1]] = np.einsum("tij,tkj->tik", func, select_a)
        row_vecs[:, 20 + 2 * i : 22 + 2 * i, :half] = np.einsum("tij,taj->tai", local_b @ op, carry_a)
        after[:, 128 * i : 128 * i + nodes, :half] = (local_b @ op).transpose(0, 2, 1)
        after[:, 128 * i + nodes + 2 * i : 128 * i + nodes + 2 * i + 2, :half] = carry_b
    after[:, 256 : 256 + nodes, :half] = select_b
    row_vecs[:, 24:26, :half] = carry_a @ select_b
    row_out.update(after=after, taken=taken, vecs=row_vecs)
    (_, _, carry_a, weight_a, _), (local_b, func_b, _, weight_b, select_b) = sides[1][1:]
    col_k = [np.einsum("tbi,ij,taj->tba", func_b, op, carry_a) for op in (np.eye(nodes), rest)]
    col_out["join"] = joined_weights(pair_weights(weight_a), col_k, pair_weights(weight_b))
    after = np.zeros((gy, 384, 128))
    col_vecs[:, 12:14, :nodes] = func_b @ rest
    both = np.concatenate([local_b, func_b], axis=1)
    for i, op in enumerate((np.eye(nodes), rest)):
        col_vecs[:, 20 + 2 * i : 22 + 2 * i, :half] = np.einsum("tij,taj->tai", local_b @ op, carry_a)
        after[:, 128 * i : 128 * i + nodes, : both.shape[1]] = (both @ op).transpose(0, 2, 1)
    after[:, 256 : 256 + nodes, :half] = select_b
    col_vecs[:, 24:26, :half] = carry_a @ select_b
    col_out.update(after=after, vecs=col_vecs)
    return packed(row_out), packed(col_out)


def parts(value, count):
    out = []
    for _ in range(count):
        out.append(value.astype(jnp.bfloat16))
        value = value - out[-1].astype(jnp.float32)
    return out


def dot(a, b, dims=((1,), (0,))):
    return lax.dot_general(
        a, b, (dims, ((), ())), precision=lax.Precision.HIGHEST, preferred_element_type=jnp.float32
    )


def pick_dot(a, b, count=3, dims=((1,), (0,)), ones=1):
    total = None
    for part in reversed(parts(b if ones == 0 else a, count)):
        x, y = (a.astype(jnp.bfloat16), part) if ones == 0 else (part, b.astype(jnp.bfloat16))
        term = lax.dot_general(x, y, (dims, ((), ())), preferred_element_type=jnp.float32)
        total = term if total is None else total + term
    return total


def iota(shape, dim):
    return lax.broadcasted_iota(jnp.int32, shape, dim)


def detail(u, alone=False):
    rows, lanes = u.shape
    lane, row = iota(u.shape, 1), iota(u.shape, 0)
    left, right = pltpu.roll(u, 1, 1), pltpu.roll(u, lanes - 1, 1)
    if alone:
        right = jnp.where(lane == lanes - 1, left, right)
    along = jnp.where(lane % 2 == 1, 0.5 * (left + right), u)
    above, below = pltpu.roll(along, 1, 0), pltpu.roll(along, rows - 1, 0)
    if alone:
        below = jnp.where(row == rows - 1, above, below)
    return u - jnp.where(row % 2 == 1, 0.5 * (above + below), along)


def spread_matrix(count, lanes, stride, width):
    shape = (lanes, width)
    row = iota(shape, 0)
    return jnp.where((iota(shape, 1) == stride * row) & (row < count), 1.0, 0.0).astype(jnp.float32)


def kernel(gx_n, gy_n, n0, row_places, col_places, *refs):
    (sal, row_in, col_in, out, out_v, u0, u1, w0, w1, tall_v, row_v, col_v,
     hrow, hcol, hcorner, hrow_in, hcol_in, hcorner_in, xs0, xr0, ys0, yr0, xs1, xr1, ys1, yr1,
     load_sem, halo_send, halo_recv, x_send, x_recv, y_send, y_recv) = refs

    def table(ref, places, name):
        at, rows, tiles = places[name]
        return jnp.concatenate([ref[at + j * rows : at + (j + 1) * rows] for j in range(tiles)], axis=1)

    row_table = functools.partial(table, row_v, row_places)
    col_table = functools.partial(table, col_v, col_places)
    gx, gy = lax.axis_index("gx"), lax.axis_index("gy")
    last_x, last_y = gx == gx_n - 1, gy == gy_n - 1

    barrier = pltpu.get_barrier_semaphore()
    x_peers = [(k, (partner(gx, k, gx_n, 1), gy)) for k in farthest_first(gx_n)]
    y_peers = [(k, (gx, partner(gy, k, gy_n, 1))) for k in farthest_first(gy_n)]
    up, left = lax.rem(gx + gx_n - 1, gx_n), lax.rem(gy + gy_n - 1, gy_n)
    greeted = [peer for _, peer in y_peers + x_peers] + [(lax.rem(gx + 1, gx_n), lax.rem(gy + 1, gy_n))]
    for peer in greeted:
        pl.semaphore_signal(barrier, inc=1, device_id=peer, device_id_type=MESH)

    loads = [
        pltpu.make_async_copy(sal.at[:, :, pl.ds(128 * j, 128)], u0.at[:, j], load_sem.at[j]) for j in range(2)
    ]
    loads.append(pltpu.make_async_copy(row_in.at[gx], row_v, load_sem.at[2]))
    loads.append(pltpu.make_async_copy(col_in.at[gy], col_v, load_sem.at[3]))
    for copy in loads:
        copy.start()

    loads[0].wait()
    loads[1].wait()
    hrow[...] = jnp.concatenate([u0[:, 0, 0, :], u0[:, 1, 0, :]], axis=1)
    hcorner[...] = u0[:, 0, 0, :]
    lane = iota((n0, 128), 1)
    packed = jnp.zeros((n0, 128), jnp.float32)
    for d in range(DEPTH):
        packed = jnp.where(lane == d, u0[d, 0, :, 0:1], packed)
        packed = jnp.where(lane == 4 + d, u0[d, 1, :, 126:127], packed)
    packed = packed.T
    hcol[...] = packed[0:4]
    def send_all(peers, axis, me, count, src, dst, send, recv):
        for k, peer in peers:
            way = (me + count - peer[axis]) // count
            pltpu.make_async_remote_copy(
                src_ref=src.at[way], dst_ref=dst.at[k - 1], send_sem=send, recv_sem=recv,
                device_id=peer, device_id_type=MESH,
            ).start()

    def send_same(peers, src, dst, send, recv):
        for k, peer in peers:
            pltpu.make_async_remote_copy(
                src_ref=src, dst_ref=dst.at[k], send_sem=send, recv_sem=recv, device_id=peer, device_id_type=MESH
            ).start()

    def gather(buf, ref, places, count):
        at, _, _ = places["weight"]
        tiles = buf.shape[2] // 128
        sums = [jnp.zeros(buf.shape[1:], jnp.float32)] * 2
        for k in range(1, count):
            for way in range(2):
                weight = ref[at + way * count + k : at + way * count + k + 1, :]
                sums[way] = sums[way] + jnp.concatenate([weight] * tiles, axis=1) * buf[k - 1]
        return sums

    def selection(n, last):
        shape = (padded_lanes(n), padded_lanes(n // 2))
        row, lane = iota(shape, 0), iota(shape, 1)
        tail = jnp.where(last, n - 4, n)
        hit = ((lane < n // 2) & (row == 2 * lane)) | ((lane == n // 2) & (row == tail))
        return jnp.where(hit, 1.0, 0.0)

    def local_level(level, n, u, w):
        h = n // 2
        rows, rows_c, lanes_c = padded_rows(n), padded_rows(h), padded_lanes(h)
        col_mat, row_mat = col_table(f"mat{level}"), row_table(f"mat{level}")[:, 0:rows]
        select = selection(n, last_y)
        base, solved = [], []
        is_tail = iota((rows_c, lanes_c), 0) == h
        for d in range(DEPTH):
            z = dot(row_mat, dot(w[d], col_mat))
            even = even_rows(tall_v, pick_dot(u[d], select), rows_c)
            even = jnp.where(is_tail & last_x, even[h - 2 : h - 1, :], even)
            base.append(jnp.where(iota((rows_c, lanes_c), 1) <= h, z, 0.0) + even)
            solved.append(z)
        return base, solved

    def row_sums(values, weights, count=2):
        sums = []
        for way in range(count):
            for d in range(DEPTH):
                rows = values[d].shape[0]
                sums.append(jnp.sum(values[d] * weights[0:rows, way : way + 1], axis=0, keepdims=True))
        return jnp.concatenate(sums, axis=0)

    def line(value, functional):
        return jnp.sum(value * functional, axis=1, keepdims=True)

    def twice(table, row, lanes):
        return jnp.concatenate(
            [jnp.broadcast_to(table[row + way : row + way + 1, 0:lanes], (4, lanes)) for way in range(2)], axis=0
        )

    def outer(column, table, row, lanes):
        return (
            column[0:4] * table[row : row + 1, 0:lanes] + column[4:8] * table[row + 1 : row + 2, 0:lanes]
        )

    def spread_out(values, count, lanes, stride, pieces):
        mat = spread_matrix(count, lanes, stride, n0)
        for d in range(DEPTH):
            add_rows(out_v, d, pick_dot(values[d][0:count], mat, pieces), stride)

    n, h = n0, n0 // 2
    wide, rows_c, lanes_c = padded_lanes(n), padded_rows(h), padded_lanes(h)
    for copy in loads[2:]:
        copy.wait()
    rv, cv = row_table("vecs"), col_table("vecs")
    col_q = cv[0:2, 0:n]
    own_cols = jnp.zeros((n, 128), jnp.float32)
    for d in range(DEPTH):
        if d == DEPTH // 2:
            pl.semaphore_wait(barrier, len(greeted))
            halos = []
            for i, (src, dst, peer) in enumerate(
                ((hrow, hrow_in, (up, gy)), (hcol, hcol_in, (gx, left)), (hcorner, hcorner_in, (up, left)))
            ):
                copy = pltpu.make_async_remote_copy(
                    src_ref=src, dst_ref=dst, send_sem=halo_send.at[i], recv_sem=halo_recv.at[i],
                    device_id=peer, device_id_type=MESH,
                )
                copy.start()
                halos.append(copy)
        value = detail(jnp.concatenate([u0[d, 0], u0[d, 1]], axis=1), True)
        w0[d] = value
        for way in range(2):
            own_cols = jnp.where(lane == 4 * way + d, line(value, col_q[way : way + 1]), own_cols)
    own_rows = row_sums([w0[d] for d in range(DEPTH)], rv[0:8, 0:n].T)
    own_cols = own_cols.T[0:8]
    none = jnp.zeros((8, 128), jnp.float32)
    own_rows = jnp.concatenate([own_rows, none], axis=1)
    own_cols = jnp.concatenate([own_cols, none], axis=1)

    for copy in halos:
        copy.wait_recv()
    at = iota((4, wide), 1)
    own_254 = jnp.concatenate([u0[:, 0, n - 2, :], u0[:, 1, n - 2, :]], axis=1)
    next_row = jnp.where(last_x, own_254, hrow_in[...])
    next_col = jnp.where(last_y, packed[4:8], hcol_in[...])
    corner = jnp.where(
        last_y, next_row[:, n - 2 : n - 1], jnp.where(last_x, next_col[:, n - 2 : n - 1], hcorner_in[:, 0:1])
    )
    alias = packed[4:8, n - 2 : n - 1]
    wider = lambda value, end: jnp.where(at == n, end, jnp.concatenate([value, none[0:4]], axis=1))
    row_change, col_change = wider(next_row - own_254, 0.0), wider(next_col - packed[4:8], corner - alias)
    next_row, next_col = wider(next_row, alias), wider(next_col, corner)

    def between(value):
        mean = 0.5 * (pltpu.roll(value, 1, 1) + pltpu.roll(value, wide - 1, 1))
        return jnp.where(at > n, 0.0, jnp.where(at % 2 == 1, mean, value))

    row_255, row_256 = -0.5 * between(row_change), next_row - between(next_row)
    col_255, col_256 = -0.5 * between(col_change), next_col - between(next_col)
    for way in range(2):
        q = rv[way : way + 1, 0:wide]
        xs0[way] = (
            own_rows[4 * way : 4 * way + 4]
            + q[:, n - 1 : n] * row_255
            + q[:, n : n + 1] * row_256
            + jnp.where(at == n - 1, line(col_255, q), 0.0)
            + jnp.where(at == n, line(col_256, q), 0.0)
        )
    send_all(x_peers, 0, gx, gx_n, xs0, xr0, x_send.at[0], x_recv.at[0])
    cols = []
    for way in range(2):
        q = cv[way : way + 1, 0:wide]
        cols.append(
            own_cols[4 * way : 4 * way + 4]
            + q[:, n - 1 : n] * col_255
            + q[:, n : n + 1] * col_256
            + jnp.where(at == n - 1, line(row_255, q), 0.0)
            + jnp.where(at == n, line(row_256, q), 0.0)
        )
    down_x = dot(jnp.concatenate(cols + [col_255, col_256], axis=0), row_table("mat0"), ((1,), (1,)))
    down_x = jnp.concatenate([down_x, jnp.zeros((16, lanes_c - rows_c), jnp.float32)], axis=1)
    select = selection(n, last_y)[0:n]
    next_even = pick_dot(next_row[:, 0:n], select)
    next_col_even = jnp.where(last_y, 0.0, pick_dot(next_col, selection(n, last_x)))
    evens = []
    for d in range(DEPTH):
        even = jnp.concatenate([u0[d, j, pl.ds(0, h, stride=2), :] for j in range(2)], axis=1)
        even = pick_dot(even, select)
        tail = jnp.where(last_x, even[h - 2 : h - 1], next_even[d : d + 1])
        tail = jnp.where(iota((8, lanes_c), 0) == 0, tail, 0.0)
        evens.append(jnp.concatenate([even, tail], axis=0))

    pltpu.make_async_copy(xr0, xr0, x_recv.at[0]).wait()
    a_right, a_left = gather(xr0, row_v, row_places, gx_n)
    q_r, q_l = cv[0:1, 0:wide], cv[1:2, 0:wide]
    p_r, p_l = rv[2:3, 0:lanes_c], rv[3:4, 0:lanes_c]
    layer = iota((4, 128), 0) == iota((4, 128), 1)
    for way, q in enumerate((q_r, q_l)):
        cols = down_x[4 * way : 4 * way + 4] + line(a_right, q) * p_r + line(a_left, q) * p_l
        ys0[way, 0:4] = cols[:, 0:h]
        ys0[way, 4:5] = jnp.sum(jnp.where(layer, cols[:, h : h + 1], 0.0), axis=0, keepdims=True)
    send_all(y_peers, 1, gy, gy_n, ys0, yr0, y_send.at[0], y_recv.at[0])
    col_mat, row_mat = col_table("mat0"), row_table("mat0")
    is_node = iota((1, lanes_c), 1) <= h
    base = []
    for d in range(DEPTH):
        z = dot(row_mat[:, 0:n], dot(w0[d], col_mat[0:n]))
        base.append(jnp.where(is_node, z, 0.0) + evens[d])
    down_turned = jnp.concatenate([col_255, col_255], axis=0).T[0:n]
    is_last = iota((n, 128), 1) == 127
    for d in range(DEPTH):
        out_v[d, 0] = w0[d, :, 0:128]
        out_v[d, 1] = w0[d, :, 128:256] + jnp.where(is_last, down_turned[:, d : d + 1], 0.0)
        for j in range(2):
            tail = iota((8, 128), 0) == 7
            fix = row_255[d : d + 1, 128 * j : 128 * j + 128]
            out_v[d, j, n - 8 : n, :] = out_v[d, j, n - 8 : n, :] + jnp.where(tail, fix, 0.0)
    carried = dot(jnp.concatenate([a_right, a_left, row_255, row_256], axis=0), col_mat)
    four = lambda row: jnp.broadcast_to(row, (4, lanes_c))
    other = jnp.concatenate(
        [jnp.where(is_node, carried, 0.0), twice(cv, 2, lanes_c)]
        + [four(jnp.where(is_node, col_mat[n - 1 + i : n + i, :], 0.0)) for i in range(2)]
        + [four(jnp.where(iota((1, lanes_c), 1) == h, 1.0, 0.0)), jnp.zeros((4, lanes_c), jnp.float32)],
        axis=0,
    )
    own = jnp.concatenate([twice(rv, 2, lanes_c), twice(rv, 4, lanes_c)], axis=0)
    rest = jnp.concatenate([down_x[8:16], next_col_even, jnp.zeros((4, lanes_c), jnp.float32)], axis=0)
    pltpu.make_async_copy(yr0, yr0, y_recv.at[0]).wait()
    ends = []
    for value in gather(yr0, col_v, col_places, gy_n):
        tail = line(jnp.where(layer, jnp.broadcast_to(value[4:5], (4, 128)), 0.0), 1.0)
        ends.append(jnp.concatenate([value[0:4], jnp.where(iota((4, 128), 1) == 0, tail, 0.0)], axis=1))
    c_right, c_left = ends
    lhs = jnp.concatenate([own, c_right, c_left, rest], axis=0).T[0:rows_c]
    for d in range(DEPTH):
        u1[d] = base[d] + dot(lhs, jnp.where(iota((40, lanes_c), 0) % 4 == d, other, 0.0))

    n, h, g = n0 // 2, n0 // 4, n0 // 8
    lane = iota((8, 128), 1)
    for d in range(DEPTH):
        w1[d] = detail(u1[d])
    ways = jnp.concatenate([rv[8:16, 0:256], row_table("taken")[:, 0:256]], axis=0).T
    functionals = jnp.concatenate([ways[:, 0:2], ways[:, 4:8]], axis=1)
    of_w = dot(row_sums([w1[d] for d in range(DEPTH)], functionals, 6), col_table("mat1"))
    taken = row_sums([u1[d] for d in range(DEPTH)], ways[:, 8:12], 4)
    of_next = of_w[8:24] + pick_dot(taken, selection(n, last_y))
    after = col_table("after")
    of_second = dot(jnp.concatenate([of_next[0:8], of_next[8:16]], axis=1), after[0:256])
    is_c = (lane == h + 1) | (lane == h + 2)
    sent = of_w[0:8] + pltpu.roll(of_second, h + 3, 1)
    for i in range(2):
        sent += pltpu.roll(jnp.where(is_c, of_w[8 + 8 * i : 16 + 8 * i], 0.0), g + 5 + 2 * i, 1)
    xs1[...] = sent
    xr1[0] = sent
    send_same(x_peers, xs1, xr1, x_send.at[1], x_recv.at[1])
    base1, solved1 = local_level(1, n, u1, w1)
    cols = jnp.zeros((padded_rows(h), 128), jnp.float32)
    spot = iota(cols.shape, 1)
    for d in range(DEPTH):
        for way in range(2):
            cols = jnp.where(spot == 4 * way + d, solved1[d][:, h + 1 + way : h + 2 + way], cols)
            cols = jnp.where(spot == 8 + 4 * way + d, line(base1[d], cv[16 + way : 17 + way, 0:128]), cols)
            cols = jnp.where(spot == 16 + 4 * way + d, line(base1[d], cv[12 + way : 13 + way, 0:128]), cols)
    cols = jnp.concatenate([cols, jnp.zeros((128 - padded_rows(h), 128), jnp.float32)], axis=0).T
    row_after = row_table("after")
    cols1, cols2 = cols[0:8], dot(jnp.concatenate([cols[8:16], cols[16:24]], axis=1), row_after[0:256])
    others = xr1.at[pl.ds(1, gx_n - 1)]
    pltpu.make_async_copy(others, others, x_recv.at[1]).wait()
    got = dot(row_table("join")[:, 0 : gx_n * 8], xr1[...].reshape(gx_n * 8, 128))
    a_1 = got[0:8]
    a_2 = pltpu.roll(got[24:32], 128 - (h + 3), 1) + dot(
        jnp.concatenate([got[8:16], got[16:24]], axis=1), after[0:256]
    )
    msg, msg2, hs = [], [], []
    for way in range(2):
        msg.append(cols1[4 * way : 4 * way + 4] + outer(a_1[:, h + 1 + way : h + 2 + way], rv, 10, 128))
        row = outer(line(a_1, cv[16 + way : 17 + way, 0:128]), rv, 20, 128)
        row += outer(line(a_1, cv[12 + way : 13 + way, 0:128]), rv, 22, 128)
        row += outer(a_2[:, g + 1 + way : g + 2 + way], rv, 18, 128)
        msg2.append(cols2[4 * way : 4 * way + 4] + row)
        block = jnp.zeros((4, 128), jnp.float32)
        for i in range(2):
            at = h + g + 6 + 2 * i + way
            h_col = got[24:32, at : at + 1] + got[8 + 8 * i : 16 + 8 * i, h + 1 + way : h + 2 + way]
            for x_way in range(2):
                block += jnp.where(iota((4, 128), 1) == h + 1 + 2 * i + x_way, h_col[4 * x_way : 4 * x_way + 4], 0.0)
        hs.append(block)
    sent = jnp.concatenate(msg, axis=0) + pltpu.roll(jnp.concatenate(msg2, axis=0), h + 5, 1)
    sent += jnp.concatenate(hs, axis=0)
    ys1[...] = sent
    yr1[0] = sent
    send_same(y_peers, ys1, yr1, y_send.at[1], y_recv.at[1])
    base2, _ = local_level(2, h, base1, [detail(base1[d]) for d in range(DEPTH)])
    spread_out([w1[d] for d in range(DEPTH)], n, 256, 2, 2)
    beside = lambda value: jnp.concatenate([value[128 * i : 128 * i + 128] for i in range(3)], axis=1)
    nodes_1 = lambda value: jnp.where(lane <= h, value, 0.0)
    nodes_2 = lambda value: jnp.where(lane <= g, value, 0.0)
    other1 = jnp.concatenate([nodes_1(a_1), twice(cv, 10, 128)], axis=0)
    across = dot(a_1, beside(after))
    other2 = jnp.concatenate(
        [nodes_2(across[:, 256:384]), nodes_2(across[:, 0:128]), nodes_2(across[:, 128:256]), nodes_2(a_2)]
        + [twice(cv, row, 128) for row in (24, 20, 22, 18)],
        axis=0,
    )
    own = jnp.concatenate([twice(rv, row, 128) for row in (24, 20, 22, 18)], axis=0)
    row_after = beside(row_after)
    others = yr1.at[pl.ds(1, gy_n - 1)]
    pltpu.make_async_copy(others, others, y_recv.at[1]).wait()
    got = dot(col_table("join"), yr1[...].reshape(gy_n * 8, 128))
    down = dot(got[0:24], row_after)
    c_2 = nodes_2(pltpu.roll(got[24:32], 128 - (h + 5), 1) + down[8:16, 0:128] + down[16:24, 128:256])
    lhs = jnp.concatenate([own, down[0:8, 256:384], down[0:8, 0:128], down[0:8, 128:256], c_2], axis=0)
    lhs = jnp.concatenate([lhs, jnp.zeros_like(lhs)], axis=0).T[0 : padded_rows(g), 0:64]
    lhs1 = jnp.concatenate([twice(rv, 10, 128), nodes_1(got[0:8])], axis=0).T[0 : padded_rows(h)]
    details, last = [], []
    for d in range(DEPTH):
        last.append(base2[d] + dot(lhs, jnp.where(iota((64, 128), 0) % 4 == d, other2, 0.0)))
        nodes = base1[d] + dot(lhs1, jnp.where(iota((16, 128), 0) % 4 == d, other1, 0.0))
        details.append(detail(nodes))
    spread_out(details, h, 128, 4, 2)
    spread_out(last, g, 128, 8, 3)
    for d in range(DEPTH):
        out[d] = jnp.concatenate([out_v[d, j] for j in range(n0 // 128)], axis=1)

    for i, copy in enumerate(halos):
        copy.wait_send()
    pltpu.make_async_copy(xr0, xr0, x_send.at[0]).wait()
    pltpu.make_async_copy(yr0, yr0, y_send.at[0]).wait()
    others = xr1.at[pl.ds(1, gx_n - 1)]
    pltpu.make_async_copy(others, others, x_send.at[1]).wait()
    others = yr1.at[pl.ds(1, gy_n - 1)]
    pltpu.make_async_copy(others, others, y_send.at[1]).wait()


def even_rows(tall_v, value, rows_c):
    rows, lanes = value.shape
    half = rows // 2
    parts = []
    for j in range(lanes // 128):
        tall_v[j, 0:rows] = value[:, 128 * j : 128 * j + 128]
        part = tall_v[j, pl.ds(0, half, stride=2), :]
        parts.append(jnp.concatenate([part, jnp.zeros((rows_c - half, 128), jnp.float32)], axis=0))
    return jnp.concatenate(parts, axis=1)


def add_rows(ref, d, value, stride):
    place = pl.ds(0, value.shape[0], stride=stride)
    for j in range(ref.shape[1]):
        ref[d, j, place, :] = ref[d, j, place, :] + value[:, 128 * j : 128 * j + 128]


def shards(salinity):
    gx_n, gy_n = lax.axis_size("gx"), lax.axis_size("gy")
    _, nx, ny = salinity.shape
    n0 = nx
    (row_tab, row_places), (col_tab, col_places) = tables(nx * gx_n, ny * gy_n, gx_n, gy_n)
    vmem = lambda *shape: pltpu.VMEM(shape, jnp.float32)
    dma = lambda count: pltpu.SemaphoreType.DMA((count,))
    wide = padded_lanes(n0)
    second = vmem(DEPTH, padded_rows(n0 // 2), padded_lanes(n0 // 2))
    scratch = [vmem(DEPTH, n0 // 128, n0, 128), vmem(DEPTH, 2, n0, 128), second, vmem(DEPTH, n0, n0), second, vmem(2, padded_rows(n0), 128)]
    scratch += [vmem(*row_tab.shape[1:]), vmem(*col_tab.shape[1:])]
    scratch += [vmem(DEPTH, n0), vmem(DEPTH, n0), vmem(DEPTH, 128)] * 2
    scratch += [vmem(2, DEPTH, wide), vmem(gx_n - 1, DEPTH, wide)]
    scratch += [vmem(2, DEPTH + 1, n0 // 2), vmem(gy_n - 1, DEPTH + 1, n0 // 2)]
    scratch += [vmem(8, 128), vmem(gx_n, 8, 128), vmem(8, 128), vmem(gy_n, 8, 128)]
    scratch += [dma(4), dma(3), dma(3), dma(2), dma(2), dma(2), dma(2)]
    anywhere = pl.BlockSpec(memory_space=pl.ANY)
    out = pl.pallas_call(
        functools.partial(kernel, gx_n, gy_n, n0, row_places, col_places),
        out_shape=jax.ShapeDtypeStruct(salinity.shape, jnp.float32),
        in_specs=[anywhere] * 3,
        out_specs=pl.BlockSpec(memory_space=pltpu.VMEM),
        scratch_shapes=scratch,
        compiler_params=pltpu.CompilerParams(
            collective_id=0, has_side_effects=True, vmem_limit_bytes=VMEM_LIMIT
        ),
    )(salinity, row_tab, col_tab)
    return out


def solution(mesh):
    placed = P(None, "gx", "gy")
    return jax.shard_map(shards, mesh=mesh, in_specs=(placed,), out_specs=placed, check_vma=False)
```

```python
import functools

import jax
import jax.numpy as jnp
import numpy as np
from jax import lax
from jax.experimental import pallas as pl
from jax.experimental.pallas import tpu as pltpu
from jax.sharding import PartitionSpec as P

LEVELS = 3
DEPTH = 4
LENGTH = 64.0
MESH = pl.DeviceIdType.MESH
TABLE_LANES = 384
INNER = {8: 2, 32: 8}
VMEM_LIMIT = 52 * 1024 * 1024


def padded_rows(count):
    return count + 8


def padded_lanes(count):
    return (count // 128 + 1) * 128 if count >= 128 else 128


def partner(me, slot, tiles, sign):
    inner = INNER.get(tiles, 1)
    outer = tiles // inner
    far = (me // inner + outer + sign * (slot // inner)) % outer
    return far * inner + (me % inner + inner + sign * (slot % inner)) % inner


def farthest_first(tiles):
    inner = INNER.get(tiles, 1)
    outer = tiles // inner
    hops = lambda k: min(k // inner, outer - k // inner) + min(k % inner, inner - k % inner)
    return sorted(range(1, tiles), key=lambda k: -hops(k))


def solver_line(count):
    off = 1.0 / (3.0 * LENGTH) - LENGTH
    inner = 4.0 / (3.0 * LENGTH) + 2.0 * LENGTH
    end = 2.0 / (3.0 * LENGTH) + LENGTH
    diag = np.full(count, inner)
    diag[0] = diag[-1] = end
    q = np.ones(count)
    p = np.ones(count)
    q[1] = -diag[0] / off
    p[-2] = -diag[-1] / off
    for i in range(1, count - 1):
        q[i + 1] = -(diag[i] * q[i]) / off - q[i - 1]
        j = count - 1 - i
        p[j - 1] = -(diag[j] * p[j]) / off - p[j + 1]
    return q, p, diag[0] * p[0] + off * p[1]


def load_block(total, coarse_ids, fine_ids):
    out = np.zeros((len(coarse_ids), len(fine_ids)))

    def mass(i, j):
        if i < 0 or i >= total or j < 0 or j >= total:
            return 0.0
        if i == j:
            return (2.0 if i in (0, total - 1) else 4.0) / 6.0
        return 1.0 / 6.0 if abs(i - j) == 1 else 0.0

    for a, k in enumerate(coarse_ids):
        if k < 0 or k >= total // 2:
            continue
        upper = 1.0 if 2 * k + 1 == total - 1 else 0.5
        for b in range(max(0, 2 * k - 2 - fine_ids[0]), min(len(fine_ids), 2 * k + 3 - fine_ids[0])):
            j = fine_ids[b]
            out[a, b] = mass(2 * k, j) + 0.5 * mass(2 * k - 1, j) + upper * mass(2 * k + 1, j)
    return out


def line_tables(total, tiles):
    n = total // tiles
    h = n // 2
    coarse = total // 2
    q, p, w = solver_line(coarse)
    local, functional, carry, weight, select, wide = [], [], [], [], [], []
    for t in range(tiles):
        first = t * h
        last_tile = t == tiles - 1
        ids = np.arange(first, first + h + 1)
        if last_tile:
            ids[h] = ids[h - 2]
        window = np.arange(first - 1, first + h + 2)
        load = load_block(total, window, np.arange(t * n, t * n + n + 1))
        inside = (window >= 0) & (window < coarse)
        safe = np.clip(window, 0, coarse - 1)
        low = np.minimum(ids[:, None], safe[None, :])
        high = np.maximum(ids[:, None], safe[None, :])
        green = np.where(inside[None, :], q[low] * p[high] / w, 0.0)
        local.append(green @ load)
        q_end = q[min(first + h, coarse - 1)]
        to_right = (np.where(inside, q[safe] / q_end, 0.0)) @ load
        to_left = (np.where(inside, p[safe] / p[first], 0.0)) @ load
        before = load_block(total, window, np.array([t * n - 1]))
        own = [np.append(f[:n], np.where(inside, v, 0.0) @ before) for f, v in
               ((to_right, q[safe] / q_end), (to_left, p[safe] / p[first]))]
        wide.append(np.stack(own + [own[0] * q_end * p[first] / w]))
        to_right[n] = 0.0
        to_left[0] = 0.0
        functional.append(np.stack([to_right, to_left]))
        carry.append(np.stack([p[ids] / p[first], q[ids] / q_end]))
        weights = np.zeros((2, tiles))
        for k in range(1, tiles):
            s = partner(t, k, tiles, -1)
            if s < t:
                weights[0, k] = q[(s + 1) * h] * p[first] / w
            else:
                weights[1, k] = q_end * p[s * h] / w
        weight.append(weights)
        pick = np.zeros((n + 1, h + 1))
        pick[2 * np.arange(h), np.arange(h)] = 1.0
        pick[n - 4 if last_tile else n, h] = 1.0
        select.append(pick)
    return [np.stack(item) for item in (local, functional, carry, weight, select, wide)]


def fit(array, shape):
    out = np.zeros(array.shape[: array.ndim - len(shape)] + tuple(shape))
    out[tuple(slice(0, size) for size in array.shape)] = array
    return out


def interpolation(nodes):
    out = np.eye(nodes)
    for i in range(1, nodes, 2):
        out[i] = 0.0
        out[i, i - 1] = out[i, i + 1] = 0.5
    return out


def pair_weights(weight):
    tiles = weight.shape[0]
    out = np.zeros((tiles, tiles, 2, 2))
    for t in range(tiles):
        for k in range(1, tiles):
            for way in range(2):
                out[t, partner(t, k, tiles, -1), way, way] = weight[t, way, k]
    return out


def joined_weights(first, couplings, second):
    tiles = first.shape[0]
    blocks = [first]
    blocks += [np.einsum("tsab,sbc,sucd->tuad", second, k, first) for k in couplings]
    blocks.append(second)
    out = np.zeros((tiles, 4, 2, DEPTH, tiles, 2, DEPTH))
    for t in range(tiles):
        for slot in range(tiles):
            for d in range(DEPTH):
                for i, block in enumerate(blocks):
                    out[t, i, :, d, slot, :, d] = block[t, partner(t, slot, tiles, -1)]
    return out.reshape(tiles, 32, tiles * 8)


def packed(tables):
    places, blocks, at = {}, [], 0
    for name, table in tables.items():
        rows, lanes = -(-table.shape[1] // 8) * 8, -(-table.shape[2] // 128) * 128
        table = fit(table, (rows, lanes))
        places[name] = (at, rows, lanes // 128)
        at += rows * (lanes // 128)
        blocks += [table[:, :, 128 * j : 128 * j + 128] for j in range(lanes // 128)]
    return np.ascontiguousarray(np.concatenate(blocks, axis=1), np.float32), places


@functools.lru_cache(maxsize=None)
def tables(nx, ny, gx, gy):
    row_vecs = np.zeros((gx, 8 * LEVELS + 8, TABLE_LANES))
    col_vecs = np.zeros((gy, 8 * LEVELS + 8, TABLE_LANES))
    row_out, col_out, sides = {}, {}, []
    for vecs, size, tiles, out in ((row_vecs, nx, gx, row_out), (col_vecs, ny, gy, col_out)):
        lines = [line_tables(size >> level, tiles) for level in range(LEVELS)]
        sides.append(lines)
        for level, (local, functional, carry, weight, select, wide) in enumerate(lines):
            n = (size >> level) // tiles
            h = n // 2
            vecs[:, 8 * level : 8 * level + 2, : n + 1] = functional
            vecs[:, 8 * level + 2 : 8 * level + 4, : h + 1] = carry
            if level == 0:
                vecs[:, 26:29, :n] = wide[:, :, :n]
                vecs[:, 26:29, n + 1] = wide[:, :, n]
            if vecs is row_vecs:
                out[f"mat{level}"] = fit(local, (padded_rows(h), padded_lanes(n)))
                if level == 0:
                    vecs[:, 4, : h + 1] = local[:, :, n - 1]
                    vecs[:, 5, : h + 1] = local[:, :, n]
            else:
                joined = np.concatenate([local, functional], axis=1).transpose(0, 2, 1)
                out[f"mat{level}"] = fit(joined, (padded_lanes(n), padded_lanes(h)))
        out["weight"] = np.repeat(lines[0][3].reshape(tiles, 2 * tiles, 1), 128, axis=2)
    nodes = (nx // gx >> 2) + 1
    inter = interpolation(nodes)
    rest = np.eye(nodes) - inter
    (local_a, _, carry_a, weight_a, select_a, _), (local_b, func_b, carry_b, weight_b, select_b, _) = sides[0][1:]
    row_k = [np.einsum("tbi,ij,taj->tba", func_b, op, carry_a) for op in (rest, inter)]
    row_out["join"] = joined_weights(pair_weights(weight_a), row_k, pair_weights(weight_b))
    after = np.zeros((gx, 384, 128))
    half = carry_b.shape[2]
    taken = np.zeros((gx, 8, TABLE_LANES))
    for i, op in enumerate((rest, inter)):
        func = func_b @ op
        row_vecs[:, 12 + 2 * i : 14 + 2 * i, : local_a.shape[2]] = np.einsum("tij,tjk->tik", func, local_a)
        taken[:, 2 * i : 2 * i + 2, : select_a.shape[1]] = np.einsum("tij,tkj->tik", func, select_a)
        row_vecs[:, 20 + 2 * i : 22 + 2 * i, :half] = np.einsum("tij,taj->tai", local_b @ op, carry_a)
        after[:, 128 * i : 128 * i + nodes, :half] = (local_b @ op).transpose(0, 2, 1)
        after[:, 128 * i + nodes + 2 * i : 128 * i + nodes + 2 * i + 2, :half] = carry_b
    after[:, 256 : 256 + nodes, :half] = select_b
    row_vecs[:, 24:26, :half] = carry_a @ select_b
    row_out.update(after=after, taken=taken, vecs=row_vecs)
    (_, _, carry_a, weight_a, _, _), (local_b, func_b, _, weight_b, select_b, _) = sides[1][1:]
    col_k = [np.einsum("tbi,ij,taj->tba", func_b, op, carry_a) for op in (np.eye(nodes), rest)]
    col_out["join"] = joined_weights(pair_weights(weight_a), col_k, pair_weights(weight_b))
    after = np.zeros((gy, 384, 128))
    col_vecs[:, 12:14, :nodes] = func_b @ rest
    both = np.concatenate([local_b, func_b], axis=1)
    for i, op in enumerate((np.eye(nodes), rest)):
        col_vecs[:, 20 + 2 * i : 22 + 2 * i, :half] = np.einsum("tij,taj->tai", local_b @ op, carry_a)
        after[:, 128 * i : 128 * i + nodes, : both.shape[1]] = (both @ op).transpose(0, 2, 1)
    after[:, 256 : 256 + nodes, :half] = select_b
    col_vecs[:, 24:26, :half] = carry_a @ select_b
    col_out.update(after=after, vecs=col_vecs)
    return packed(row_out), packed(col_out)


def parts(value, count):
    out = []
    for _ in range(count):
        out.append(value.astype(jnp.bfloat16))
        value = value - out[-1].astype(jnp.float32)
    return out


def dot(a, b, dims=((1,), (0,))):
    return lax.dot_general(
        a, b, (dims, ((), ())), precision=lax.Precision.HIGHEST, preferred_element_type=jnp.float32
    )


def pick_dot(a, b, count=3, dims=((1,), (0,)), ones=1):
    total = None
    for part in reversed(parts(b if ones == 0 else a, count)):
        x, y = (a.astype(jnp.bfloat16), part) if ones == 0 else (part, b.astype(jnp.bfloat16))
        term = lax.dot_general(x, y, (dims, ((), ())), preferred_element_type=jnp.float32)
        total = term if total is None else total + term
    return total


def iota(shape, dim):
    return lax.broadcasted_iota(jnp.int32, shape, dim)


def detail(u, alone=False):
    rows, lanes = u.shape
    lane, row = iota(u.shape, 1), iota(u.shape, 0)
    left, right = pltpu.roll(u, 1, 1), pltpu.roll(u, lanes - 1, 1)
    if alone:
        right = jnp.where(lane == lanes - 1, left, right)
    along = jnp.where(lane % 2 == 1, 0.5 * (left + right), u)
    above, below = pltpu.roll(along, 1, 0), pltpu.roll(along, rows - 1, 0)
    if alone:
        below = jnp.where(row == rows - 1, above, below)
    return u - jnp.where(row % 2 == 1, 0.5 * (above + below), along)


def spread_matrix(count, lanes, stride, width):
    shape = (lanes, width)
    row = iota(shape, 0)
    return jnp.where((iota(shape, 1) == stride * row) & (row < count), 1.0, 0.0).astype(jnp.float32)


def kernel(gx_n, gy_n, n0, row_places, col_places, *refs):
    (sal, row_in, col_in, out, out_v, u0, u1, w0, w1, tall_v, row_v, col_v,
     hrow, hcol, hcorner, hrow_in, hcol_in, hcorner_in, xs0, xr0, ys0, yr0, xs1, xr1, ys1, yr1,
     load_sem, halo_send, halo_recv, x_send, x_recv, y_send, y_recv) = refs

    def table(ref, places, name):
        at, rows, tiles = places[name]
        return jnp.concatenate([ref[at + j * rows : at + (j + 1) * rows] for j in range(tiles)], axis=1)

    row_table = functools.partial(table, row_v, row_places)
    col_table = functools.partial(table, col_v, col_places)
    gx, gy = lax.axis_index("gx"), lax.axis_index("gy")
    last_x, last_y = gx == gx_n - 1, gy == gy_n - 1

    barrier = pltpu.get_barrier_semaphore()
    x_peers = [(k, (partner(gx, k, gx_n, 1), gy)) for k in farthest_first(gx_n)]
    y_peers = [(k, (gx, partner(gy, k, gy_n, 1))) for k in farthest_first(gy_n)]
    up, left = lax.rem(gx + gx_n - 1, gx_n), lax.rem(gy + gy_n - 1, gy_n)
    greeted = [peer for _, peer in y_peers + x_peers] + [(lax.rem(gx + 1, gx_n), lax.rem(gy + 1, gy_n))]
    for peer in greeted:
        pl.semaphore_signal(barrier, inc=1, device_id=peer, device_id_type=MESH)

    loads = [
        pltpu.make_async_copy(sal.at[:, :, pl.ds(128 * j, 128)], u0.at[:, j], load_sem.at[j]) for j in range(2)
    ]
    loads.append(pltpu.make_async_copy(row_in.at[gx], row_v, load_sem.at[2]))
    loads.append(pltpu.make_async_copy(col_in.at[gy], col_v, load_sem.at[3]))
    for copy in loads:
        copy.start()

    loads[0].wait()
    loads[1].wait()
    hrow[...] = jnp.concatenate([u0[:, 0, 0, :], u0[:, 1, 0, :]], axis=1)
    hcorner[...] = u0[:, 0, 0, :]
    lane = iota((n0, 128), 1)
    packed = jnp.zeros((n0, 128), jnp.float32)
    for d in range(DEPTH):
        packed = jnp.where(lane == d, u0[d, 0, :, 0:1], packed)
        packed = jnp.where(lane == 4 + d, u0[d, 1, :, 126:127], packed)
    packed = packed.T
    hcol[...] = packed[0:4]
    def send_all(peers, axis, me, count, src, dst, send, recv):
        for k, peer in peers:
            before = (me + count - 1 - peer[axis]) // count
            way = before + before * (1 - (me + count - 2 - peer[axis]) // count)
            pltpu.make_async_remote_copy(
                src_ref=src.at[way], dst_ref=dst.at[k - 1], send_sem=send, recv_sem=recv,
                device_id=peer, device_id_type=MESH,
            ).start()

    def send_same(peers, src, dst, send, recv):
        for k, peer in peers:
            pltpu.make_async_remote_copy(
                src_ref=src, dst_ref=dst.at[k], send_sem=send, recv_sem=recv, device_id=peer, device_id_type=MESH
            ).start()

    def gather(buf, ref, places, count):
        at, _, _ = places["weight"]
        tiles = buf.shape[2] // 128
        sums = [jnp.zeros(buf.shape[1:], jnp.float32)] * 2
        for k in range(1, count):
            for way in range(2):
                weight = ref[at + way * count + k : at + way * count + k + 1, :]
                sums[way] = sums[way] + jnp.concatenate([weight] * tiles, axis=1) * buf[k - 1]
        return sums

    def selection(n, last):
        shape = (padded_lanes(n), padded_lanes(n // 2))
        row, lane = iota(shape, 0), iota(shape, 1)
        tail = jnp.where(last, n - 4, n)
        hit = ((lane < n // 2) & (row == 2 * lane)) | ((lane == n // 2) & (row == tail))
        return jnp.where(hit, 1.0, 0.0)

    def local_level(level, n, u, w):
        h = n // 2
        rows, rows_c, lanes_c = padded_rows(n), padded_rows(h), padded_lanes(h)
        col_mat, row_mat = col_table(f"mat{level}"), row_table(f"mat{level}")[:, 0:rows]
        select = selection(n, last_y)
        base, solved = [], []
        is_tail = iota((rows_c, lanes_c), 0) == h
        for d in range(DEPTH):
            z = dot(row_mat, dot(w[d], col_mat))
            even = even_rows(tall_v, pick_dot(u[d], select), rows_c)
            even = jnp.where(is_tail & last_x, even[h - 2 : h - 1, :], even)
            base.append(jnp.where(iota((rows_c, lanes_c), 1) <= h, z, 0.0) + even)
            solved.append(z)
        return base, solved

    def row_sums(values, weights, count=2):
        sums = []
        for way in range(count):
            for d in range(DEPTH):
                rows = values[d].shape[0]
                sums.append(jnp.sum(values[d] * weights[0:rows, way : way + 1], axis=0, keepdims=True))
        return jnp.concatenate(sums, axis=0)

    def line(value, functional):
        return jnp.sum(value * functional, axis=1, keepdims=True)

    def twice(table, row, lanes):
        return jnp.concatenate(
            [jnp.broadcast_to(table[row + way : row + way + 1, 0:lanes], (4, lanes)) for way in range(2)], axis=0
        )

    def outer(column, table, row, lanes):
        return (
            column[0:4] * table[row : row + 1, 0:lanes] + column[4:8] * table[row + 1 : row + 2, 0:lanes]
        )

    def spread_out(values, count, lanes, stride, pieces):
        mat = spread_matrix(count, lanes, stride, n0)
        for d in range(DEPTH):
            add_rows(out_v, d, pick_dot(values[d][0:count], mat, pieces), stride)

    n, h = n0, n0 // 2
    wide, rows_c, lanes_c = padded_lanes(n), padded_rows(h), padded_lanes(h)
    for copy in loads[2:]:
        copy.wait()
    rv, cv = row_table("vecs"), col_table("vecs")
    col_q = cv[0:2, 0:n]
    own_cols = jnp.zeros((n, 128), jnp.float32)
    for d in range(DEPTH):
        value = detail(jnp.concatenate([u0[d, 0], u0[d, 1]], axis=1), True)
        w0[d] = value
        for way in range(2):
            own_cols = jnp.where(lane == 4 * way + d, line(value, col_q[way : way + 1]), own_cols)
    own_rows = row_sums([w0[d] for d in range(DEPTH)], rv[24:32, 0:n].T[:, 2:4])
    own_cols = own_cols.T[0:8]
    none = jnp.zeros((8, 128), jnp.float32)
    own_rows = jnp.concatenate([own_rows, none], axis=1)
    own_cols = jnp.concatenate([own_cols, none], axis=1)
    at = iota((4, wide), 1)
    own_254 = jnp.concatenate([u0[:, 0, n - 2, :], u0[:, 1, n - 2, :]], axis=1)
    alias = packed[4:8, n - 2 : n - 1]
    wider = lambda value, end: jnp.where(at == n, end, jnp.concatenate([value, none[0:4]], axis=1))

    def between(value):
        mean = 0.5 * (pltpu.roll(value, 1, 1) + pltpu.roll(value, wide - 1, 1))
        return jnp.where(at > n, 0.0, jnp.where(at % 2 == 1, mean, value))

    def edges(next_row, next_col, corner):
        corner = jnp.where(
            last_y, next_row[:, n - 2 : n - 1], jnp.where(last_x, next_col[:, n - 2 : n - 1], corner)
        )
        row_change, col_change = wider(next_row - own_254, 0.0), wider(next_col - packed[4:8], corner - alias)
        next_row, next_col = wider(next_row, alias), wider(next_col, corner)
        rows = -0.5 * between(row_change), next_row - between(next_row)
        cols = -0.5 * between(col_change), next_col - between(next_col)
        return rows + cols + (next_row, next_col)

    zero_row = jnp.where(last_x, own_254, 0.0)
    zero_col = jnp.where(last_y, packed[4:8], 0.0)
    end_row, _, end_col, _, _, _ = edges(zero_row, zero_col, 0.0)
    first_row, first_col = hrow[...], hcol[...]
    prior_row = -0.5 * between(wider(first_row, jnp.where(last_y, first_row[:, n - 2 : n - 1], 0.0)))
    prior_row = jnp.where(at == n, 0.0, prior_row)
    prior_col = -0.5 * between(wider(first_col, jnp.where(last_x, first_col[:, n - 2 : n - 1], 0.0)))
    prior_col = jnp.where(at == n, 0.0, prior_col)
    prior_row = jnp.where(at == n + 1, -0.25 * first_row[:, 0:1], prior_row)
    row_0 = jnp.concatenate([w0[:, 0, :], none[0:4]], axis=1)
    for way in range(2):
        q = rv[26 + way : 27 + way, 0:wide]
        q_own = jnp.where(iota((1, wide), 1) < n, q, 0.0)
        message = own_rows[4 * way : 4 * way + 4] + q[:, n - 1 : n] * end_row
        message += jnp.where(at == n - 1, line(end_col, q_own), 0.0)
        message += jnp.where(at == n + 1, line(prior_col, q_own), 0.0)
        message = jnp.where(at == n, 0.0, message)
        xs0[way] = message + q[:, n + 1 : n + 2] * prior_row
        if way == 1:
            message -= q[:, 0:1] * row_0
            message -= jnp.where(at == n - 1, q[:, 0:1] * end_col[:, 0:1], 0.0)
            message -= jnp.where(at == n + 1, q[:, 0:1] * prior_col[:, 0:1], 0.0)
            xs0[2] = message
    pl.semaphore_wait(barrier, len(greeted))
    send_all(x_peers, 0, gx, gx_n, xs0, xr0, x_send.at[0], x_recv.at[0])
    halos = []
    for i, (src, dst, peer) in enumerate(
        ((hrow, hrow_in, (up, gy)), (hcol, hcol_in, (gx, left)), (hcorner, hcorner_in, (up, left)))
    ):
        copy = pltpu.make_async_remote_copy(
            src_ref=src, dst_ref=dst, send_sem=halo_send.at[i], recv_sem=halo_recv.at[i],
            device_id=peer, device_id_type=MESH,
        )
        copy.start()
        halos.append(copy)
    for copy in halos:
        copy.wait_recv()
    row_255, row_256, col_255, col_256, next_row, next_col = edges(
        jnp.where(last_x, own_254, hrow_in[...]), jnp.where(last_y, packed[4:8], hcol_in[...]), hcorner_in[:, 0:1]
    )
    cols = []
    for way in range(2):
        q = cv[way : way + 1, 0:wide]
        cols.append(
            own_cols[4 * way : 4 * way + 4]
            + q[:, n - 1 : n] * col_255
            + q[:, n : n + 1] * col_256
            + jnp.where(at == n - 1, line(row_255, q), 0.0)
            + jnp.where(at == n, line(row_256, q), 0.0)
        )
    down_x = dot(jnp.concatenate(cols + [col_255, col_256], axis=0), row_table("mat0"), ((1,), (1,)))
    down_x = jnp.concatenate([down_x, jnp.zeros((16, lanes_c - rows_c), jnp.float32)], axis=1)
    select = selection(n, last_y)[0:n]
    next_even = pick_dot(next_row[:, 0:n], select)
    next_col_even = jnp.where(last_y, 0.0, pick_dot(next_col, selection(n, last_x)))
    evens = []
    for d in range(DEPTH):
        even = jnp.concatenate([u0[d, j, pl.ds(0, h, stride=2), :] for j in range(2)], axis=1)
        even = pick_dot(even, select)
        tail = jnp.where(last_x, even[h - 2 : h - 1], next_even[d : d + 1])
        tail = jnp.where(iota((8, lanes_c), 0) == 0, tail, 0.0)
        evens.append(jnp.concatenate([even, tail], axis=0))

    pltpu.make_async_copy(xr0, xr0, x_recv.at[0]).wait()
    a_right, a_left = gather(xr0, row_v, row_places, gx_n)
    a_right += rv[28:29, n + 1 : n + 2] * prior_row
    p_r, p_l = rv[2:3, 0:lanes_c], rv[3:4, 0:lanes_c]
    lane4 = iota((4, 128), 1)
    layer = iota((4, 128), 0)
    shared = jnp.zeros((4, 128), jnp.float32)
    for i, value in enumerate((a_right[:, n + 1 : n + 2], a_left[:, n + 1 : n + 2], a_right[:, 0:1], a_left[:, 0:1])):
        shared = jnp.where(lane4 == 4 * (i + 1) + layer, value, shared)
    q_right, q_left = cv[26:27, 0:wide], cv[27:28, 0:wide]
    q_near = jnp.where((iota((1, wide), 1) == 0) | (iota((1, wide), 1) == n + 1), 0.0, q_left)
    for i, q in enumerate((q_right, q_left, q_near)):
        way = (i + 1) // 2
        cols = down_x[4 * way : 4 * way + 4] + line(a_right, q) * p_r + line(a_left, q) * p_l
        ys0[i, 0:4] = cols[:, 0:h]
        ys0[i, 4:5] = jnp.sum(jnp.where(lane4 == layer, cols[:, h : h + 1], shared), axis=0, keepdims=True)
    send_all(y_peers, 1, gy, gy_n, ys0, yr0, y_send.at[0], y_recv.at[0])
    col_mat, row_mat = col_table("mat0"), row_table("mat0")
    is_node = iota((1, lanes_c), 1) <= h
    base = []
    for d in range(DEPTH):
        z = dot(row_mat[:, 0:n], dot(w0[d], col_mat[0:n]))
        base.append(jnp.where(is_node, z, 0.0) + evens[d])
    down_turned = jnp.concatenate([col_255, col_255], axis=0).T[0:n]
    is_last = iota((n, 128), 1) == 127
    for d in range(DEPTH):
        out_v[d, 0] = w0[d, :, 0:128]
        out_v[d, 1] = w0[d, :, 128:256] + jnp.where(is_last, down_turned[:, d : d + 1], 0.0)
        for j in range(2):
            tail = iota((8, 128), 0) == 7
            fix = row_255[d : d + 1, 128 * j : 128 * j + 128]
            out_v[d, j, n - 8 : n, :] = out_v[d, j, n - 8 : n, :] + jnp.where(tail, fix, 0.0)
    carried = dot(jnp.concatenate([a_right, a_left, row_255, row_256], axis=0), col_mat)
    four = lambda row: jnp.broadcast_to(row, (4, lanes_c))
    other = jnp.concatenate(
        [jnp.where(is_node, carried, 0.0), twice(cv, 2, lanes_c)]
        + [four(jnp.where(is_node, col_mat[n - 1 + i : n + i, :], 0.0)) for i in range(2)]
        + [four(jnp.where(iota((1, lanes_c), 1) == h, 1.0, 0.0)), jnp.zeros((4, lanes_c), jnp.float32)],
        axis=0,
    )
    own = jnp.concatenate([twice(rv, 2, lanes_c), twice(rv, 4, lanes_c)], axis=0)
    rest = jnp.concatenate([down_x[8:16], next_col_even, jnp.zeros((4, lanes_c), jnp.float32)], axis=0)
    pltpu.make_async_copy(yr0, yr0, y_recv.at[0]).wait()
    ends = []
    for value in gather(yr0, col_v, col_places, gy_n):
        tail = line(jnp.where(lane4 == layer, jnp.broadcast_to(value[4:5], (4, 128)), 0.0), 1.0)
        ends.append(jnp.concatenate([value[0:4], jnp.where(iota((4, 128), 1) == 0, tail, 0.0)], axis=1))
    c_right, c_left = ends
    c_right += cv[28:29, n + 1 : n + 2] * (a_right[:, n + 1 : n + 2] * p_r + a_left[:, n + 1 : n + 2] * p_l)
    inner = INNER.get(gy_n, 1)
    near = inner - 1 + (gy_n - inner) * ((gy % inner + 1) // inner)
    told = jnp.where(last_y, 0.0, jnp.broadcast_to(yr0[near - 1, 4:5, :], (4, 128)))
    told = [line(jnp.where(lane4 == 4 * (i + 1) + layer, told, 0.0), 1.0) for i in range(4)]
    ends_y = [jnp.where(is_node, col_mat[n - 1 + i : n + i, :], 0.0) for i in range(2)]
    late = jnp.concatenate([told[i] * ends_y[0] + told[2 + i] * ends_y[1] for i in range(2)], axis=0)
    other = other + jnp.concatenate([late, jnp.zeros((32, lanes_c), jnp.float32)], axis=0)
    lhs = jnp.concatenate([own, c_right, c_left, rest], axis=0).T[0:rows_c]
    for d in range(DEPTH):
        u1[d] = base[d] + dot(lhs, jnp.where(iota((40, lanes_c), 0) % 4 == d, other, 0.0))

    n, h, g = n0 // 2, n0 // 4, n0 // 8
    lane = iota((8, 128), 1)
    for d in range(DEPTH):
        w1[d] = detail(u1[d])
    ways = jnp.concatenate([rv[8:16, 0:256], row_table("taken")[:, 0:256]], axis=0).T
    functionals = jnp.concatenate([ways[:, 0:2], ways[:, 4:8]], axis=1)
    of_w = dot(row_sums([w1[d] for d in range(DEPTH)], functionals, 6), col_table("mat1"))
    taken = row_sums([u1[d] for d in range(DEPTH)], ways[:, 8:12], 4)
    of_next = of_w[8:24] + pick_dot(taken, selection(n, last_y))
    after = col_table("after")
    of_second = dot(jnp.concatenate([of_next[0:8], of_next[8:16]], axis=1), after[0:256])
    is_c = (lane == h + 1) | (lane == h + 2)
    sent = of_w[0:8] + pltpu.roll(of_second, h + 3, 1)
    for i in range(2):
        sent += pltpu.roll(jnp.where(is_c, of_w[8 + 8 * i : 16 + 8 * i], 0.0), g + 5 + 2 * i, 1)
    xs1[...] = sent
    xr1[0] = sent
    send_same(x_peers, xs1, xr1, x_send.at[1], x_recv.at[1])
    base1, solved1 = local_level(1, n, u1, w1)
    cols = jnp.zeros((padded_rows(h), 128), jnp.float32)
    spot = iota(cols.shape, 1)
    for d in range(DEPTH):
        for way in range(2):
            cols = jnp.where(spot == 4 * way + d, solved1[d][:, h + 1 + way : h + 2 + way], cols)
            cols = jnp.where(spot == 8 + 4 * way + d, line(base1[d], cv[16 + way : 17 + way, 0:128]), cols)
            cols = jnp.where(spot == 16 + 4 * way + d, line(base1[d], cv[12 + way : 13 + way, 0:128]), cols)
    cols = jnp.concatenate([cols, jnp.zeros((128 - padded_rows(h), 128), jnp.float32)], axis=0).T
    row_after = row_table("after")
    cols1, cols2 = cols[0:8], dot(jnp.concatenate([cols[8:16], cols[16:24]], axis=1), row_after[0:256])
    others = xr1.at[pl.ds(1, gx_n - 1)]
    pltpu.make_async_copy(others, others, x_recv.at[1]).wait()
    got = dot(row_table("join")[:, 0 : gx_n * 8], xr1[...].reshape(gx_n * 8, 128))
    a_1 = got[0:8]
    a_2 = pltpu.roll(got[24:32], 128 - (h + 3), 1) + dot(
        jnp.concatenate([got[8:16], got[16:24]], axis=1), after[0:256]
    )
    msg, msg2, hs = [], [], []
    for way in range(2):
        msg.append(cols1[4 * way : 4 * way + 4] + outer(a_1[:, h + 1 + way : h + 2 + way], rv, 10, 128))
        row = outer(line(a_1, cv[16 + way : 17 + way, 0:128]), rv, 20, 128)
        row += outer(line(a_1, cv[12 + way : 13 + way, 0:128]), rv, 22, 128)
        row += outer(a_2[:, g + 1 + way : g + 2 + way], rv, 18, 128)
        msg2.append(cols2[4 * way : 4 * way + 4] + row)
        block = jnp.zeros((4, 128), jnp.float32)
        for i in range(2):
            at = h + g + 6 + 2 * i + way
            h_col = got[24:32, at : at + 1] + got[8 + 8 * i : 16 + 8 * i, h + 1 + way : h + 2 + way]
            for x_way in range(2):
                block += jnp.where(iota((4, 128), 1) == h + 1 + 2 * i + x_way, h_col[4 * x_way : 4 * x_way + 4], 0.0)
        hs.append(block)
    sent = jnp.concatenate(msg, axis=0) + pltpu.roll(jnp.concatenate(msg2, axis=0), h + 5, 1)
    sent += jnp.concatenate(hs, axis=0)
    ys1[...] = sent
    yr1[0] = sent
    send_same(y_peers, ys1, yr1, y_send.at[1], y_recv.at[1])
    base2, _ = local_level(2, h, base1, [detail(base1[d]) for d in range(DEPTH)])
    spread_out([w1[d] for d in range(DEPTH)], n, 256, 2, 2)
    beside = lambda value: jnp.concatenate([value[128 * i : 128 * i + 128] for i in range(3)], axis=1)
    nodes_1 = lambda value: jnp.where(lane <= h, value, 0.0)
    nodes_2 = lambda value: jnp.where(lane <= g, value, 0.0)
    other1 = jnp.concatenate([nodes_1(a_1), twice(cv, 10, 128)], axis=0)
    across = dot(a_1, beside(after))
    other2 = jnp.concatenate(
        [nodes_2(across[:, 256:384]), nodes_2(across[:, 0:128]), nodes_2(across[:, 128:256]), nodes_2(a_2)]
        + [twice(cv, row, 128) for row in (24, 20, 22, 18)],
        axis=0,
    )
    own = jnp.concatenate([twice(rv, row, 128) for row in (24, 20, 22, 18)], axis=0)
    row_after = beside(row_after)
    others = yr1.at[pl.ds(1, gy_n - 1)]
    pltpu.make_async_copy(others, others, y_recv.at[1]).wait()
    got = dot(col_table("join"), yr1[...].reshape(gy_n * 8, 128))
    down = dot(got[0:24], row_after)
    c_2 = nodes_2(pltpu.roll(got[24:32], 128 - (h + 5), 1) + down[8:16, 0:128] + down[16:24, 128:256])
    lhs = jnp.concatenate([own, down[0:8, 256:384], down[0:8, 0:128], down[0:8, 128:256], c_2], axis=0)
    lhs = jnp.concatenate([lhs, jnp.zeros_like(lhs)], axis=0).T[0 : padded_rows(g), 0:64]
    lhs1 = jnp.concatenate([twice(rv, 10, 128), nodes_1(got[0:8])], axis=0).T[0 : padded_rows(h)]
    details, last = [], []
    for d in range(DEPTH):
        last.append(base2[d] + dot(lhs, jnp.where(iota((64, 128), 0) % 4 == d, other2, 0.0)))
        nodes = base1[d] + dot(lhs1, jnp.where(iota((16, 128), 0) % 4 == d, other1, 0.0))
        details.append(detail(nodes))
    spread_out(details, h, 128, 4, 2)
    spread_out(last, g, 128, 8, 3)
    for d in range(DEPTH):
        out[d] = jnp.concatenate([out_v[d, j] for j in range(n0 // 128)], axis=1)

    for i, copy in enumerate(halos):
        copy.wait_send()
    pltpu.make_async_copy(xr0, xr0, x_send.at[0]).wait()
    pltpu.make_async_copy(yr0, yr0, y_send.at[0]).wait()
    others = xr1.at[pl.ds(1, gx_n - 1)]
    pltpu.make_async_copy(others, others, x_send.at[1]).wait()
    others = yr1.at[pl.ds(1, gy_n - 1)]
    pltpu.make_async_copy(others, others, y_send.at[1]).wait()


def even_rows(tall_v, value, rows_c):
    rows, lanes = value.shape
    half = rows // 2
    parts = []
    for j in range(lanes // 128):
        tall_v[j, 0:rows] = value[:, 128 * j : 128 * j + 128]
        part = tall_v[j, pl.ds(0, half, stride=2), :]
        parts.append(jnp.concatenate([part, jnp.zeros((rows_c - half, 128), jnp.float32)], axis=0))
    return jnp.concatenate(parts, axis=1)


def add_rows(ref, d, value, stride):
    place = pl.ds(0, value.shape[0], stride=stride)
    for j in range(ref.shape[1]):
        ref[d, j, place, :] = ref[d, j, place, :] + value[:, 128 * j : 128 * j + 128]


def shards(salinity):
    gx_n, gy_n = lax.axis_size("gx"), lax.axis_size("gy")
    _, nx, ny = salinity.shape
    n0 = nx
    (row_tab, row_places), (col_tab, col_places) = tables(nx * gx_n, ny * gy_n, gx_n, gy_n)
    vmem = lambda *shape: pltpu.VMEM(shape, jnp.float32)
    dma = lambda count: pltpu.SemaphoreType.DMA((count,))
    wide = padded_lanes(n0)
    second = vmem(DEPTH, padded_rows(n0 // 2), padded_lanes(n0 // 2))
    scratch = [vmem(DEPTH, n0 // 128, n0, 128), vmem(DEPTH, 2, n0, 128), second, vmem(DEPTH, n0, n0), second, vmem(2, padded_rows(n0), 128)]
    scratch += [vmem(*row_tab.shape[1:]), vmem(*col_tab.shape[1:])]
    scratch += [vmem(DEPTH, n0), vmem(DEPTH, n0), vmem(DEPTH, 128)] * 2
    scratch += [vmem(3, DEPTH, wide), vmem(gx_n - 1, DEPTH, wide)]
    scratch += [vmem(3, DEPTH + 1, n0 // 2), vmem(gy_n - 1, DEPTH + 1, n0 // 2)]
    scratch += [vmem(8, 128), vmem(gx_n, 8, 128), vmem(8, 128), vmem(gy_n, 8, 128)]
    scratch += [dma(4), dma(3), dma(3), dma(2), dma(2), dma(2), dma(2)]
    anywhere = pl.BlockSpec(memory_space=pl.ANY)
    out = pl.pallas_call(
        functools.partial(kernel, gx_n, gy_n, n0, row_places, col_places),
        out_shape=jax.ShapeDtypeStruct(salinity.shape, jnp.float32),
        in_specs=[anywhere] * 3,
        out_specs=pl.BlockSpec(memory_space=pltpu.VMEM),
        scratch_shapes=scratch,
        compiler_params=pltpu.CompilerParams(
            collective_id=0, has_side_effects=True, vmem_limit_bytes=VMEM_LIMIT
        ),
    )(salinity, row_tab, col_tab)
    return out


def solution(mesh):
    placed = P(None, "gx", "gy")
    return jax.shard_map(shards, mesh=mesh, in_specs=(placed,), out_specs=placed, check_vma=False)
```

```python
import functools

import jax
import jax.numpy as jnp
import numpy as np
from jax import lax
from jax.experimental import pallas as pl
from jax.experimental.pallas import tpu as pltpu
from jax.sharding import PartitionSpec as P

LEVELS = 3
DEPTH = 4
LENGTH = 64.0
MESH = pl.DeviceIdType.MESH
TABLE_LANES = 384
BEFORE_HALO = 2
INNER = {8: 2, 32: 8}
VMEM_LIMIT = 52 * 1024 * 1024


def padded_rows(count):
    return count + 8


def padded_lanes(count):
    return (count // 128 + 1) * 128 if count >= 128 else 128


def partner(me, slot, tiles, sign):
    inner = INNER.get(tiles, 1)
    outer = tiles // inner
    far = (me // inner + outer + sign * (slot // inner)) % outer
    return far * inner + (me % inner + inner + sign * (slot % inner)) % inner


def farthest_first(tiles):
    inner = INNER.get(tiles, 1)
    outer = tiles // inner
    hops = lambda k: min(k // inner, outer - k // inner) + min(k % inner, inner - k % inner)
    return sorted(range(1, tiles), key=lambda k: -hops(k))


def solver_line(count):
    off = 1.0 / (3.0 * LENGTH) - LENGTH
    inner = 4.0 / (3.0 * LENGTH) + 2.0 * LENGTH
    end = 2.0 / (3.0 * LENGTH) + LENGTH
    diag = np.full(count, inner)
    diag[0] = diag[-1] = end
    q = np.ones(count)
    p = np.ones(count)
    q[1] = -diag[0] / off
    p[-2] = -diag[-1] / off
    for i in range(1, count - 1):
        q[i + 1] = -(diag[i] * q[i]) / off - q[i - 1]
        j = count - 1 - i
        p[j - 1] = -(diag[j] * p[j]) / off - p[j + 1]
    return q, p, diag[0] * p[0] + off * p[1]


def load_block(total, coarse_ids, fine_ids):
    out = np.zeros((len(coarse_ids), len(fine_ids)))

    def mass(i, j):
        if i < 0 or i >= total or j < 0 or j >= total:
            return 0.0
        if i == j:
            return (2.0 if i in (0, total - 1) else 4.0) / 6.0
        return 1.0 / 6.0 if abs(i - j) == 1 else 0.0

    for a, k in enumerate(coarse_ids):
        if k < 0 or k >= total // 2:
            continue
        upper = 1.0 if 2 * k + 1 == total - 1 else 0.5
        for b in range(max(0, 2 * k - 2 - fine_ids[0]), min(len(fine_ids), 2 * k + 3 - fine_ids[0])):
            j = fine_ids[b]
            out[a, b] = mass(2 * k, j) + 0.5 * mass(2 * k - 1, j) + upper * mass(2 * k + 1, j)
    return out


def line_tables(total, tiles):
    n = total // tiles
    h = n // 2
    coarse = total // 2
    q, p, w = solver_line(coarse)
    local, functional, carry, weight, select, wide = [], [], [], [], [], []
    for t in range(tiles):
        first = t * h
        last_tile = t == tiles - 1
        ids = np.arange(first, first + h + 1)
        if last_tile:
            ids[h] = ids[h - 2]
        window = np.arange(first - 1, first + h + 2)
        load = load_block(total, window, np.arange(t * n, t * n + n + 1))
        inside = (window >= 0) & (window < coarse)
        safe = np.clip(window, 0, coarse - 1)
        low = np.minimum(ids[:, None], safe[None, :])
        high = np.maximum(ids[:, None], safe[None, :])
        green = np.where(inside[None, :], q[low] * p[high] / w, 0.0)
        local.append(green @ load)
        q_end = q[min(first + h, coarse - 1)]
        to_right = (np.where(inside, q[safe] / q_end, 0.0)) @ load
        to_left = (np.where(inside, p[safe] / p[first], 0.0)) @ load
        before = load_block(total, window, np.array([t * n - 1]))
        own = [np.append(f[:n], np.where(inside, v, 0.0) @ before) for f, v in
               ((to_right, q[safe] / q_end), (to_left, p[safe] / p[first]))]
        wide.append(np.stack(own + [own[0] * q_end * p[first] / w]))
        to_right[n] = 0.0
        to_left[0] = 0.0
        functional.append(np.stack([to_right, to_left]))
        carry.append(np.stack([p[ids] / p[first], q[ids] / q_end]))
        weights = np.zeros((2, tiles))
        for k in range(1, tiles):
            s = partner(t, k, tiles, -1)
            if s < t:
                weights[0, k] = q[(s + 1) * h] * p[first] / w
            else:
                weights[1, k] = q_end * p[s * h] / w
        weight.append(weights)
        pick = np.zeros((n + 1, h + 1))
        pick[2 * np.arange(h), np.arange(h)] = 1.0
        pick[n - 4 if last_tile else n, h] = 1.0
        select.append(pick)
    return [np.stack(item) for item in (local, functional, carry, weight, select, wide)]


def fit(array, shape):
    out = np.zeros(array.shape[: array.ndim - len(shape)] + tuple(shape))
    out[tuple(slice(0, size) for size in array.shape)] = array
    return out


def interpolation(nodes):
    out = np.eye(nodes)
    for i in range(1, nodes, 2):
        out[i] = 0.0
        out[i, i - 1] = out[i, i + 1] = 0.5
    return out


def pair_weights(weight):
    tiles = weight.shape[0]
    out = np.zeros((tiles, tiles, 2, 2))
    for t in range(tiles):
        for k in range(1, tiles):
            for way in range(2):
                out[t, partner(t, k, tiles, -1), way, way] = weight[t, way, k]
    return out


def joined_weights(first, couplings, second):
    tiles = first.shape[0]
    blocks = [first]
    blocks += [np.einsum("tsab,sbc,sucd->tuad", second, k, first) for k in couplings]
    blocks.append(second)
    out = np.zeros((tiles, 4, 2, DEPTH, tiles, 2, DEPTH))
    for t in range(tiles):
        for slot in range(tiles):
            for d in range(DEPTH):
                for i, block in enumerate(blocks):
                    out[t, i, :, d, slot, :, d] = block[t, partner(t, slot, tiles, -1)]
    return out.reshape(tiles, 32, tiles * 8)


def packed(tables):
    places, blocks, at = {}, [], 0
    for name, table in tables.items():
        rows, lanes = -(-table.shape[1] // 8) * 8, -(-table.shape[2] // 128) * 128
        table = fit(table, (rows, lanes))
        places[name] = (at, rows, lanes // 128)
        at += rows * (lanes // 128)
        blocks += [table[:, :, 128 * j : 128 * j + 128] for j in range(lanes // 128)]
    return np.ascontiguousarray(np.concatenate(blocks, axis=1), np.float32), places


@functools.lru_cache(maxsize=None)
def tables(nx, ny, gx, gy):
    row_vecs = np.zeros((gx, 8 * LEVELS + 8, TABLE_LANES))
    col_vecs = np.zeros((gy, 8 * LEVELS + 8, TABLE_LANES))
    row_out, col_out, sides = {}, {}, []
    for vecs, size, tiles, out in ((row_vecs, nx, gx, row_out), (col_vecs, ny, gy, col_out)):
        lines = [line_tables(size >> level, tiles) for level in range(LEVELS)]
        sides.append(lines)
        for level, (local, functional, carry, weight, select, wide) in enumerate(lines):
            n = (size >> level) // tiles
            h = n // 2
            vecs[:, 8 * level : 8 * level + 2, : n + 1] = functional
            vecs[:, 8 * level + 2 : 8 * level + 4, : h + 1] = carry
            if level == 0:
                vecs[:, 26:29, :n] = wide[:, :, :n]
                vecs[:, 26:29, n + 1] = wide[:, :, n]
            if vecs is row_vecs:
                out[f"mat{level}"] = fit(local, (padded_rows(h), padded_lanes(n)))
                if level == 0:
                    vecs[:, 4, : h + 1] = local[:, :, n - 1]
                    vecs[:, 5, : h + 1] = local[:, :, n]
            else:
                joined = np.concatenate([local, functional], axis=1).transpose(0, 2, 1)
                out[f"mat{level}"] = fit(joined, (padded_lanes(n), padded_lanes(h)))
        out["weight"] = np.repeat(lines[0][3].reshape(tiles, 2 * tiles, 1), 128, axis=2)
    nodes = (nx // gx >> 2) + 1
    inter = interpolation(nodes)
    rest = np.eye(nodes) - inter
    (local_a, _, carry_a, weight_a, select_a, _), (local_b, func_b, carry_b, weight_b, select_b, _) = sides[0][1:]
    row_k = [np.einsum("tbi,ij,taj->tba", func_b, op, carry_a) for op in (rest, inter)]
    row_out["join"] = joined_weights(pair_weights(weight_a), row_k, pair_weights(weight_b))
    after = np.zeros((gx, 384, 128))
    half = carry_b.shape[2]
    taken = np.zeros((gx, 8, TABLE_LANES))
    for i, op in enumerate((rest, inter)):
        func = func_b @ op
        row_vecs[:, 12 + 2 * i : 14 + 2 * i, : local_a.shape[2]] = np.einsum("tij,tjk->tik", func, local_a)
        taken[:, 2 * i : 2 * i + 2, : select_a.shape[1]] = np.einsum("tij,tkj->tik", func, select_a)
        row_vecs[:, 20 + 2 * i : 22 + 2 * i, :half] = np.einsum("tij,taj->tai", local_b @ op, carry_a)
        after[:, 128 * i : 128 * i + nodes, :half] = (local_b @ op).transpose(0, 2, 1)
        after[:, 128 * i + nodes + 2 * i : 128 * i + nodes + 2 * i + 2, :half] = carry_b
    after[:, 256 : 256 + nodes, :half] = select_b
    row_vecs[:, 24:26, :half] = carry_a @ select_b
    fine = local_a.shape[2]
    inter_a = interpolation(fine)
    rest_a = np.eye(fine) - inter_a
    of_w = [sides[0][1][1], row_vecs[:, 12:14, :fine], row_vecs[:, 14:16, :fine]]
    late = [of_w[0] @ rest_a, of_w[0] @ inter_a]
    for i in range(2):
        late += [of_w[1 + i] @ rest_a, of_w[1 + i] @ inter_a, taken[:, 2 * i : 2 * i + 2, :fine]]
    late = np.stack(late, axis=1)
    late_own = np.einsum("tmxi,tpi->txpm", late, sides[0][0][2]).reshape(gx, 4, 8)
    late = late.reshape(gx, 16, fine).transpose(0, 2, 1)
    row_out.update(after=after, taken=taken, vecs=row_vecs, late=fit(late, (256, 128)), late_own=fit(late_own, (8, 128)))
    (_, _, carry_a, weight_a, _, _), (local_b, func_b, _, weight_b, select_b, _) = sides[1][1:]
    col_k = [np.einsum("tbi,ij,taj->tba", func_b, op, carry_a) for op in (np.eye(nodes), rest)]
    col_out["join"] = joined_weights(pair_weights(weight_a), col_k, pair_weights(weight_b))
    after = np.zeros((gy, 384, 128))
    col_vecs[:, 12:14, :nodes] = func_b @ rest
    both = np.concatenate([local_b, func_b], axis=1)
    for i, op in enumerate((np.eye(nodes), rest)):
        col_vecs[:, 20 + 2 * i : 22 + 2 * i, :half] = np.einsum("tij,taj->tai", local_b @ op, carry_a)
        after[:, 128 * i : 128 * i + nodes, : both.shape[1]] = (both @ op).transpose(0, 2, 1)
    after[:, 256 : 256 + nodes, :half] = select_b
    col_vecs[:, 24:26, :half] = carry_a @ select_b
    first = np.concatenate(sides[1][1][0:2], axis=1)
    select_a = sides[1][1][4]
    vectors = [sides[1][0][2][:, 0], sides[1][0][2][:, 1], sides[1][0][0][:, :, -2], sides[1][0][0][:, :, -1]]
    late = np.zeros((gy, 4, 8, 128))
    lanes = first.shape[1]
    for i, vector in enumerate(vectors):
        for t in range(gy):
            for k, op in enumerate((np.eye(fine), rest_a)):
                image = first[t] @ (op @ vector[t])
                late[t, i, k, :lanes] = image
                for m, second in enumerate((np.eye(nodes), rest)):
                    at = 2 + 3 * m + k
                    late[t, i, at, lanes : lanes + both.shape[1]] = both[t] @ (second @ image[:nodes])
                    start = lanes + both.shape[1] + 2 * m
                    late[t, i, at, start : start + 2] = image[nodes:lanes]
            for m, second in enumerate((np.eye(nodes), rest)):
                late[t, i, 4 + 3 * m, lanes : lanes + both.shape[1]] = both[t] @ (second @ (vector[t] @ select_a[t]))
    col_out.update(after=after, vecs=col_vecs, late=late.reshape(gy, 32, 128))
    return packed(row_out), packed(col_out)


def parts(value, count):
    out = []
    for _ in range(count):
        out.append(value.astype(jnp.bfloat16))
        value = value - out[-1].astype(jnp.float32)
    return out


def dot(a, b, dims=((1,), (0,))):
    return lax.dot_general(
        a, b, (dims, ((), ())), precision=lax.Precision.HIGHEST, preferred_element_type=jnp.float32
    )


def pick_dot(a, b, count=3, dims=((1,), (0,)), ones=1):
    total = None
    for part in reversed(parts(b if ones == 0 else a, count)):
        x, y = (a.astype(jnp.bfloat16), part) if ones == 0 else (part, b.astype(jnp.bfloat16))
        term = lax.dot_general(x, y, (dims, ((), ())), preferred_element_type=jnp.float32)
        total = term if total is None else total + term
    return total


def iota(shape, dim):
    return lax.broadcasted_iota(jnp.int32, shape, dim)


def detail(u, alone=False):
    rows, lanes = u.shape
    lane, row = iota(u.shape, 1), iota(u.shape, 0)
    left, right = pltpu.roll(u, 1, 1), pltpu.roll(u, lanes - 1, 1)
    if alone:
        right = jnp.where(lane == lanes - 1, left, right)
    along = jnp.where(lane % 2 == 1, 0.5 * (left + right), u)
    above, below = pltpu.roll(along, 1, 0), pltpu.roll(along, rows - 1, 0)
    if alone:
        below = jnp.where(row == rows - 1, above, below)
    return u - jnp.where(row % 2 == 1, 0.5 * (above + below), along)


def spread_matrix(count, lanes, stride, width):
    shape = (lanes, width)
    row = iota(shape, 0)
    return jnp.where((iota(shape, 1) == stride * row) & (row < count), 1.0, 0.0).astype(jnp.float32)


def kernel(gx_n, gy_n, n0, row_places, col_places, *refs):
    (sal, row_in, col_in, out, out_v, u0, u1, w0, w1, tall_v, row_v, col_v,
     hrow, hcol, hcorner, hrow_in, hcol_in, hcorner_in, xs0, xr0, ys0, yr0, xs1, xr1, ys1, yr1,
     load_sem, halo_send, halo_recv, x_send, x_recv, y_send, y_recv) = refs

    def table(ref, places, name):
        at, rows, tiles = places[name]
        return jnp.concatenate([ref[at + j * rows : at + (j + 1) * rows] for j in range(tiles)], axis=1)

    row_table = functools.partial(table, row_v, row_places)
    col_table = functools.partial(table, col_v, col_places)
    gx, gy = lax.axis_index("gx"), lax.axis_index("gy")
    last_x, last_y = gx == gx_n - 1, gy == gy_n - 1

    barrier = pltpu.get_barrier_semaphore()
    x_peers = [(k, (partner(gx, k, gx_n, 1), gy)) for k in farthest_first(gx_n)]
    y_peers = [(k, (gx, partner(gy, k, gy_n, 1))) for k in farthest_first(gy_n)]
    up, left = lax.rem(gx + gx_n - 1, gx_n), lax.rem(gy + gy_n - 1, gy_n)
    greeted = [peer for _, peer in y_peers + x_peers] + [(lax.rem(gx + 1, gx_n), lax.rem(gy + 1, gy_n))]
    for peer in greeted:
        pl.semaphore_signal(barrier, inc=1, device_id=peer, device_id_type=MESH)

    loads = [
        pltpu.make_async_copy(sal.at[:, :, pl.ds(128 * j, 128)], u0.at[:, j], load_sem.at[j]) for j in range(2)
    ]
    loads.append(pltpu.make_async_copy(row_in.at[gx], row_v, load_sem.at[2]))
    loads.append(pltpu.make_async_copy(col_in.at[gy], col_v, load_sem.at[3]))
    for copy in loads:
        copy.start()

    loads[0].wait()
    loads[1].wait()
    hrow[...] = jnp.concatenate([u0[:, 0, 0, :], u0[:, 1, 0, :]], axis=1)
    hcorner[...] = u0[:, 0, 0, :]
    lane = iota((n0, 128), 1)
    packed = jnp.zeros((n0, 128), jnp.float32)
    for d in range(DEPTH):
        packed = jnp.where(lane == d, u0[d, 0, :, 0:1], packed)
        packed = jnp.where(lane == 4 + d, u0[d, 1, :, 126:127], packed)
    packed = packed.T
    hcol[...] = packed[0:4]
    def send_all(peers, axis, me, count, src, dst, send, recv):
        for k, peer in peers:
            before = (me + count - 1 - peer[axis]) // count
            way = before + before * (1 - (me + count - 2 - peer[axis]) // count)
            pltpu.make_async_remote_copy(
                src_ref=src.at[way], dst_ref=dst.at[k - 1], send_sem=send, recv_sem=recv,
                device_id=peer, device_id_type=MESH,
            ).start()

    def send_same(peers, src, dst, send, recv):
        for k, peer in peers:
            pltpu.make_async_remote_copy(
                src_ref=src, dst_ref=dst.at[k], send_sem=send, recv_sem=recv, device_id=peer, device_id_type=MESH
            ).start()

    def gather(buf, ref, places, count):
        at, _, _ = places["weight"]
        tiles = buf.shape[2] // 128
        sums = [jnp.zeros(buf.shape[1:], jnp.float32)] * 2
        for k in range(1, count):
            for way in range(2):
                weight = ref[at + way * count + k : at + way * count + k + 1, :]
                sums[way] = sums[way] + jnp.concatenate([weight] * tiles, axis=1) * buf[k - 1]
        return sums

    def selection(n, last):
        shape = (padded_lanes(n), padded_lanes(n // 2))
        row, lane = iota(shape, 0), iota(shape, 1)
        tail = jnp.where(last, n - 4, n)
        hit = ((lane < n // 2) & (row == 2 * lane)) | ((lane == n // 2) & (row == tail))
        return jnp.where(hit, 1.0, 0.0)

    def local_level(level, n, u, w):
        h = n // 2
        rows, rows_c, lanes_c = padded_rows(n), padded_rows(h), padded_lanes(h)
        col_mat, row_mat = col_table(f"mat{level}"), row_table(f"mat{level}")[:, 0:rows]
        select = selection(n, last_y)
        base, solved = [], []
        is_tail = iota((rows_c, lanes_c), 0) == h
        for d in range(DEPTH):
            z = dot(row_mat, dot(w[d], col_mat))
            even = even_rows(tall_v, pick_dot(u[d], select), rows_c)
            even = jnp.where(is_tail & last_x, even[h - 2 : h - 1, :], even)
            base.append(jnp.where(iota((rows_c, lanes_c), 1) <= h, z, 0.0) + even)
            solved.append(z)
        return base, solved

    def row_sums(values, weights, count=2):
        sums = []
        for way in range(count):
            for d in range(DEPTH):
                rows = values[d].shape[0]
                sums.append(jnp.sum(values[d] * weights[0:rows, way : way + 1], axis=0, keepdims=True))
        return jnp.concatenate(sums, axis=0)

    def line(value, functional):
        return jnp.sum(value * functional, axis=1, keepdims=True)

    def twice(table, row, lanes):
        return jnp.concatenate(
            [jnp.broadcast_to(table[row + way : row + way + 1, 0:lanes], (4, lanes)) for way in range(2)], axis=0
        )

    def outer(column, table, row, lanes):
        return (
            column[0:4] * table[row : row + 1, 0:lanes] + column[4:8] * table[row + 1 : row + 2, 0:lanes]
        )

    def spread_out(values, count, lanes, stride, pieces):
        mat = spread_matrix(count, lanes, stride, n0)
        for d in range(DEPTH):
            add_rows(out_v, d, pick_dot(values[d][0:count], mat, pieces), stride)

    n, h = n0, n0 // 2
    wide, rows_c, lanes_c = padded_lanes(n), padded_rows(h), padded_lanes(h)
    for copy in loads[2:]:
        copy.wait()
    rv, cv = row_table("vecs"), col_table("vecs")
    col_q = cv[0:2, 0:n]
    own_cols = jnp.zeros((n, 128), jnp.float32)
    for d in range(DEPTH):
        value = detail(jnp.concatenate([u0[d, 0], u0[d, 1]], axis=1), True)
        w0[d] = value
        for way in range(2):
            own_cols = jnp.where(lane == 4 * way + d, line(value, col_q[way : way + 1]), own_cols)
    own_rows = row_sums([w0[d] for d in range(DEPTH)], rv[24:32, 0:n].T[:, 2:4])
    own_cols = own_cols.T[0:8]
    none = jnp.zeros((8, 128), jnp.float32)
    own_rows = jnp.concatenate([own_rows, none], axis=1)
    own_cols = jnp.concatenate([own_cols, none], axis=1)
    at = iota((4, wide), 1)
    own_254 = jnp.concatenate([u0[:, 0, n - 2, :], u0[:, 1, n - 2, :]], axis=1)
    alias = packed[4:8, n - 2 : n - 1]
    wider = lambda value, end: jnp.where(at == n, end, jnp.concatenate([value, none[0:4]], axis=1))

    def between(value):
        mean = 0.5 * (pltpu.roll(value, 1, 1) + pltpu.roll(value, wide - 1, 1))
        return jnp.where(at > n, 0.0, jnp.where(at % 2 == 1, mean, value))

    def edges(next_row, next_col, corner):
        corner = jnp.where(
            last_y, next_row[:, n - 2 : n - 1], jnp.where(last_x, next_col[:, n - 2 : n - 1], corner)
        )
        row_change, col_change = wider(next_row - own_254, 0.0), wider(next_col - packed[4:8], corner - alias)
        next_row, next_col = wider(next_row, alias), wider(next_col, corner)
        rows = -0.5 * between(row_change), next_row - between(next_row)
        cols = -0.5 * between(col_change), next_col - between(next_col)
        return rows + cols + (next_row, next_col)

    zero_row = jnp.where(last_x, own_254, 0.0)
    zero_col = jnp.where(last_y, packed[4:8], 0.0)
    end_row, _, end_col, _, _, _ = edges(zero_row, zero_col, 0.0)
    first_row, first_col = hrow[...], hcol[...]
    prior_row = -0.5 * between(wider(first_row, jnp.where(last_y, first_row[:, n - 2 : n - 1], 0.0)))
    prior_row = jnp.where(at == n, 0.0, prior_row)
    prior_col = -0.5 * between(wider(first_col, jnp.where(last_x, first_col[:, n - 2 : n - 1], 0.0)))
    prior_col = jnp.where(at == n, 0.0, prior_col)
    prior_row = jnp.where(at == n + 1, -0.25 * first_row[:, 0:1], prior_row)
    row_0 = jnp.concatenate([w0[:, 0, :], none[0:4]], axis=1)
    for way in range(2):
        q = rv[26 + way : 27 + way, 0:wide]
        q_own = jnp.where(iota((1, wide), 1) < n, q, 0.0)
        message = own_rows[4 * way : 4 * way + 4] + q[:, n - 1 : n] * end_row
        message += jnp.where(at == n - 1, line(end_col, q_own), 0.0)
        message += jnp.where(at == n + 1, line(prior_col, q_own), 0.0)
        message = jnp.where(at == n, 0.0, message)
        xs0[way] = message + q[:, n + 1 : n + 2] * prior_row
        if way == 1:
            message -= q[:, 0:1] * row_0
            message -= jnp.where(at == n - 1, q[:, 0:1] * end_col[:, 0:1], 0.0)
            message -= jnp.where(at == n + 1, q[:, 0:1] * prior_col[:, 0:1], 0.0)
            xs0[2] = message
    pl.semaphore_wait(barrier, len(greeted))
    send_all(x_peers, 0, gx, gx_n, xs0, xr0, x_send.at[0], x_recv.at[0])
    halos = []
    for i, (src, dst, peer) in enumerate(
        ((hrow, hrow_in, (up, gy)), (hcol, hcol_in, (gx, left)), (hcorner, hcorner_in, (up, left)))
    ):
        copy = pltpu.make_async_remote_copy(
            src_ref=src, dst_ref=dst, send_sem=halo_send.at[i], recv_sem=halo_recv.at[i],
            device_id=peer, device_id_type=MESH,
        )
        copy.start()
        halos.append(copy)
    col_mat, row_mat = col_table("mat0"), row_table("mat0")
    is_node = iota((1, lanes_c), 1) <= h

    def dense(layers):
        half = jnp.concatenate([dot(row_mat[:, 0:n0], w0[d]) for d in layers], axis=0)
        value = jnp.where(is_node, dot(half, col_mat[0:n0]), 0.0)
        return [value[i * rows_c : (i + 1) * rows_c] for i in range(len(layers))]

    base = dense(range(BEFORE_HALO))
    for copy in halos:
        copy.wait_recv()
    row_255, row_256, col_255, col_256, next_row, next_col = edges(
        jnp.where(last_x, own_254, hrow_in[...]), jnp.where(last_y, packed[4:8], hcol_in[...]), hcorner_in[:, 0:1]
    )
    cols = []
    for way in range(2):
        q = cv[way : way + 1, 0:wide]
        cols.append(
            own_cols[4 * way : 4 * way + 4]
            + q[:, n - 1 : n] * col_255
            + q[:, n : n + 1] * col_256
            + jnp.where(at == n - 1, line(row_255, q), 0.0)
            + jnp.where(at == n, line(row_256, q), 0.0)
        )
    down_x = dot(jnp.concatenate(cols + [col_255, col_256], axis=0), row_table("mat0"), ((1,), (1,)))
    down_x = jnp.concatenate([down_x, jnp.zeros((16, lanes_c - rows_c), jnp.float32)], axis=1)
    select = selection(n, last_y)[0:n]
    next_even = pick_dot(next_row[:, 0:n], select)
    next_col_even = jnp.where(last_y, 0.0, pick_dot(next_col, selection(n, last_x)))
    evens = []
    for d in range(DEPTH):
        even = jnp.concatenate([u0[d, j, pl.ds(0, h, stride=2), :] for j in range(2)], axis=1)
        even = pick_dot(even, select)
        tail = jnp.where(last_x, even[h - 2 : h - 1], next_even[d : d + 1])
        tail = jnp.where(iota((8, lanes_c), 0) == 0, tail, 0.0)
        evens.append(jnp.concatenate([even, tail], axis=0))

    pltpu.make_async_copy(xr0, xr0, x_recv.at[0]).wait()
    a_right, a_left = gather(xr0, row_v, row_places, gx_n)
    a_right += rv[28:29, n + 1 : n + 2] * prior_row
    p_r, p_l = rv[2:3, 0:lanes_c], rv[3:4, 0:lanes_c]
    lane4 = iota((4, 128), 1)
    layer = iota((4, 128), 0)
    shared = jnp.zeros((4, 128), jnp.float32)
    for i, value in enumerate((a_right[:, n + 1 : n + 2], a_left[:, n + 1 : n + 2], a_right[:, 0:1], a_left[:, 0:1])):
        shared = jnp.where(lane4 == 4 * (i + 1) + layer, value, shared)
    q_right, q_left = cv[26:27, 0:wide], cv[27:28, 0:wide]
    q_near = jnp.where((iota((1, wide), 1) == 0) | (iota((1, wide), 1) == n + 1), 0.0, q_left)
    for i, q in enumerate((q_right, q_left, q_near)):
        way = (i + 1) // 2
        cols = down_x[4 * way : 4 * way + 4] + line(a_right, q) * p_r + line(a_left, q) * p_l
        ys0[i, 0:4] = cols[:, 0:h]
        ys0[i, 4:5] = jnp.sum(jnp.where(lane4 == layer, cols[:, h : h + 1], shared), axis=0, keepdims=True)
    send_all(y_peers, 1, gy, gy_n, ys0, yr0, y_send.at[0], y_recv.at[0])
    base += dense(range(BEFORE_HALO, DEPTH))
    base = [base[d] + evens[d] for d in range(DEPTH)]
    carried = dot(jnp.concatenate([a_right, a_left, row_255, row_256], axis=0), col_mat)
    four = lambda row: jnp.broadcast_to(row, (4, lanes_c))
    other = jnp.concatenate(
        [jnp.where(is_node, carried, 0.0), twice(cv, 2, lanes_c)]
        + [four(jnp.where(is_node, col_mat[n - 1 + i : n + i, :], 0.0)) for i in range(2)]
        + [four(jnp.where(iota((1, lanes_c), 1) == h, 1.0, 0.0)), jnp.zeros((4, lanes_c), jnp.float32)],
        axis=0,
    )
    own = jnp.concatenate([twice(rv, 2, lanes_c), twice(rv, 4, lanes_c)], axis=0)
    rest = jnp.concatenate([down_x[8:16], next_col_even, jnp.zeros((4, lanes_c), jnp.float32)], axis=0)
    lhs = jnp.concatenate([own, jnp.zeros((8, lanes_c), jnp.float32), rest], axis=0).T[0:rows_c]
    for d in range(DEPTH):
        u1[d] = base[d] + dot(lhs, jnp.where(iota((40, lanes_c), 0) % 4 == d, other, 0.0))
        w1[d] = detail(u1[d])

    n, h, g = n0 // 2, n0 // 4, n0 // 8
    lane = iota((8, 128), 1)
    ways = jnp.concatenate([rv[8:16, 0:256], row_table("taken")[:, 0:256]], axis=0).T
    functionals = jnp.concatenate([ways[:, 0:2], ways[:, 4:8]], axis=1)
    of_w = dot(row_sums([w1[d] for d in range(DEPTH)], functionals, 6), col_table("mat1"))
    taken = row_sums([u1[d] for d in range(DEPTH)], ways[:, 8:12], 4)
    of_next = of_w[8:24] + pick_dot(taken, selection(n, last_y))
    after = col_table("after")
    of_second = dot(jnp.concatenate([of_next[0:8], of_next[8:16]], axis=1), after[0:256])
    is_c = (lane == h + 1) | (lane == h + 2)
    sent = of_w[0:8] + pltpu.roll(of_second, h + 3, 1)
    for i in range(2):
        sent += pltpu.roll(jnp.where(is_c, of_w[8 + 8 * i : 16 + 8 * i], 0.0), g + 5 + 2 * i, 1)
    late_rows, late_own = col_table("late"), row_table("late_own")
    late_ends = [dot(late_own[:, 0:8], late_rows[16 + 8 * i : 24 + 8 * i]) for i in range(2)]
    late_table = row_table("late")

    pltpu.make_async_copy(yr0, yr0, y_recv.at[0]).wait()
    ends = []
    for value in gather(yr0, col_v, col_places, gy_n):
        tail = line(jnp.where(lane4 == layer, jnp.broadcast_to(value[4:5], (4, 128)), 0.0), 1.0)
        ends.append(jnp.concatenate([value[0:4], jnp.where(lane4 == 0, tail, 0.0)], axis=1))
    c_right, c_left = ends
    c_right += cv[28:29, n0 + 1 : n0 + 2] * (a_right[:, n0 + 1 : n0 + 2] * p_r + a_left[:, n0 + 1 : n0 + 2] * p_l)
    inner = INNER.get(gy_n, 1)
    near = inner - 1 + (gy_n - inner) * ((gy % inner + 1) // inner)
    told = jnp.where(last_y, 0.0, jnp.broadcast_to(yr0[near - 1, 4:5, :], (4, 128)))
    told = [line(jnp.where(lane4 == 4 * (i + 1) + layer, told, 0.0), 1.0) for i in range(4)]
    carries = jnp.concatenate([c_right, c_left], axis=0)
    scalars = dot(carries, late_table)
    change = []
    for x_way in range(2):
        part = jnp.zeros((4, 128), jnp.float32)
        for m in range(8):
            for way in range(2):
                scalar = scalars[4 * way : 4 * way + 4, 2 * m + x_way : 2 * m + x_way + 1]
                part += scalar * late_rows[8 * way + m : 8 * way + m + 1]
        for i in range(4):
            row = 2 * x_way + i % 2
            part += told[i] * late_ends[i // 2][row : row + 1]
        change.append(part)
    sent = sent + jnp.concatenate(change, axis=0)
    xs1[...] = sent
    xr1[0] = sent
    send_same(x_peers, xs1, xr1, x_send.at[1], x_recv.at[1])
    ends_y = [jnp.where(is_node, col_mat[n0 - 1 + i : n0 + i, :], 0.0) for i in range(2)]
    late = jnp.concatenate([told[i] * ends_y[0] + told[2 + i] * ends_y[1] for i in range(2)], axis=0)
    lhs = jnp.concatenate([carries, twice(rv, 2, lanes_c)], axis=0).T[0:rows_c]
    other = jnp.concatenate([twice(cv, 2, lanes_c), late], axis=0)
    for d in range(DEPTH):
        u1[d] = u1[d] + dot(lhs, jnp.where(iota((16, lanes_c), 0) % 4 == d, other, 0.0))
        w1[d] = detail(u1[d])
    base1, solved1 = local_level(1, n, u1, w1)
    cols = jnp.zeros((padded_rows(h), 128), jnp.float32)
    spot = iota(cols.shape, 1)
    for d in range(DEPTH):
        for way in range(2):
            cols = jnp.where(spot == 4 * way + d, solved1[d][:, h + 1 + way : h + 2 + way], cols)
            cols = jnp.where(spot == 8 + 4 * way + d, line(base1[d], cv[16 + way : 17 + way, 0:128]), cols)
            cols = jnp.where(spot == 16 + 4 * way + d, line(base1[d], cv[12 + way : 13 + way, 0:128]), cols)
    cols = jnp.concatenate([cols, jnp.zeros((128 - padded_rows(h), 128), jnp.float32)], axis=0).T
    row_after = row_table("after")
    cols1, cols2 = cols[0:8], dot(jnp.concatenate([cols[8:16], cols[16:24]], axis=1), row_after[0:256])
    others = xr1.at[pl.ds(1, gx_n - 1)]
    pltpu.make_async_copy(others, others, x_recv.at[1]).wait()
    got = dot(row_table("join")[:, 0 : gx_n * 8], xr1[...].reshape(gx_n * 8, 128))
    a_1 = got[0:8]
    a_2 = pltpu.roll(got[24:32], 128 - (h + 3), 1) + dot(
        jnp.concatenate([got[8:16], got[16:24]], axis=1), after[0:256]
    )
    msg, msg2, hs = [], [], []
    for way in range(2):
        msg.append(cols1[4 * way : 4 * way + 4] + outer(a_1[:, h + 1 + way : h + 2 + way], rv, 10, 128))
        row = outer(line(a_1, cv[16 + way : 17 + way, 0:128]), rv, 20, 128)
        row += outer(line(a_1, cv[12 + way : 13 + way, 0:128]), rv, 22, 128)
        row += outer(a_2[:, g + 1 + way : g + 2 + way], rv, 18, 128)
        msg2.append(cols2[4 * way : 4 * way + 4] + row)
        block = jnp.zeros((4, 128), jnp.float32)
        for i in range(2):
            at = h + g + 6 + 2 * i + way
            h_col = got[24:32, at : at + 1] + got[8 + 8 * i : 16 + 8 * i, h + 1 + way : h + 2 + way]
            for x_way in range(2):
                block += jnp.where(iota((4, 128), 1) == h + 1 + 2 * i + x_way, h_col[4 * x_way : 4 * x_way + 4], 0.0)
        hs.append(block)
    sent = jnp.concatenate(msg, axis=0) + pltpu.roll(jnp.concatenate(msg2, axis=0), h + 5, 1)
    sent += jnp.concatenate(hs, axis=0)
    ys1[...] = sent
    yr1[0] = sent
    send_same(y_peers, ys1, yr1, y_send.at[1], y_recv.at[1])
    down_turned = jnp.concatenate([col_255, col_255], axis=0).T[0:n0]
    is_last = iota((n0, 128), 1) == 127
    for d in range(DEPTH):
        out_v[d, 0] = w0[d, :, 0:128]
        out_v[d, 1] = w0[d, :, 128:256] + jnp.where(is_last, down_turned[:, d : d + 1], 0.0)
        for j in range(2):
            tail = iota((8, 128), 0) == 7
            fix = row_255[d : d + 1, 128 * j : 128 * j + 128]
            out_v[d, j, n0 - 8 : n0, :] = out_v[d, j, n0 - 8 : n0, :] + jnp.where(tail, fix, 0.0)
    base2, _ = local_level(2, h, base1, [detail(base1[d]) for d in range(DEPTH)])
    spread_out([w1[d] for d in range(DEPTH)], n, 256, 2, 2)
    beside = lambda value: jnp.concatenate([value[128 * i : 128 * i + 128] for i in range(3)], axis=1)
    nodes_1 = lambda value: jnp.where(lane <= h, value, 0.0)
    nodes_2 = lambda value: jnp.where(lane <= g, value, 0.0)
    other1 = jnp.concatenate([nodes_1(a_1), twice(cv, 10, 128)], axis=0)
    across = dot(a_1, beside(after))
    other2 = jnp.concatenate(
        [nodes_2(across[:, 256:384]), nodes_2(across[:, 0:128]), nodes_2(across[:, 128:256]), nodes_2(a_2)]
        + [twice(cv, row, 128) for row in (24, 20, 22, 18)],
        axis=0,
    )
    own = jnp.concatenate([twice(rv, row, 128) for row in (24, 20, 22, 18)], axis=0)
    row_after = beside(row_after)
    others = yr1.at[pl.ds(1, gy_n - 1)]
    pltpu.make_async_copy(others, others, y_recv.at[1]).wait()
    got = dot(col_table("join"), yr1[...].reshape(gy_n * 8, 128))
    down = dot(got[0:24], row_after)
    c_2 = nodes_2(pltpu.roll(got[24:32], 128 - (h + 5), 1) + down[8:16, 0:128] + down[16:24, 128:256])
    lhs = jnp.concatenate([own, down[0:8, 256:384], down[0:8, 0:128], down[0:8, 128:256], c_2], axis=0)
    lhs = jnp.concatenate([lhs, jnp.zeros_like(lhs)], axis=0).T[0 : padded_rows(g), 0:64]
    lhs1 = jnp.concatenate([twice(rv, 10, 128), nodes_1(got[0:8])], axis=0).T[0 : padded_rows(h)]
    details, last = [], []
    for d in range(DEPTH):
        last.append(base2[d] + dot(lhs, jnp.where(iota((64, 128), 0) % 4 == d, other2, 0.0)))
        nodes = base1[d] + dot(lhs1, jnp.where(iota((16, 128), 0) % 4 == d, other1, 0.0))
        details.append(detail(nodes))
    spread_out(details, h, 128, 4, 2)
    spread_out(last, g, 128, 8, 3)
    for d in range(DEPTH):
        out[d] = jnp.concatenate([out_v[d, j] for j in range(n0 // 128)], axis=1)

    for i, copy in enumerate(halos):
        copy.wait_send()
    pltpu.make_async_copy(xr0, xr0, x_send.at[0]).wait()
    pltpu.make_async_copy(yr0, yr0, y_send.at[0]).wait()
    others = xr1.at[pl.ds(1, gx_n - 1)]
    pltpu.make_async_copy(others, others, x_send.at[1]).wait()
    others = yr1.at[pl.ds(1, gy_n - 1)]
    pltpu.make_async_copy(others, others, y_send.at[1]).wait()


def even_rows(tall_v, value, rows_c):
    rows, lanes = value.shape
    half = rows // 2
    parts = []
    for j in range(lanes // 128):
        tall_v[j, 0:rows] = value[:, 128 * j : 128 * j + 128]
        part = tall_v[j, pl.ds(0, half, stride=2), :]
        parts.append(jnp.concatenate([part, jnp.zeros((rows_c - half, 128), jnp.float32)], axis=0))
    return jnp.concatenate(parts, axis=1)


def add_rows(ref, d, value, stride):
    place = pl.ds(0, value.shape[0], stride=stride)
    for j in range(ref.shape[1]):
        ref[d, j, place, :] = ref[d, j, place, :] + value[:, 128 * j : 128 * j + 128]


def shards(salinity):
    gx_n, gy_n = lax.axis_size("gx"), lax.axis_size("gy")
    _, nx, ny = salinity.shape
    n0 = nx
    (row_tab, row_places), (col_tab, col_places) = tables(nx * gx_n, ny * gy_n, gx_n, gy_n)
    vmem = lambda *shape: pltpu.VMEM(shape, jnp.float32)
    dma = lambda count: pltpu.SemaphoreType.DMA((count,))
    wide = padded_lanes(n0)
    second = vmem(DEPTH, padded_rows(n0 // 2), padded_lanes(n0 // 2))
    scratch = [vmem(DEPTH, n0 // 128, n0, 128), vmem(DEPTH, 2, n0, 128), second, vmem(DEPTH, n0, n0), second, vmem(2, padded_rows(n0), 128)]
    scratch += [vmem(*row_tab.shape[1:]), vmem(*col_tab.shape[1:])]
    scratch += [vmem(DEPTH, n0), vmem(DEPTH, n0), vmem(DEPTH, 128)] * 2
    scratch += [vmem(3, DEPTH, wide), vmem(gx_n - 1, DEPTH, wide)]
    scratch += [vmem(3, DEPTH + 1, n0 // 2), vmem(gy_n - 1, DEPTH + 1, n0 // 2)]
    scratch += [vmem(8, 128), vmem(gx_n, 8, 128), vmem(8, 128), vmem(gy_n, 8, 128)]
    scratch += [dma(4), dma(3), dma(3), dma(2), dma(2), dma(2), dma(2)]
    anywhere = pl.BlockSpec(memory_space=pl.ANY)
    out = pl.pallas_call(
        functools.partial(kernel, gx_n, gy_n, n0, row_places, col_places),
        out_shape=jax.ShapeDtypeStruct(salinity.shape, jnp.float32),
        in_specs=[anywhere] * 3,
        out_specs=pl.BlockSpec(memory_space=pltpu.VMEM),
        scratch_shapes=scratch,
        compiler_params=pltpu.CompilerParams(
            collective_id=0, has_side_effects=True, vmem_limit_bytes=VMEM_LIMIT
        ),
    )(salinity, row_tab, col_tab)
    return out


def solution(mesh):
    placed = P(None, "gx", "gy")
    return jax.shard_map(shards, mesh=mesh, in_specs=(placed,), out_specs=placed, check_vma=False)
```

```python
import functools

import jax
import jax.numpy as jnp
import numpy as np
from jax import lax
from jax.experimental import pallas as pl
from jax.experimental.pallas import tpu as pltpu
from jax.sharding import PartitionSpec as P

LEVELS = 3
DEPTH = 4
LENGTH = 64.0
MESH = pl.DeviceIdType.MESH
TABLE_LANES = 384
BEFORE_HALO = 3
INNER = {8: 2, 32: 8}
VMEM_LIMIT = 52 * 1024 * 1024


def padded_rows(count):
    return count + 8


def padded_lanes(count):
    return (count // 128 + 1) * 128 if count >= 128 else 128


def partner(me, slot, tiles, sign):
    inner = INNER.get(tiles, 1)
    outer = tiles // inner
    far = (me // inner + outer + sign * (slot // inner)) % outer
    return far * inner + (me % inner + inner + sign * (slot % inner)) % inner


def farthest_first(tiles):
    inner = INNER.get(tiles, 1)
    outer = tiles // inner
    hops = lambda k: min(k // inner, outer - k // inner) + min(k % inner, inner - k % inner)
    return sorted(range(1, tiles), key=lambda k: -hops(k))


def solver_line(count):
    off = 1.0 / (3.0 * LENGTH) - LENGTH
    inner = 4.0 / (3.0 * LENGTH) + 2.0 * LENGTH
    end = 2.0 / (3.0 * LENGTH) + LENGTH
    diag = np.full(count, inner)
    diag[0] = diag[-1] = end
    q = np.ones(count)
    p = np.ones(count)
    q[1] = -diag[0] / off
    p[-2] = -diag[-1] / off
    for i in range(1, count - 1):
        q[i + 1] = -(diag[i] * q[i]) / off - q[i - 1]
        j = count - 1 - i
        p[j - 1] = -(diag[j] * p[j]) / off - p[j + 1]
    return q, p, diag[0] * p[0] + off * p[1]


def load_block(total, coarse_ids, fine_ids):
    out = np.zeros((len(coarse_ids), len(fine_ids)))

    def mass(i, j):
        if i < 0 or i >= total or j < 0 or j >= total:
            return 0.0
        if i == j:
            return (2.0 if i in (0, total - 1) else 4.0) / 6.0
        return 1.0 / 6.0 if abs(i - j) == 1 else 0.0

    for a, k in enumerate(coarse_ids):
        if k < 0 or k >= total // 2:
            continue
        upper = 1.0 if 2 * k + 1 == total - 1 else 0.5
        for b in range(max(0, 2 * k - 2 - fine_ids[0]), min(len(fine_ids), 2 * k + 3 - fine_ids[0])):
            j = fine_ids[b]
            out[a, b] = mass(2 * k, j) + 0.5 * mass(2 * k - 1, j) + upper * mass(2 * k + 1, j)
    return out


def line_tables(total, tiles):
    n = total // tiles
    h = n // 2
    coarse = total // 2
    q, p, w = solver_line(coarse)
    local, functional, carry, weight, select, wide = [], [], [], [], [], []
    for t in range(tiles):
        first = t * h
        last_tile = t == tiles - 1
        ids = np.arange(first, first + h + 1)
        if last_tile:
            ids[h] = ids[h - 2]
        window = np.arange(first - 1, first + h + 2)
        load = load_block(total, window, np.arange(t * n, t * n + n + 1))
        inside = (window >= 0) & (window < coarse)
        safe = np.clip(window, 0, coarse - 1)
        low = np.minimum(ids[:, None], safe[None, :])
        high = np.maximum(ids[:, None], safe[None, :])
        green = np.where(inside[None, :], q[low] * p[high] / w, 0.0)
        local.append(green @ load)
        q_end = q[min(first + h, coarse - 1)]
        to_right = (np.where(inside, q[safe] / q_end, 0.0)) @ load
        to_left = (np.where(inside, p[safe] / p[first], 0.0)) @ load
        before = load_block(total, window, np.array([t * n - 1]))
        own = [np.append(f[:n], np.where(inside, v, 0.0) @ before) for f, v in
               ((to_right, q[safe] / q_end), (to_left, p[safe] / p[first]))]
        wide.append(np.stack(own + [own[0] * q_end * p[first] / w]))
        to_right[n] = 0.0
        to_left[0] = 0.0
        functional.append(np.stack([to_right, to_left]))
        carry.append(np.stack([p[ids] / p[first], q[ids] / q_end]))
        weights = np.zeros((2, tiles))
        for k in range(1, tiles):
            s = partner(t, k, tiles, -1)
            if s < t:
                weights[0, k] = q[(s + 1) * h] * p[first] / w
            else:
                weights[1, k] = q_end * p[s * h] / w
        weight.append(weights)
        pick = np.zeros((n + 1, h + 1))
        pick[2 * np.arange(h), np.arange(h)] = 1.0
        pick[n - 4 if last_tile else n, h] = 1.0
        select.append(pick)
    return [np.stack(item) for item in (local, functional, carry, weight, select, wide)]


def fit(array, shape):
    out = np.zeros(array.shape[: array.ndim - len(shape)] + tuple(shape))
    out[tuple(slice(0, size) for size in array.shape)] = array
    return out


def interpolation(nodes):
    out = np.eye(nodes)
    for i in range(1, nodes, 2):
        out[i] = 0.0
        out[i, i - 1] = out[i, i + 1] = 0.5
    return out


def pair_weights(weight):
    tiles = weight.shape[0]
    out = np.zeros((tiles, tiles, 2, 2))
    for t in range(tiles):
        for k in range(1, tiles):
            for way in range(2):
                out[t, partner(t, k, tiles, -1), way, way] = weight[t, way, k]
    return out


def joined_weights(first, couplings, second):
    tiles = first.shape[0]
    blocks = [first]
    blocks += [np.einsum("tsab,sbc,sucd->tuad", second, k, first) for k in couplings]
    blocks.append(second)
    out = np.zeros((tiles, 4, 2, DEPTH, tiles, 2, DEPTH))
    for t in range(tiles):
        for slot in range(tiles):
            for d in range(DEPTH):
                for i, block in enumerate(blocks):
                    out[t, i, :, d, slot, :, d] = block[t, partner(t, slot, tiles, -1)]
    return out.reshape(tiles, 32, tiles * 8)


def packed(tables):
    places, blocks, at = {}, [], 0
    for name, table in tables.items():
        rows, lanes = -(-table.shape[1] // 8) * 8, -(-table.shape[2] // 128) * 128
        table = fit(table, (rows, lanes))
        places[name] = (at, rows, lanes // 128)
        at += rows * (lanes // 128)
        blocks += [table[:, :, 128 * j : 128 * j + 128] for j in range(lanes // 128)]
    return np.ascontiguousarray(np.concatenate(blocks, axis=1), np.float32), places


@functools.lru_cache(maxsize=None)
def tables(nx, ny, gx, gy):
    row_vecs = np.zeros((gx, 8 * LEVELS + 8, TABLE_LANES))
    col_vecs = np.zeros((gy, 8 * LEVELS + 8, TABLE_LANES))
    row_out, col_out, sides = {}, {}, []
    for vecs, size, tiles, out in ((row_vecs, nx, gx, row_out), (col_vecs, ny, gy, col_out)):
        lines = [line_tables(size >> level, tiles) for level in range(LEVELS)]
        sides.append(lines)
        for level, (local, functional, carry, weight, select, wide) in enumerate(lines):
            n = (size >> level) // tiles
            h = n // 2
            vecs[:, 8 * level : 8 * level + 2, : n + 1] = functional
            vecs[:, 8 * level + 2 : 8 * level + 4, : h + 1] = carry
            if level == 0:
                vecs[:, 26:29, :n] = wide[:, :, :n]
                vecs[:, 26:29, n + 1] = wide[:, :, n]
            if vecs is row_vecs:
                out[f"mat{level}"] = fit(local, (padded_rows(h), padded_lanes(n)))
                if level == 0:
                    vecs[:, 4, : h + 1] = local[:, :, n - 1]
                    vecs[:, 5, : h + 1] = local[:, :, n]
            else:
                joined = np.concatenate([local, functional], axis=1).transpose(0, 2, 1)
                out[f"mat{level}"] = fit(joined, (padded_lanes(n), padded_lanes(h)))
        out["weight"] = np.repeat(lines[0][3].reshape(tiles, 2 * tiles, 1), 128, axis=2)
    nodes = (nx // gx >> 2) + 1
    inter = interpolation(nodes)
    rest = np.eye(nodes) - inter
    (local_a, _, carry_a, weight_a, select_a, _), (local_b, func_b, carry_b, weight_b, select_b, _) = sides[0][1:]
    row_k = [np.einsum("tbi,ij,taj->tba", func_b, op, carry_a) for op in (rest, inter)]
    row_out["join"] = joined_weights(pair_weights(weight_a), row_k, pair_weights(weight_b))
    after = np.zeros((gx, 384, 128))
    half = carry_b.shape[2]
    taken = np.zeros((gx, 8, TABLE_LANES))
    for i, op in enumerate((rest, inter)):
        func = func_b @ op
        row_vecs[:, 12 + 2 * i : 14 + 2 * i, : local_a.shape[2]] = np.einsum("tij,tjk->tik", func, local_a)
        taken[:, 2 * i : 2 * i + 2, : select_a.shape[1]] = np.einsum("tij,tkj->tik", func, select_a)
        row_vecs[:, 20 + 2 * i : 22 + 2 * i, :half] = np.einsum("tij,taj->tai", local_b @ op, carry_a)
        after[:, 128 * i : 128 * i + nodes, :half] = (local_b @ op).transpose(0, 2, 1)
        after[:, 128 * i + nodes + 2 * i : 128 * i + nodes + 2 * i + 2, :half] = carry_b
    after[:, 256 : 256 + nodes, :half] = select_b
    row_vecs[:, 24:26, :half] = carry_a @ select_b
    fine = local_a.shape[2]
    inter_a = interpolation(fine)
    rest_a = np.eye(fine) - inter_a
    of_w = [sides[0][1][1], row_vecs[:, 12:14, :fine], row_vecs[:, 14:16, :fine]]
    late = [of_w[0] @ rest_a, of_w[0] @ inter_a]
    for i in range(2):
        late += [of_w[1 + i] @ rest_a, of_w[1 + i] @ inter_a, taken[:, 2 * i : 2 * i + 2, :fine]]
    late = np.stack(late, axis=1)
    late_own = np.einsum("tmxi,tpi->txpm", late, sides[0][0][2]).reshape(gx, 4, 8)
    late = late.reshape(gx, 16, fine).transpose(0, 2, 1)
    row_out.update(after=after, taken=taken, vecs=row_vecs, late=fit(late, (256, 128)), late_own=fit(late_own, (8, 128)))
    (_, _, carry_a, weight_a, _, _), (local_b, func_b, _, weight_b, select_b, _) = sides[1][1:]
    col_k = [np.einsum("tbi,ij,taj->tba", func_b, op, carry_a) for op in (np.eye(nodes), rest)]
    col_out["join"] = joined_weights(pair_weights(weight_a), col_k, pair_weights(weight_b))
    after = np.zeros((gy, 384, 128))
    col_vecs[:, 12:14, :nodes] = func_b @ rest
    both = np.concatenate([local_b, func_b], axis=1)
    for i, op in enumerate((np.eye(nodes), rest)):
        col_vecs[:, 20 + 2 * i : 22 + 2 * i, :half] = np.einsum("tij,taj->tai", local_b @ op, carry_a)
        after[:, 128 * i : 128 * i + nodes, : both.shape[1]] = (both @ op).transpose(0, 2, 1)
    after[:, 256 : 256 + nodes, :half] = select_b
    col_vecs[:, 24:26, :half] = carry_a @ select_b
    first = np.concatenate(sides[1][1][0:2], axis=1)
    select_a = sides[1][1][4]
    vectors = [sides[1][0][2][:, 0], sides[1][0][2][:, 1], sides[1][0][0][:, :, -2], sides[1][0][0][:, :, -1]]
    late = np.zeros((gy, 4, 8, 128))
    lanes = first.shape[1]
    for i, vector in enumerate(vectors):
        for t in range(gy):
            for k, op in enumerate((np.eye(fine), rest_a)):
                image = first[t] @ (op @ vector[t])
                late[t, i, k, :lanes] = image
                for m, second in enumerate((np.eye(nodes), rest)):
                    at = 2 + 3 * m + k
                    late[t, i, at, lanes : lanes + both.shape[1]] = both[t] @ (second @ image[:nodes])
                    start = lanes + both.shape[1] + 2 * m
                    late[t, i, at, start : start + 2] = image[nodes:lanes]
            for m, second in enumerate((np.eye(nodes), rest)):
                late[t, i, 4 + 3 * m, lanes : lanes + both.shape[1]] = both[t] @ (second @ (vector[t] @ select_a[t]))
    col_out.update(after=after, vecs=col_vecs, late=late.reshape(gy, 32, 128))
    return packed(row_out), packed(col_out)


def parts(value, count):
    out = []
    for _ in range(count):
        out.append(value.astype(jnp.bfloat16))
        value = value - out[-1].astype(jnp.float32)
    return out


def dot(a, b, dims=((1,), (0,))):
    return lax.dot_general(
        a, b, (dims, ((), ())), precision=lax.Precision.HIGHEST, preferred_element_type=jnp.float32
    )


def pick_dot(a, b, count=3, dims=((1,), (0,)), ones=1):
    total = None
    for part in reversed(parts(b if ones == 0 else a, count)):
        x, y = (a.astype(jnp.bfloat16), part) if ones == 0 else (part, b.astype(jnp.bfloat16))
        term = lax.dot_general(x, y, (dims, ((), ())), preferred_element_type=jnp.float32)
        total = term if total is None else total + term
    return total


def iota(shape, dim):
    return lax.broadcasted_iota(jnp.int32, shape, dim)


def detail(u, alone=False):
    rows, lanes = u.shape
    lane, row = iota(u.shape, 1), iota(u.shape, 0)
    left, right = pltpu.roll(u, 1, 1), pltpu.roll(u, lanes - 1, 1)
    if alone:
        right = jnp.where(lane == lanes - 1, left, right)
    along = jnp.where(lane % 2 == 1, 0.5 * (left + right), u)
    above, below = pltpu.roll(along, 1, 0), pltpu.roll(along, rows - 1, 0)
    if alone:
        below = jnp.where(row == rows - 1, above, below)
    return u - jnp.where(row % 2 == 1, 0.5 * (above + below), along)


def spread_matrix(count, lanes, stride, width):
    shape = (lanes, width)
    row = iota(shape, 0)
    return jnp.where((iota(shape, 1) == stride * row) & (row < count), 1.0, 0.0).astype(jnp.float32)


def kernel(gx_n, gy_n, n0, row_places, col_places, *refs):
    (sal, row_in, col_in, out, out_v, u0, u1, w0, w1, tall_v, row_v, col_v,
     hrow, hcol, hcorner, hrow_in, hcol_in, hcorner_in, xs0, xr0, ys0, yr0, xs1, xr1, ys1, yr1,
     load_sem, halo_send, halo_recv, x_send, x_recv, y_send, y_recv) = refs

    def table(ref, places, name):
        at, rows, tiles = places[name]
        return jnp.concatenate([ref[at + j * rows : at + (j + 1) * rows] for j in range(tiles)], axis=1)

    row_table = functools.partial(table, row_v, row_places)
    col_table = functools.partial(table, col_v, col_places)
    gx, gy = lax.axis_index("gx"), lax.axis_index("gy")
    last_x, last_y = gx == gx_n - 1, gy == gy_n - 1

    barrier = pltpu.get_barrier_semaphore()
    x_peers = [(k, (partner(gx, k, gx_n, 1), gy)) for k in farthest_first(gx_n)]
    y_peers = [(k, (gx, partner(gy, k, gy_n, 1))) for k in farthest_first(gy_n)]
    up, left = lax.rem(gx + gx_n - 1, gx_n), lax.rem(gy + gy_n - 1, gy_n)
    greeted = [peer for _, peer in y_peers + x_peers] + [(lax.rem(gx + 1, gx_n), lax.rem(gy + 1, gy_n))]
    for peer in greeted:
        pl.semaphore_signal(barrier, inc=1, device_id=peer, device_id_type=MESH)

    loads = [
        pltpu.make_async_copy(sal.at[:, :, pl.ds(128 * j, 128)], u0.at[:, j], load_sem.at[j]) for j in range(2)
    ]
    loads.append(pltpu.make_async_copy(row_in.at[gx], row_v, load_sem.at[2]))
    loads.append(pltpu.make_async_copy(col_in.at[gy], col_v, load_sem.at[3]))
    for copy in loads:
        copy.start()

    loads[0].wait()
    loads[1].wait()
    hrow[...] = jnp.concatenate([u0[:, 0, 0, :], u0[:, 1, 0, :]], axis=1)
    hcorner[...] = u0[:, 0, 0, :]
    lane = iota((n0, 128), 1)
    packed = jnp.zeros((n0, 128), jnp.float32)
    for d in range(DEPTH):
        packed = jnp.where(lane == d, u0[d, 0, :, 0:1], packed)
        packed = jnp.where(lane == 4 + d, u0[d, 1, :, 126:127], packed)
    packed = packed.T
    hcol[...] = packed[0:4]
    def send_all(peers, axis, me, count, src, dst, send, recv):
        for k, peer in peers:
            before = (me + count - 1 - peer[axis]) // count
            way = before + before * (1 - (me + count - 2 - peer[axis]) // count)
            pltpu.make_async_remote_copy(
                src_ref=src.at[way], dst_ref=dst.at[k - 1], send_sem=send, recv_sem=recv,
                device_id=peer, device_id_type=MESH,
            ).start()

    def send_same(peers, src, dst, send, recv):
        for k, peer in peers:
            pltpu.make_async_remote_copy(
                src_ref=src, dst_ref=dst.at[k], send_sem=send, recv_sem=recv, device_id=peer, device_id_type=MESH
            ).start()

    def gather(buf, ref, places, count):
        at, _, _ = places["weight"]
        tiles = buf.shape[2] // 128
        sums = [jnp.zeros(buf.shape[1:], jnp.float32)] * 2
        for k in range(1, count):
            for way in range(2):
                weight = ref[at + way * count + k : at + way * count + k + 1, :]
                sums[way] = sums[way] + jnp.concatenate([weight] * tiles, axis=1) * buf[k - 1]
        return sums

    def selection(n, last):
        shape = (padded_lanes(n), padded_lanes(n // 2))
        row, lane = iota(shape, 0), iota(shape, 1)
        tail = jnp.where(last, n - 4, n)
        hit = ((lane < n // 2) & (row == 2 * lane)) | ((lane == n // 2) & (row == tail))
        return jnp.where(hit, 1.0, 0.0)

    def local_level(level, n, u, w):
        h = n // 2
        rows, rows_c, lanes_c = padded_rows(n), padded_rows(h), padded_lanes(h)
        col_mat, row_mat = col_table(f"mat{level}"), row_table(f"mat{level}")[:, 0:rows]
        select = selection(n, last_y)
        base, solved = [], []
        is_tail = iota((rows_c, lanes_c), 0) == h
        for d in range(DEPTH):
            z = dot(row_mat, dot(w[d], col_mat))
            even = pick_dot(even_rows(tall_v, u[d], rows_c), select)
            even = jnp.where(is_tail & last_x, even[h - 2 : h - 1, :], even)
            base.append(jnp.where(iota((rows_c, lanes_c), 1) <= h, z, 0.0) + even)
            solved.append(z)
        return base, solved

    def row_sums(values, weights, count=2):
        sums = []
        for way in range(count):
            for d in range(DEPTH):
                rows = values[d].shape[0]
                sums.append(jnp.sum(values[d] * weights[0:rows, way : way + 1], axis=0, keepdims=True))
        return jnp.concatenate(sums, axis=0)

    def line(value, functional):
        return jnp.sum(value * functional, axis=1, keepdims=True)

    def twice(table, row, lanes):
        return jnp.concatenate(
            [jnp.broadcast_to(table[row + way : row + way + 1, 0:lanes], (4, lanes)) for way in range(2)], axis=0
        )

    def outer(column, table, row, lanes):
        return (
            column[0:4] * table[row : row + 1, 0:lanes] + column[4:8] * table[row + 1 : row + 2, 0:lanes]
        )

    def spread_out(values, count, lanes, stride, pieces):
        mat = spread_matrix(count, lanes, stride, n0)
        for d in range(DEPTH):
            add_rows(out_v, d, pick_dot(values[d][0:count], mat, pieces), stride)

    n, h = n0, n0 // 2
    wide, rows_c, lanes_c = padded_lanes(n), padded_rows(h), padded_lanes(h)
    for copy in loads[2:]:
        copy.wait()
    rv, cv = row_table("vecs"), col_table("vecs")
    col_q = cv[0:2, 0:n]
    own_cols = jnp.zeros((n, 128), jnp.float32)
    for d in range(DEPTH):
        value = detail(jnp.concatenate([u0[d, 0], u0[d, 1]], axis=1), True)
        w0[d] = value
        for way in range(2):
            own_cols = jnp.where(lane == 4 * way + d, line(value, col_q[way : way + 1]), own_cols)
    own_rows = row_sums([w0[d] for d in range(DEPTH)], rv[24:32, 0:n].T[:, 2:4])
    own_cols = own_cols.T[0:8]
    none = jnp.zeros((8, 128), jnp.float32)
    own_rows = jnp.concatenate([own_rows, none], axis=1)
    own_cols = jnp.concatenate([own_cols, none], axis=1)
    at = iota((4, wide), 1)
    own_254 = jnp.concatenate([u0[:, 0, n - 2, :], u0[:, 1, n - 2, :]], axis=1)
    alias = packed[4:8, n - 2 : n - 1]
    wider = lambda value, end: jnp.where(at == n, end, jnp.concatenate([value, none[0:4]], axis=1))

    def between(value):
        mean = 0.5 * (pltpu.roll(value, 1, 1) + pltpu.roll(value, wide - 1, 1))
        return jnp.where(at > n, 0.0, jnp.where(at % 2 == 1, mean, value))

    def edges(next_row, next_col, corner):
        corner = jnp.where(
            last_y, next_row[:, n - 2 : n - 1], jnp.where(last_x, next_col[:, n - 2 : n - 1], corner)
        )
        row_change, col_change = wider(next_row - own_254, 0.0), wider(next_col - packed[4:8], corner - alias)
        next_row, next_col = wider(next_row, alias), wider(next_col, corner)
        rows = -0.5 * between(row_change), next_row - between(next_row)
        cols = -0.5 * between(col_change), next_col - between(next_col)
        return rows + cols + (next_row, next_col)

    zero_row = jnp.where(last_x, own_254, 0.0)
    zero_col = jnp.where(last_y, packed[4:8], 0.0)
    end_row, _, end_col, _, _, _ = edges(zero_row, zero_col, 0.0)
    first_row, first_col = hrow[...], hcol[...]
    prior_row = -0.5 * between(wider(first_row, jnp.where(last_y, first_row[:, n - 2 : n - 1], 0.0)))
    prior_row = jnp.where(at == n, 0.0, prior_row)
    prior_col = -0.5 * between(wider(first_col, jnp.where(last_x, first_col[:, n - 2 : n - 1], 0.0)))
    prior_col = jnp.where(at == n, 0.0, prior_col)
    prior_row = jnp.where(at == n + 1, -0.25 * first_row[:, 0:1], prior_row)
    row_0 = jnp.concatenate([w0[:, 0, :], none[0:4]], axis=1)
    for way in range(2):
        q = rv[26 + way : 27 + way, 0:wide]
        q_own = jnp.where(iota((1, wide), 1) < n, q, 0.0)
        message = own_rows[4 * way : 4 * way + 4] + q[:, n - 1 : n] * end_row
        message += jnp.where(at == n - 1, line(end_col, q_own), 0.0)
        message += jnp.where(at == n + 1, line(prior_col, q_own), 0.0)
        message = jnp.where(at == n, 0.0, message)
        xs0[way] = message + q[:, n + 1 : n + 2] * prior_row
        if way == 1:
            message -= q[:, 0:1] * row_0
            message -= jnp.where(at == n - 1, q[:, 0:1] * end_col[:, 0:1], 0.0)
            message -= jnp.where(at == n + 1, q[:, 0:1] * prior_col[:, 0:1], 0.0)
            xs0[2] = message
    pl.semaphore_wait(barrier, len(greeted))
    send_all(x_peers, 0, gx, gx_n, xs0, xr0, x_send.at[0], x_recv.at[0])
    halos = []
    for i, (src, dst, peer) in enumerate(
        ((hrow, hrow_in, (up, gy)), (hcol, hcol_in, (gx, left)), (hcorner, hcorner_in, (up, left)))
    ):
        copy = pltpu.make_async_remote_copy(
            src_ref=src, dst_ref=dst, send_sem=halo_send.at[i], recv_sem=halo_recv.at[i],
            device_id=peer, device_id_type=MESH,
        )
        copy.start()
        halos.append(copy)
    col_mat, row_mat = col_table("mat0"), row_table("mat0")
    is_node = iota((1, lanes_c), 1) <= h

    def dense(layers):
        half = jnp.concatenate([dot(row_mat[:, 0:n0], w0[d]) for d in layers], axis=0)
        value = jnp.where(is_node, dot(half, col_mat[0:n0]), 0.0)
        return [value[i * rows_c : (i + 1) * rows_c] for i in range(len(layers))]

    base = dense(range(BEFORE_HALO))
    for copy in halos:
        copy.wait_recv()
    row_255, row_256, col_255, col_256, next_row, next_col = edges(
        jnp.where(last_x, own_254, hrow_in[...]), jnp.where(last_y, packed[4:8], hcol_in[...]), hcorner_in[:, 0:1]
    )
    cols = []
    for way in range(2):
        q = cv[way : way + 1, 0:wide]
        cols.append(
            own_cols[4 * way : 4 * way + 4]
            + q[:, n - 1 : n] * col_255
            + q[:, n : n + 1] * col_256
            + jnp.where(at == n - 1, line(row_255, q), 0.0)
            + jnp.where(at == n, line(row_256, q), 0.0)
        )
    down_x = dot(jnp.concatenate(cols + [col_255, col_256], axis=0), row_table("mat0"), ((1,), (1,)))
    down_x = jnp.concatenate([down_x, jnp.zeros((16, lanes_c - rows_c), jnp.float32)], axis=1)
    select = selection(n, last_y)[0:n]
    next_even = pick_dot(next_row[:, 0:n], select)
    next_col_even = jnp.where(last_y, 0.0, pick_dot(next_col, selection(n, last_x)))
    evens = []
    for d in range(DEPTH):
        even = jnp.concatenate([u0[d, j, pl.ds(0, h, stride=2), :] for j in range(2)], axis=1)
        even = pick_dot(even, select)
        tail = jnp.where(last_x, even[h - 2 : h - 1], next_even[d : d + 1])
        tail = jnp.where(iota((8, lanes_c), 0) == 0, tail, 0.0)
        evens.append(jnp.concatenate([even, tail], axis=0))

    pltpu.make_async_copy(xr0, xr0, x_recv.at[0]).wait()
    a_right, a_left = gather(xr0, row_v, row_places, gx_n)
    a_right += rv[28:29, n + 1 : n + 2] * prior_row
    p_r, p_l = rv[2:3, 0:lanes_c], rv[3:4, 0:lanes_c]
    lane4 = iota((4, 128), 1)
    layer = iota((4, 128), 0)
    shared = jnp.zeros((4, 128), jnp.float32)
    for i, value in enumerate((a_right[:, n + 1 : n + 2], a_left[:, n + 1 : n + 2], a_right[:, 0:1], a_left[:, 0:1])):
        shared = jnp.where(lane4 == 4 * (i + 1) + layer, value, shared)
    q_right, q_left = cv[26:27, 0:wide], cv[27:28, 0:wide]
    q_near = jnp.where((iota((1, wide), 1) == 0) | (iota((1, wide), 1) == n + 1), 0.0, q_left)
    for i, q in enumerate((q_right, q_left, q_near)):
        way = (i + 1) // 2
        cols = down_x[4 * way : 4 * way + 4] + line(a_right, q) * p_r + line(a_left, q) * p_l
        ys0[i, 0:4] = cols[:, 0:h]
        ys0[i, 4:5] = jnp.sum(jnp.where(lane4 == layer, cols[:, h : h + 1], shared), axis=0, keepdims=True)
    send_all(y_peers, 1, gy, gy_n, ys0, yr0, y_send.at[0], y_recv.at[0])
    base += dense(range(BEFORE_HALO, DEPTH))
    base = [base[d] + evens[d] for d in range(DEPTH)]
    carried = dot(jnp.concatenate([a_right, a_left, row_255, row_256], axis=0), col_mat)
    four = lambda row: jnp.broadcast_to(row, (4, lanes_c))
    other = jnp.concatenate(
        [jnp.where(is_node, carried, 0.0), twice(cv, 2, lanes_c)]
        + [four(jnp.where(is_node, col_mat[n - 1 + i : n + i, :], 0.0)) for i in range(2)]
        + [four(jnp.where(iota((1, lanes_c), 1) == h, 1.0, 0.0)), jnp.zeros((4, lanes_c), jnp.float32)],
        axis=0,
    )
    own = jnp.concatenate([twice(rv, 2, lanes_c), twice(rv, 4, lanes_c)], axis=0)
    rest = jnp.concatenate([down_x[8:16], next_col_even, jnp.zeros((4, lanes_c), jnp.float32)], axis=0)
    itself = cv[28:29, n0 + 1 : n0 + 2] * (a_right[:, n0 + 1 : n0 + 2] * p_r + a_left[:, n0 + 1 : n0 + 2] * p_l)
    itself = jnp.concatenate([itself, jnp.zeros((4, lanes_c), jnp.float32)], axis=0)
    lhs = jnp.concatenate([own, itself, rest], axis=0).T[0:rows_c]
    for d in range(DEPTH):
        u1[d] = base[d] + dot(lhs, jnp.where(iota((40, lanes_c), 0) % 4 == d, other, 0.0))
        w1[d] = detail(u1[d])

    n, h, g = n0 // 2, n0 // 4, n0 // 8
    lane = iota((8, 128), 1)
    ways = jnp.concatenate([rv[8:16, 0:256], row_table("taken")[:, 0:256]], axis=0).T
    functionals = jnp.concatenate([ways[:, 0:2], ways[:, 4:8]], axis=1)
    of_w = dot(row_sums([w1[d] for d in range(DEPTH)], functionals, 6), col_table("mat1"))
    taken = row_sums([u1[d] for d in range(DEPTH)], ways[:, 8:12], 4)
    of_next = of_w[8:24] + pick_dot(taken, selection(n, last_y))
    after = col_table("after")
    of_second = dot(jnp.concatenate([of_next[0:8], of_next[8:16]], axis=1), after[0:256])
    is_c = (lane == h + 1) | (lane == h + 2)
    sent = of_w[0:8] + pltpu.roll(of_second, h + 3, 1)
    for i in range(2):
        sent += pltpu.roll(jnp.where(is_c, of_w[8 + 8 * i : 16 + 8 * i], 0.0), g + 5 + 2 * i, 1)
    late_rows, late_own = col_table("late"), row_table("late_own")
    late_ends = [dot(late_own[:, 0:8], late_rows[16 + 8 * i : 24 + 8 * i]) for i in range(2)]
    late_table = row_table("late")

    pltpu.make_async_copy(yr0, yr0, y_recv.at[0]).wait()
    values = gather(yr0, col_v, col_places, gy_n)
    carries = jnp.concatenate([value[0:4] for value in values], axis=0)
    spot = iota((8, 128), 1) == iota((8, 128), 0) % 4
    tails = jnp.concatenate([jnp.broadcast_to(value[4:5], (4, 128)) for value in values], axis=0)
    tails = line(jnp.where(spot, tails, 0.0), 1.0)
    inner = INNER.get(gy_n, 1)
    near = inner - 1 + (gy_n - inner) * ((gy % inner + 1) // inner)
    told = jnp.where(last_y, 0.0, jnp.broadcast_to(yr0[near - 1, 4:5, :], (4, 128)))
    told = [line(jnp.where(lane4 == 4 * (i + 1) + layer, told, 0.0), 1.0) for i in range(4)]
    scalars = dot(carries, late_table[0:128]) + tails * late_table[128:129]
    change = []
    for x_way in range(2):
        part = jnp.zeros((4, 128), jnp.float32)
        for m in range(8):
            for way in range(2):
                scalar = scalars[4 * way : 4 * way + 4, 2 * m + x_way : 2 * m + x_way + 1]
                part += scalar * late_rows[8 * way + m : 8 * way + m + 1]
        for i in range(4):
            row = 2 * x_way + i % 2
            part += told[i] * late_ends[i // 2][row : row + 1]
        change.append(part)
    sent = sent + jnp.concatenate(change, axis=0)
    xs1[...] = sent
    xr1[0] = sent
    send_same(x_peers, xs1, xr1, x_send.at[1], x_recv.at[1])
    ends_y = [jnp.where(is_node, col_mat[n0 - 1 + i : n0 + i, :], 0.0) for i in range(2)]
    late = jnp.concatenate([told[i] * ends_y[0] + told[2 + i] * ends_y[1] for i in range(2)], axis=0)
    carries = jnp.concatenate([carries, jnp.where(lane == 0, tails, 0.0)], axis=1)
    lhs = jnp.concatenate([carries, twice(rv, 2, lanes_c)], axis=0).T[0:rows_c]
    other = jnp.concatenate([twice(cv, 2, lanes_c), late], axis=0)
    for d in range(DEPTH):
        u1[d] = u1[d] + dot(lhs, jnp.where(iota((16, lanes_c), 0) % 4 == d, other, 0.0))
        w1[d] = detail(u1[d])
    base1, solved1 = local_level(1, n, u1, w1)
    cols = jnp.zeros((padded_rows(h), 128), jnp.float32)
    spot = iota(cols.shape, 1)
    for d in range(DEPTH):
        for way in range(2):
            cols = jnp.where(spot == 4 * way + d, solved1[d][:, h + 1 + way : h + 2 + way], cols)
            cols = jnp.where(spot == 8 + 4 * way + d, line(base1[d], cv[16 + way : 17 + way, 0:128]), cols)
            cols = jnp.where(spot == 16 + 4 * way + d, line(base1[d], cv[12 + way : 13 + way, 0:128]), cols)
    cols = jnp.concatenate([cols, jnp.zeros((128 - padded_rows(h), 128), jnp.float32)], axis=0).T
    row_after = row_table("after")
    cols1, cols2 = cols[0:8], dot(jnp.concatenate([cols[8:16], cols[16:24]], axis=1), row_after[0:256])
    others = xr1.at[pl.ds(1, gx_n - 1)]
    pltpu.make_async_copy(others, others, x_recv.at[1]).wait()
    got = dot(row_table("join")[:, 0 : gx_n * 8], xr1[...].reshape(gx_n * 8, 128))
    a_1 = got[0:8]
    a_2 = pltpu.roll(got[24:32], 128 - (h + 3), 1) + dot(
        jnp.concatenate([got[8:16], got[16:24]], axis=1), after[0:256]
    )
    msg, msg2, hs = [], [], []
    for way in range(2):
        msg.append(cols1[4 * way : 4 * way + 4] + outer(a_1[:, h + 1 + way : h + 2 + way], rv, 10, 128))
        row = outer(line(a_1, cv[16 + way : 17 + way, 0:128]), rv, 20, 128)
        row += outer(line(a_1, cv[12 + way : 13 + way, 0:128]), rv, 22, 128)
        row += outer(a_2[:, g + 1 + way : g + 2 + way], rv, 18, 128)
        msg2.append(cols2[4 * way : 4 * way + 4] + row)
        block = jnp.zeros((4, 128), jnp.float32)
        for i in range(2):
            at = h + g + 6 + 2 * i + way
            h_col = got[24:32, at : at + 1] + got[8 + 8 * i : 16 + 8 * i, h + 1 + way : h + 2 + way]
            for x_way in range(2):
                block += jnp.where(iota((4, 128), 1) == h + 1 + 2 * i + x_way, h_col[4 * x_way : 4 * x_way + 4], 0.0)
        hs.append(block)
    sent = jnp.concatenate(msg, axis=0) + pltpu.roll(jnp.concatenate(msg2, axis=0), h + 5, 1)
    sent += jnp.concatenate(hs, axis=0)
    ys1[...] = sent
    yr1[0] = sent
    send_same(y_peers, ys1, yr1, y_send.at[1], y_recv.at[1])
    down_turned = jnp.concatenate([col_255, col_255], axis=0).T[0:n0]
    is_last = iota((n0, 128), 1) == 127
    for d in range(DEPTH):
        out_v[d, 0] = w0[d, :, 0:128]
        out_v[d, 1] = w0[d, :, 128:256] + jnp.where(is_last, down_turned[:, d : d + 1], 0.0)
        for j in range(2):
            tail = iota((8, 128), 0) == 7
            fix = row_255[d : d + 1, 128 * j : 128 * j + 128]
            out_v[d, j, n0 - 8 : n0, :] = out_v[d, j, n0 - 8 : n0, :] + jnp.where(tail, fix, 0.0)
    base2, _ = local_level(2, h, base1, [detail(base1[d]) for d in range(DEPTH)])
    spread_out([w1[d] for d in range(DEPTH)], n, 256, 2, 2)
    beside = lambda value: jnp.concatenate([value[128 * i : 128 * i + 128] for i in range(3)], axis=1)
    nodes_1 = lambda value: jnp.where(lane <= h, value, 0.0)
    nodes_2 = lambda value: jnp.where(lane <= g, value, 0.0)
    other1 = jnp.concatenate([nodes_1(a_1), twice(cv, 10, 128)], axis=0)
    across = dot(a_1, beside(after))
    other2 = jnp.concatenate(
        [nodes_2(across[:, 256:384]), nodes_2(across[:, 0:128]), nodes_2(across[:, 128:256]), nodes_2(a_2)]
        + [twice(cv, row, 128) for row in (24, 20, 22, 18)],
        axis=0,
    )
    own = jnp.concatenate([twice(rv, row, 128) for row in (24, 20, 22, 18)], axis=0)
    row_after = beside(row_after)
    others = yr1.at[pl.ds(1, gy_n - 1)]
    pltpu.make_async_copy(others, others, y_recv.at[1]).wait()
    got = dot(col_table("join"), yr1[...].reshape(gy_n * 8, 128))
    down = dot(got[0:24], row_after)
    c_2 = nodes_2(pltpu.roll(got[24:32], 128 - (h + 5), 1) + down[8:16, 0:128] + down[16:24, 128:256])
    lhs = jnp.concatenate([own, down[0:8, 256:384], down[0:8, 0:128], down[0:8, 128:256], c_2], axis=0)
    lhs = jnp.concatenate([lhs, jnp.zeros_like(lhs)], axis=0).T[0 : padded_rows(g), 0:64]
    lhs1 = jnp.concatenate([twice(rv, 10, 128), nodes_1(got[0:8])], axis=0).T[0 : padded_rows(h)]
    details, last = [], []
    for d in range(DEPTH):
        last.append(base2[d] + dot(lhs, jnp.where(iota((64, 128), 0) % 4 == d, other2, 0.0)))
        nodes = base1[d] + dot(lhs1, jnp.where(iota((16, 128), 0) % 4 == d, other1, 0.0))
        details.append(detail(nodes))
    spread_out(details, h, 128, 4, 2)
    spread_out(last, g, 128, 8, 3)
    for d in range(DEPTH):
        out[d] = jnp.concatenate([out_v[d, j] for j in range(n0 // 128)], axis=1)

    for i, copy in enumerate(halos):
        copy.wait_send()
    pltpu.make_async_copy(xr0, xr0, x_send.at[0]).wait()
    pltpu.make_async_copy(yr0, yr0, y_send.at[0]).wait()
    others = xr1.at[pl.ds(1, gx_n - 1)]
    pltpu.make_async_copy(others, others, x_send.at[1]).wait()
    others = yr1.at[pl.ds(1, gy_n - 1)]
    pltpu.make_async_copy(others, others, y_send.at[1]).wait()


def even_rows(tall_v, value, rows_c):
    rows, lanes = value.shape
    half = rows // 2
    parts = []
    for j in range(lanes // 128):
        tall_v[j, 0:rows] = value[:, 128 * j : 128 * j + 128]
        part = tall_v[j, pl.ds(0, half, stride=2), :]
        parts.append(jnp.concatenate([part, jnp.zeros((rows_c - half, 128), jnp.float32)], axis=0))
    return jnp.concatenate(parts, axis=1)


def add_rows(ref, d, value, stride):
    place = pl.ds(0, value.shape[0], stride=stride)
    for j in range(ref.shape[1]):
        ref[d, j, place, :] = ref[d, j, place, :] + value[:, 128 * j : 128 * j + 128]


def shards(salinity):
    gx_n, gy_n = lax.axis_size("gx"), lax.axis_size("gy")
    _, nx, ny = salinity.shape
    n0 = nx
    (row_tab, row_places), (col_tab, col_places) = tables(nx * gx_n, ny * gy_n, gx_n, gy_n)
    vmem = lambda *shape: pltpu.VMEM(shape, jnp.float32)
    dma = lambda count: pltpu.SemaphoreType.DMA((count,))
    wide = padded_lanes(n0)
    second = vmem(DEPTH, padded_rows(n0 // 2), padded_lanes(n0 // 2))
    scratch = [vmem(DEPTH, n0 // 128, n0, 128), vmem(DEPTH, 2, n0, 128), second, vmem(DEPTH, n0, n0), second, vmem(2, padded_rows(n0), 128)]
    scratch += [vmem(*row_tab.shape[1:]), vmem(*col_tab.shape[1:])]
    scratch += [vmem(DEPTH, n0), vmem(DEPTH, n0), vmem(DEPTH, 128)] * 2
    scratch += [vmem(3, DEPTH, wide), vmem(gx_n - 1, DEPTH, wide)]
    scratch += [vmem(3, DEPTH + 1, n0 // 2), vmem(gy_n - 1, DEPTH + 1, n0 // 2)]
    scratch += [vmem(8, 128), vmem(gx_n, 8, 128), vmem(8, 128), vmem(gy_n, 8, 128)]
    scratch += [dma(4), dma(3), dma(3), dma(2), dma(2), dma(2), dma(2)]
    anywhere = pl.BlockSpec(memory_space=pl.ANY)
    out = pl.pallas_call(
        functools.partial(kernel, gx_n, gy_n, n0, row_places, col_places),
        out_shape=jax.ShapeDtypeStruct(salinity.shape, jnp.float32),
        in_specs=[anywhere] * 3,
        out_specs=pl.BlockSpec(memory_space=pltpu.VMEM),
        scratch_shapes=scratch,
        compiler_params=pltpu.CompilerParams(
            collective_id=0, has_side_effects=True, vmem_limit_bytes=VMEM_LIMIT
        ),
    )(salinity, row_tab, col_tab)
    return out


def solution(mesh):
    placed = P(None, "gx", "gy")
    return jax.shard_map(shards, mesh=mesh, in_specs=(placed,), out_specs=placed, check_vma=False)
```

```python
import functools

import jax
import jax.numpy as jnp
import numpy as np
from jax import lax
from jax.experimental import pallas as pl
from jax.experimental.pallas import tpu as pltpu
from jax.sharding import PartitionSpec as P

LEVELS = 3
DEPTH = 4
LENGTH = 64.0
MESH = pl.DeviceIdType.MESH
TABLE_LANES = 384
BEFORE_HALO = 2
INNER = {8: 2, 32: 8}
VMEM_LIMIT = 52 * 1024 * 1024


def padded_rows(count):
    return count + 8


def padded_lanes(count):
    return (count // 128 + 1) * 128 if count >= 128 else 128


def partner(me, slot, tiles, sign):
    inner = INNER.get(tiles, 1)
    outer = tiles // inner
    far = (me // inner + outer + sign * (slot // inner)) % outer
    return far * inner + (me % inner + inner + sign * (slot % inner)) % inner


def farthest_first(tiles):
    inner = INNER.get(tiles, 1)
    outer = tiles // inner
    hops = lambda k: min(k // inner, outer - k // inner) + min(k % inner, inner - k % inner)
    return sorted(range(1, tiles), key=lambda k: -hops(k))


def solver_line(count):
    off = 1.0 / (3.0 * LENGTH) - LENGTH
    inner = 4.0 / (3.0 * LENGTH) + 2.0 * LENGTH
    end = 2.0 / (3.0 * LENGTH) + LENGTH
    diag = np.full(count, inner)
    diag[0] = diag[-1] = end
    q = np.ones(count)
    p = np.ones(count)
    q[1] = -diag[0] / off
    p[-2] = -diag[-1] / off
    for i in range(1, count - 1):
        q[i + 1] = -(diag[i] * q[i]) / off - q[i - 1]
        j = count - 1 - i
        p[j - 1] = -(diag[j] * p[j]) / off - p[j + 1]
    return q, p, diag[0] * p[0] + off * p[1]


def load_block(total, coarse_ids, fine_ids):
    out = np.zeros((len(coarse_ids), len(fine_ids)))

    def mass(i, j):
        if i < 0 or i >= total or j < 0 or j >= total:
            return 0.0
        if i == j:
            return (2.0 if i in (0, total - 1) else 4.0) / 6.0
        return 1.0 / 6.0 if abs(i - j) == 1 else 0.0

    for a, k in enumerate(coarse_ids):
        if k < 0 or k >= total // 2:
            continue
        upper = 1.0 if 2 * k + 1 == total - 1 else 0.5
        for b in range(max(0, 2 * k - 2 - fine_ids[0]), min(len(fine_ids), 2 * k + 3 - fine_ids[0])):
            j = fine_ids[b]
            out[a, b] = mass(2 * k, j) + 0.5 * mass(2 * k - 1, j) + upper * mass(2 * k + 1, j)
    return out


def line_tables(total, tiles):
    n = total // tiles
    h = n // 2
    coarse = total // 2
    q, p, w = solver_line(coarse)
    local, functional, carry, weight, select, wide = [], [], [], [], [], []
    for t in range(tiles):
        first = t * h
        last_tile = t == tiles - 1
        ids = np.arange(first, first + h + 1)
        if last_tile:
            ids[h] = ids[h - 2]
        window = np.arange(first - 1, first + h + 2)
        load = load_block(total, window, np.arange(t * n, t * n + n + 1))
        inside = (window >= 0) & (window < coarse)
        safe = np.clip(window, 0, coarse - 1)
        low = np.minimum(ids[:, None], safe[None, :])
        high = np.maximum(ids[:, None], safe[None, :])
        green = np.where(inside[None, :], q[low] * p[high] / w, 0.0)
        local.append(green @ load)
        q_end = q[min(first + h, coarse - 1)]
        to_right = (np.where(inside, q[safe] / q_end, 0.0)) @ load
        to_left = (np.where(inside, p[safe] / p[first], 0.0)) @ load
        before = load_block(total, window, np.array([t * n - 1]))
        own = [np.append(f[:n], np.where(inside, v, 0.0) @ before) for f, v in
               ((to_right, q[safe] / q_end), (to_left, p[safe] / p[first]))]
        wide.append(np.stack(own + [own[0] * q_end * p[first] / w]))
        to_right[n] = 0.0
        to_left[0] = 0.0
        functional.append(np.stack([to_right, to_left]))
        carry.append(np.stack([p[ids] / p[first], q[ids] / q_end]))
        weights = np.zeros((2, tiles))
        for k in range(1, tiles):
            s = partner(t, k, tiles, -1)
            if s < t:
                weights[0, k] = q[(s + 1) * h] * p[first] / w
            else:
                weights[1, k] = q_end * p[s * h] / w
        weight.append(weights)
        pick = np.zeros((n + 1, h + 1))
        pick[2 * np.arange(h), np.arange(h)] = 1.0
        pick[n - 4 if last_tile else n, h] = 1.0
        select.append(pick)
    return [np.stack(item) for item in (local, functional, carry, weight, select, wide)]


def fit(array, shape):
    out = np.zeros(array.shape[: array.ndim - len(shape)] + tuple(shape))
    out[tuple(slice(0, size) for size in array.shape)] = array
    return out


def interpolation(nodes):
    out = np.eye(nodes)
    for i in range(1, nodes, 2):
        out[i] = 0.0
        out[i, i - 1] = out[i, i + 1] = 0.5
    return out


def pair_weights(weight):
    tiles = weight.shape[0]
    out = np.zeros((tiles, tiles, 2, 2))
    for t in range(tiles):
        for k in range(1, tiles):
            for way in range(2):
                out[t, partner(t, k, tiles, -1), way, way] = weight[t, way, k]
    return out


def joined_weights(first, couplings, second):
    tiles = first.shape[0]
    blocks = [first]
    blocks += [np.einsum("tsab,sbc,sucd->tuad", second, k, first) for k in couplings]
    blocks.append(second)
    out = np.zeros((tiles, 4, 2, DEPTH, tiles, 2, DEPTH))
    for t in range(tiles):
        for slot in range(tiles):
            for d in range(DEPTH):
                for i, block in enumerate(blocks):
                    out[t, i, :, d, slot, :, d] = block[t, partner(t, slot, tiles, -1)]
    return out.reshape(tiles, 32, tiles * 8)


def packed(tables):
    places, blocks, at = {}, [], 0
    for name, table in tables.items():
        rows, lanes = -(-table.shape[1] // 8) * 8, -(-table.shape[2] // 128) * 128
        table = fit(table, (rows, lanes))
        places[name] = (at, rows, lanes // 128)
        at += rows * (lanes // 128)
        blocks += [table[:, :, 128 * j : 128 * j + 128] for j in range(lanes // 128)]
    return np.ascontiguousarray(np.concatenate(blocks, axis=1), np.float32), places


@functools.lru_cache(maxsize=None)
def tables(nx, ny, gx, gy):
    row_vecs = np.zeros((gx, 8 * LEVELS + 8, TABLE_LANES))
    col_vecs = np.zeros((gy, 8 * LEVELS + 8, TABLE_LANES))
    row_out, col_out, sides = {}, {}, []
    for vecs, size, tiles, out in ((row_vecs, nx, gx, row_out), (col_vecs, ny, gy, col_out)):
        lines = [line_tables(size >> level, tiles) for level in range(LEVELS)]
        sides.append(lines)
        for level, (local, functional, carry, weight, select, wide) in enumerate(lines):
            n = (size >> level) // tiles
            h = n // 2
            vecs[:, 8 * level : 8 * level + 2, : n + 1] = functional
            vecs[:, 8 * level + 2 : 8 * level + 4, : h + 1] = carry
            if level == 0:
                vecs[:, 26:29, :n] = wide[:, :, :n]
                vecs[:, 26:29, n + 1] = wide[:, :, n]
            if vecs is row_vecs:
                out[f"mat{level}"] = fit(local, (padded_rows(h), padded_lanes(n)))
                if level == 0:
                    vecs[:, 4, : h + 1] = local[:, :, n - 1]
                    vecs[:, 5, : h + 1] = local[:, :, n]
            else:
                joined = np.concatenate([local, functional], axis=1).transpose(0, 2, 1)
                out[f"mat{level}"] = fit(joined, (padded_lanes(n), padded_lanes(h)))
        out["weight"] = np.repeat(lines[0][3].reshape(tiles, 2 * tiles, 1), 128, axis=2)
    nodes = (nx // gx >> 2) + 1
    inter = interpolation(nodes)
    rest = np.eye(nodes) - inter
    (local_a, _, carry_a, weight_a, select_a, _), (local_b, func_b, carry_b, weight_b, select_b, _) = sides[0][1:]
    row_k = [np.einsum("tbi,ij,taj->tba", func_b, op, carry_a) for op in (rest, inter)]
    row_out["join"] = joined_weights(pair_weights(weight_a), row_k, pair_weights(weight_b))
    after = np.zeros((gx, 384, 128))
    half = carry_b.shape[2]
    taken = np.zeros((gx, 8, TABLE_LANES))
    for i, op in enumerate((rest, inter)):
        func = func_b @ op
        row_vecs[:, 12 + 2 * i : 14 + 2 * i, : local_a.shape[2]] = np.einsum("tij,tjk->tik", func, local_a)
        taken[:, 2 * i : 2 * i + 2, : select_a.shape[1]] = np.einsum("tij,tkj->tik", func, select_a)
        row_vecs[:, 20 + 2 * i : 22 + 2 * i, :half] = np.einsum("tij,taj->tai", local_b @ op, carry_a)
        after[:, 128 * i : 128 * i + nodes, :half] = (local_b @ op).transpose(0, 2, 1)
        after[:, 128 * i + nodes + 2 * i : 128 * i + nodes + 2 * i + 2, :half] = carry_b
    after[:, 256 : 256 + nodes, :half] = select_b
    row_vecs[:, 24:26, :half] = carry_a @ select_b
    fine = local_a.shape[2]
    inter_a = interpolation(fine)
    rest_a = np.eye(fine) - inter_a
    of_w = [sides[0][1][1], row_vecs[:, 12:14, :fine], row_vecs[:, 14:16, :fine]]
    late = [of_w[0] @ rest_a, of_w[0] @ inter_a]
    for i in range(2):
        late += [of_w[1 + i] @ rest_a, of_w[1 + i] @ inter_a, taken[:, 2 * i : 2 * i + 2, :fine]]
    late = np.stack(late, axis=1)
    late_own = np.einsum("tmxi,tpi->txpm", late, sides[0][0][2]).reshape(gx, 4, 8)
    late = late.reshape(gx, 16, fine).transpose(0, 2, 1)
    row_out.update(after=after, taken=taken, vecs=row_vecs, late=fit(late, (256, 128)), late_own=fit(late_own, (8, 128)))
    (_, _, carry_a, weight_a, _, _), (local_b, func_b, _, weight_b, select_b, _) = sides[1][1:]
    col_k = [np.einsum("tbi,ij,taj->tba", func_b, op, carry_a) for op in (np.eye(nodes), rest)]
    col_out["join"] = joined_weights(pair_weights(weight_a), col_k, pair_weights(weight_b))
    after = np.zeros((gy, 384, 128))
    col_vecs[:, 12:14, :nodes] = func_b @ rest
    both = np.concatenate([local_b, func_b], axis=1)
    for i, op in enumerate((np.eye(nodes), rest)):
        col_vecs[:, 20 + 2 * i : 22 + 2 * i, :half] = np.einsum("tij,taj->tai", local_b @ op, carry_a)
        after[:, 128 * i : 128 * i + nodes, : both.shape[1]] = (both @ op).transpose(0, 2, 1)
    after[:, 256 : 256 + nodes, :half] = select_b
    col_vecs[:, 24:26, :half] = carry_a @ select_b
    first = np.concatenate(sides[1][1][0:2], axis=1)
    select_a = sides[1][1][4]
    vectors = [sides[1][0][2][:, 0], sides[1][0][2][:, 1], sides[1][0][0][:, :, -2], sides[1][0][0][:, :, -1]]
    late = np.zeros((gy, 4, 8, 128))
    lanes = first.shape[1]
    for i, vector in enumerate(vectors):
        for t in range(gy):
            for k, op in enumerate((np.eye(fine), rest_a)):
                image = first[t] @ (op @ vector[t])
                late[t, i, k, :lanes] = image
                for m, second in enumerate((np.eye(nodes), rest)):
                    at = 2 + 3 * m + k
                    late[t, i, at, lanes : lanes + both.shape[1]] = both[t] @ (second @ image[:nodes])
                    start = lanes + both.shape[1] + 2 * m
                    late[t, i, at, start : start + 2] = image[nodes:lanes]
            for m, second in enumerate((np.eye(nodes), rest)):
                late[t, i, 4 + 3 * m, lanes : lanes + both.shape[1]] = both[t] @ (second @ (vector[t] @ select_a[t]))
    col_out.update(after=after, vecs=col_vecs, late=late.reshape(gy, 32, 128))
    return packed(row_out), packed(col_out)


def parts(value, count):
    out = []
    for _ in range(count):
        out.append(value.astype(jnp.bfloat16))
        value = value - out[-1].astype(jnp.float32)
    return out


def dot(a, b, dims=((1,), (0,))):
    return lax.dot_general(
        a, b, (dims, ((), ())), precision=lax.Precision.HIGHEST, preferred_element_type=jnp.float32
    )


def pick_dot(a, b, count=3, dims=((1,), (0,)), ones=1):
    total = None
    for part in reversed(parts(b if ones == 0 else a, count)):
        x, y = (a.astype(jnp.bfloat16), part) if ones == 0 else (part, b.astype(jnp.bfloat16))
        term = lax.dot_general(x, y, (dims, ((), ())), preferred_element_type=jnp.float32)
        total = term if total is None else total + term
    return total


def iota(shape, dim):
    return lax.broadcasted_iota(jnp.int32, shape, dim)


def detail(u, alone=False):
    rows, lanes = u.shape
    lane, row = iota(u.shape, 1), iota(u.shape, 0)
    left, right = pltpu.roll(u, 1, 1), pltpu.roll(u, lanes - 1, 1)
    if alone:
        right = jnp.where(lane == lanes - 1, left, right)
    along = jnp.where(lane % 2 == 1, 0.5 * (left + right), u)
    above, below = pltpu.roll(along, 1, 0), pltpu.roll(along, rows - 1, 0)
    if alone:
        below = jnp.where(row == rows - 1, above, below)
    return u - jnp.where(row % 2 == 1, 0.5 * (above + below), along)


def spread_matrix(count, lanes, stride, width):
    shape = (lanes, width)
    row = iota(shape, 0)
    return jnp.where((iota(shape, 1) == stride * row) & (row < count), 1.0, 0.0).astype(jnp.float32)


def kernel(gx_n, gy_n, n0, row_places, col_places, *refs):
    (sal, row_in, col_in, out, out_v, u0, u1, w0, w1, tall_v, row_v, col_v,
     hrow, hcol, hcorner, hrow_in, hcol_in, hcorner_in, xs0, xr0, ys0, yr0, xs1, xr1, ys1, yr1,
     load_sem, halo_send, halo_recv, x_send, x_recv, y_send, y_recv) = refs

    def table(ref, places, name):
        at, rows, tiles = places[name]
        return jnp.concatenate([ref[at + j * rows : at + (j + 1) * rows] for j in range(tiles)], axis=1)

    row_table = functools.partial(table, row_v, row_places)
    col_table = functools.partial(table, col_v, col_places)
    gx, gy = lax.axis_index("gx"), lax.axis_index("gy")
    last_x, last_y = gx == gx_n - 1, gy == gy_n - 1

    barrier = pltpu.get_barrier_semaphore()
    x_peers = [(k, (partner(gx, k, gx_n, 1), gy)) for k in farthest_first(gx_n)]
    y_peers = [(k, (gx, partner(gy, k, gy_n, 1))) for k in farthest_first(gy_n)]
    up, left = lax.rem(gx + gx_n - 1, gx_n), lax.rem(gy + gy_n - 1, gy_n)
    greeted = [peer for _, peer in y_peers + x_peers] + [(lax.rem(gx + 1, gx_n), lax.rem(gy + 1, gy_n))]
    for peer in greeted:
        pl.semaphore_signal(barrier, inc=1, device_id=peer, device_id_type=MESH)

    loads = [
        pltpu.make_async_copy(sal.at[:, :, pl.ds(128 * j, 128)], u0.at[:, j], load_sem.at[j]) for j in range(2)
    ]
    loads.append(pltpu.make_async_copy(row_in.at[gx], row_v, load_sem.at[2]))
    loads.append(pltpu.make_async_copy(col_in.at[gy], col_v, load_sem.at[3]))
    for copy in loads:
        copy.start()

    loads[0].wait()
    loads[1].wait()
    hrow[...] = jnp.concatenate([u0[:, 0, 0, :], u0[:, 1, 0, :]], axis=1)
    hcorner[...] = u0[:, 0, 0, :]
    lane = iota((n0, 128), 1)
    packed = jnp.zeros((n0, 128), jnp.float32)
    for d in range(DEPTH):
        packed = jnp.where(lane == d, u0[d, 0, :, 0:1], packed)
        packed = jnp.where(lane == 4 + d, u0[d, 1, :, 126:127], packed)
    packed = packed.T
    hcol[...] = packed[0:4]
    def send_all(peers, axis, me, count, src, dst, send, recv):
        for k, peer in peers:
            before = (me + count - 1 - peer[axis]) // count
            way = before + before * (1 - (me + count - 2 - peer[axis]) // count)
            pltpu.make_async_remote_copy(
                src_ref=src.at[way], dst_ref=dst.at[k - 1], send_sem=send, recv_sem=recv,
                device_id=peer, device_id_type=MESH,
            ).start()

    def send_same(peers, src, dst, send, recv):
        for k, peer in peers:
            pltpu.make_async_remote_copy(
                src_ref=src, dst_ref=dst.at[k], send_sem=send, recv_sem=recv, device_id=peer, device_id_type=MESH
            ).start()

    def gather(buf, ref, places, count):
        at, _, _ = places["weight"]
        tiles = buf.shape[2] // 128
        sums = [jnp.zeros(buf.shape[1:], jnp.float32)] * 2
        for k in range(1, count):
            for way in range(2):
                weight = ref[at + way * count + k : at + way * count + k + 1, :]
                sums[way] = sums[way] + jnp.concatenate([weight] * tiles, axis=1) * buf[k - 1]
        return sums

    def selection(n, last):
        shape = (padded_lanes(n), padded_lanes(n // 2))
        row, lane = iota(shape, 0), iota(shape, 1)
        tail = jnp.where(last, n - 4, n)
        hit = ((lane < n // 2) & (row == 2 * lane)) | ((lane == n // 2) & (row == tail))
        return jnp.where(hit, 1.0, 0.0)

    def local_level(level, n, u, w):
        h = n // 2
        rows, rows_c, lanes_c = padded_rows(n), padded_rows(h), padded_lanes(h)
        col_mat, row_mat = col_table(f"mat{level}"), row_table(f"mat{level}")[:, 0:rows]
        select = selection(n, last_y)
        base, solved = [], []
        is_tail = iota((rows_c, lanes_c), 0) == h
        for d in range(DEPTH):
            z = dot(row_mat, dot(w[d], col_mat))
            even = even_rows(tall_v, pick_dot(u[d], select), rows_c)
            even = jnp.where(is_tail & last_x, even[h - 2 : h - 1, :], even)
            base.append(jnp.where(iota((rows_c, lanes_c), 1) <= h, z, 0.0) + even)
            solved.append(z)
        return base, solved

    def row_sums(values, weights, count=2):
        sums = []
        for way in range(count):
            for d in range(DEPTH):
                rows = values[d].shape[0]
                sums.append(jnp.sum(values[d] * weights[0:rows, way : way + 1], axis=0, keepdims=True))
        return jnp.concatenate(sums, axis=0)

    def line(value, functional):
        return jnp.sum(value * functional, axis=1, keepdims=True)

    def twice(table, row, lanes):
        return jnp.concatenate(
            [jnp.broadcast_to(table[row + way : row + way + 1, 0:lanes], (4, lanes)) for way in range(2)], axis=0
        )

    def outer(column, table, row, lanes):
        return (
            column[0:4] * table[row : row + 1, 0:lanes] + column[4:8] * table[row + 1 : row + 2, 0:lanes]
        )

    def spread_out(values, count, lanes, stride, pieces):
        mat = spread_matrix(count, lanes, stride, n0)
        for d in range(DEPTH):
            add_rows(out_v, d, pick_dot(values[d][0:count], mat, pieces), stride)

    n, h = n0, n0 // 2
    wide, rows_c, lanes_c = padded_lanes(n), padded_rows(h), padded_lanes(h)
    for copy in loads[2:]:
        copy.wait()
    rv, cv = row_table("vecs"), col_table("vecs")
    col_q = cv[0:2, 0:n]
    own_cols = jnp.zeros((n, 128), jnp.float32)
    for d in range(DEPTH):
        value = detail(jnp.concatenate([u0[d, 0], u0[d, 1]], axis=1), True)
        w0[d] = value
        for way in range(2):
            own_cols = jnp.where(lane == 4 * way + d, line(value, col_q[way : way + 1]), own_cols)
    own_rows = row_sums([w0[d] for d in range(DEPTH)], rv[24:32, 0:n].T[:, 2:4])
    own_cols = own_cols.T[0:8]
    none = jnp.zeros((8, 128), jnp.float32)
    own_rows = jnp.concatenate([own_rows, none], axis=1)
    own_cols = jnp.concatenate([own_cols, none], axis=1)
    at = iota((4, wide), 1)
    own_254 = jnp.concatenate([u0[:, 0, n - 2, :], u0[:, 1, n - 2, :]], axis=1)
    alias = packed[4:8, n - 2 : n - 1]
    wider = lambda value, end: jnp.where(at == n, end, jnp.concatenate([value, none[0:4]], axis=1))

    def between(value):
        mean = 0.5 * (pltpu.roll(value, 1, 1) + pltpu.roll(value, wide - 1, 1))
        return jnp.where(at > n, 0.0, jnp.where(at % 2 == 1, mean, value))

    def edges(next_row, next_col, corner):
        corner = jnp.where(
            last_y, next_row[:, n - 2 : n - 1], jnp.where(last_x, next_col[:, n - 2 : n - 1], corner)
        )
        row_change, col_change = wider(next_row - own_254, 0.0), wider(next_col - packed[4:8], corner - alias)
        next_row, next_col = wider(next_row, alias), wider(next_col, corner)
        rows = -0.5 * between(row_change), next_row - between(next_row)
        cols = -0.5 * between(col_change), next_col - between(next_col)
        return rows + cols + (next_row, next_col)

    zero_row = jnp.where(last_x, own_254, 0.0)
    zero_col = jnp.where(last_y, packed[4:8], 0.0)
    end_row, _, end_col, _, _, _ = edges(zero_row, zero_col, 0.0)
    first_row, first_col = hrow[...], hcol[...]
    prior_row = -0.5 * between(wider(first_row, jnp.where(last_y, first_row[:, n - 2 : n - 1], 0.0)))
    prior_row = jnp.where(at == n, 0.0, prior_row)
    prior_col = -0.5 * between(wider(first_col, jnp.where(last_x, first_col[:, n - 2 : n - 1], 0.0)))
    prior_col = jnp.where(at == n, 0.0, prior_col)
    prior_row = jnp.where(at == n + 1, -0.25 * first_row[:, 0:1], prior_row)
    row_0 = jnp.concatenate([w0[:, 0, :], none[0:4]], axis=1)
    for way in range(2):
        q = rv[26 + way : 27 + way, 0:wide]
        q_own = jnp.where(iota((1, wide), 1) < n, q, 0.0)
        message = own_rows[4 * way : 4 * way + 4] + q[:, n - 1 : n] * end_row
        message += jnp.where(at == n - 1, line(end_col, q_own), 0.0)
        message += jnp.where(at == n + 1, line(prior_col, q_own), 0.0)
        message = jnp.where(at == n, 0.0, message)
        xs0[way] = message + q[:, n + 1 : n + 2] * prior_row
        if way == 1:
            message -= q[:, 0:1] * row_0
            message -= jnp.where(at == n - 1, q[:, 0:1] * end_col[:, 0:1], 0.0)
            message -= jnp.where(at == n + 1, q[:, 0:1] * prior_col[:, 0:1], 0.0)
            xs0[2] = message
    pl.semaphore_wait(barrier, len(greeted))
    send_all(x_peers, 0, gx, gx_n, xs0, xr0, x_send.at[0], x_recv.at[0])
    halos = []
    for i, (src, dst, peer) in enumerate(
        ((hrow, hrow_in, (up, gy)), (hcol, hcol_in, (gx, left)), (hcorner, hcorner_in, (up, left)))
    ):
        copy = pltpu.make_async_remote_copy(
            src_ref=src, dst_ref=dst, send_sem=halo_send.at[i], recv_sem=halo_recv.at[i],
            device_id=peer, device_id_type=MESH,
        )
        copy.start()
        halos.append(copy)
    col_mat, row_mat = col_table("mat0"), row_table("mat0")
    is_node = iota((1, lanes_c), 1) <= h

    def dense(layers):
        half = jnp.concatenate([dot(row_mat[:, 0:n0], w0[d]) for d in layers], axis=0)
        value = jnp.where(is_node, dot(half, col_mat[0:n0]), 0.0)
        return [value[i * rows_c : (i + 1) * rows_c] for i in range(len(layers))]

    base = dense(range(BEFORE_HALO))
    for copy in halos:
        copy.wait_recv()
    row_255, row_256, col_255, col_256, next_row, next_col = edges(
        jnp.where(last_x, own_254, hrow_in[...]), jnp.where(last_y, packed[4:8], hcol_in[...]), hcorner_in[:, 0:1]
    )
    cols = []
    for way in range(2):
        q = cv[way : way + 1, 0:wide]
        cols.append(
            own_cols[4 * way : 4 * way + 4]
            + q[:, n - 1 : n] * col_255
            + q[:, n : n + 1] * col_256
            + jnp.where(at == n - 1, line(row_255, q), 0.0)
            + jnp.where(at == n, line(row_256, q), 0.0)
        )
    down_x = dot(jnp.concatenate(cols + [col_255, col_256], axis=0), row_table("mat0"), ((1,), (1,)))
    down_x = jnp.concatenate([down_x, jnp.zeros((16, lanes_c - rows_c), jnp.float32)], axis=1)
    select = selection(n, last_y)[0:n]
    next_even = pick_dot(next_row[:, 0:n], select)
    next_col_even = jnp.where(last_y, 0.0, pick_dot(next_col, selection(n, last_x)))
    evens = []
    for d in range(DEPTH):
        even = jnp.concatenate([u0[d, j, pl.ds(0, h, stride=2), :] for j in range(2)], axis=1)
        even = pick_dot(even, select)
        tail = jnp.where(last_x, even[h - 2 : h - 1], next_even[d : d + 1])
        tail = jnp.where(iota((8, lanes_c), 0) == 0, tail, 0.0)
        evens.append(jnp.concatenate([even, tail], axis=0))

    pltpu.make_async_copy(xr0, xr0, x_recv.at[0]).wait()
    a_right, a_left = gather(xr0, row_v, row_places, gx_n)
    a_right += rv[28:29, n + 1 : n + 2] * prior_row
    p_r, p_l = rv[2:3, 0:lanes_c], rv[3:4, 0:lanes_c]
    lane4 = iota((4, 128), 1)
    layer = iota((4, 128), 0)
    shared = jnp.zeros((4, 128), jnp.float32)
    for i, value in enumerate((a_right[:, n + 1 : n + 2], a_left[:, n + 1 : n + 2], a_right[:, 0:1], a_left[:, 0:1])):
        shared = jnp.where(lane4 == 4 * (i + 1) + layer, value, shared)
    q_right, q_left = cv[26:27, 0:wide], cv[27:28, 0:wide]
    q_near = jnp.where((iota((1, wide), 1) == 0) | (iota((1, wide), 1) == n + 1), 0.0, q_left)
    for i, q in enumerate((q_right, q_left, q_near)):
        way = (i + 1) // 2
        cols = down_x[4 * way : 4 * way + 4] + line(a_right, q) * p_r + line(a_left, q) * p_l
        ys0[i, 0:4] = cols[:, 0:h]
        ys0[i, 4:5] = jnp.sum(jnp.where(lane4 == layer, cols[:, h : h + 1], shared), axis=0, keepdims=True)
    send_all(y_peers, 1, gy, gy_n, ys0, yr0, y_send.at[0], y_recv.at[0])
    base += dense(range(BEFORE_HALO, DEPTH))
    base = [base[d] + evens[d] for d in range(DEPTH)]
    carried = dot(jnp.concatenate([a_right, a_left, row_255, row_256], axis=0), col_mat)
    four = lambda row: jnp.broadcast_to(row, (4, lanes_c))
    other = jnp.concatenate(
        [jnp.where(is_node, carried, 0.0), twice(cv, 2, lanes_c)]
        + [four(jnp.where(is_node, col_mat[n - 1 + i : n + i, :], 0.0)) for i in range(2)]
        + [four(jnp.where(iota((1, lanes_c), 1) == h, 1.0, 0.0)), jnp.zeros((4, lanes_c), jnp.float32)],
        axis=0,
    )
    own = jnp.concatenate([twice(rv, 2, lanes_c), twice(rv, 4, lanes_c)], axis=0)
    rest = jnp.concatenate([down_x[8:16], next_col_even, jnp.zeros((4, lanes_c), jnp.float32)], axis=0)
    lhs = jnp.concatenate([own, jnp.zeros((8, lanes_c), jnp.float32), rest], axis=0).T[0:rows_c]
    for d in range(DEPTH):
        u1[d] = base[d] + dot(lhs, jnp.where(iota((40, lanes_c), 0) % 4 == d, other, 0.0))
        w1[d] = detail(u1[d])

    n, h, g = n0 // 2, n0 // 4, n0 // 8
    lane = iota((8, 128), 1)
    ways = jnp.concatenate([rv[8:16, 0:256], row_table("taken")[:, 0:256]], axis=0).T
    functionals = jnp.concatenate([ways[:, 0:2], ways[:, 4:8]], axis=1)
    of_w = dot(row_sums([w1[d] for d in range(DEPTH)], functionals, 6), col_table("mat1"))
    taken = row_sums([u1[d] for d in range(DEPTH)], ways[:, 8:12], 4)
    of_next = of_w[8:24] + pick_dot(taken, selection(n, last_y))
    after = col_table("after")
    of_second = dot(jnp.concatenate([of_next[0:8], of_next[8:16]], axis=1), after[0:256])
    is_c = (lane == h + 1) | (lane == h + 2)
    sent = of_w[0:8] + pltpu.roll(of_second, h + 3, 1)
    for i in range(2):
        sent += pltpu.roll(jnp.where(is_c, of_w[8 + 8 * i : 16 + 8 * i], 0.0), g + 5 + 2 * i, 1)
    late_rows, late_own = col_table("late"), row_table("late_own")
    late_ends = [dot(late_own[:, 0:8], late_rows[16 + 8 * i : 24 + 8 * i]) for i in range(2)]
    late_table = row_table("late")

    pltpu.make_async_copy(yr0, yr0, y_recv.at[0]).wait()
    ends = []
    for value in gather(yr0, col_v, col_places, gy_n):
        tail = line(jnp.where(lane4 == layer, jnp.broadcast_to(value[4:5], (4, 128)), 0.0), 1.0)
        ends.append(jnp.concatenate([value[0:4], jnp.where(lane4 == 0, tail, 0.0)], axis=1))
    c_right, c_left = ends
    c_right += cv[28:29, n0 + 1 : n0 + 2] * (a_right[:, n0 + 1 : n0 + 2] * p_r + a_left[:, n0 + 1 : n0 + 2] * p_l)
    inner = INNER.get(gy_n, 1)
    near = inner - 1 + (gy_n - inner) * ((gy % inner + 1) // inner)
    told = jnp.where(last_y, 0.0, jnp.broadcast_to(yr0[near - 1, 4:5, :], (4, 128)))
    told = [line(jnp.where(lane4 == 4 * (i + 1) + layer, told, 0.0), 1.0) for i in range(4)]
    carries = jnp.concatenate([c_right, c_left], axis=0)
    scalars = dot(carries, late_table)
    change = []
    for x_way in range(2):
        part = jnp.zeros((4, 128), jnp.float32)
        for m in range(8):
            for way in range(2):
                scalar = scalars[4 * way : 4 * way + 4, 2 * m + x_way : 2 * m + x_way + 1]
                part += scalar * late_rows[8 * way + m : 8 * way + m + 1]
        for i in range(4):
            row = 2 * x_way + i % 2
            part += told[i] * late_ends[i // 2][row : row + 1]
        change.append(part)
    sent = sent + jnp.concatenate(change, axis=0)
    xs1[...] = sent
    xr1[0] = sent
    send_same(x_peers, xs1, xr1, x_send.at[1], x_recv.at[1])
    ends_y = [jnp.where(is_node, col_mat[n0 - 1 + i : n0 + i, :], 0.0) for i in range(2)]
    late = jnp.concatenate([told[i] * ends_y[0] + told[2 + i] * ends_y[1] for i in range(2)], axis=0)
    lhs = jnp.concatenate([carries, twice(rv, 2, lanes_c)], axis=0).T[0:rows_c]
    other = jnp.concatenate([twice(cv, 2, lanes_c), late], axis=0)
    for d in range(DEPTH):
        u1[d] = u1[d] + dot(lhs, jnp.where(iota((16, lanes_c), 0) % 4 == d, other, 0.0))
        w1[d] = detail(u1[d])
    base1, solved1 = local_level(1, n, u1, w1)
    cols = jnp.zeros((padded_rows(h), 128), jnp.float32)
    spot = iota(cols.shape, 1)
    for d in range(DEPTH):
        for way in range(2):
            cols = jnp.where(spot == 4 * way + d, solved1[d][:, h + 1 + way : h + 2 + way], cols)
            cols = jnp.where(spot == 8 + 4 * way + d, line(base1[d], cv[16 + way : 17 + way, 0:128]), cols)
            cols = jnp.where(spot == 16 + 4 * way + d, line(base1[d], cv[12 + way : 13 + way, 0:128]), cols)
    cols = jnp.concatenate([cols, jnp.zeros((128 - padded_rows(h), 128), jnp.float32)], axis=0).T
    row_after = row_table("after")
    cols1, cols2 = cols[0:8], dot(jnp.concatenate([cols[8:16], cols[16:24]], axis=1), row_after[0:256])
    others = xr1.at[pl.ds(1, gx_n - 1)]
    pltpu.make_async_copy(others, others, x_recv.at[1]).wait()
    got = dot(row_table("join")[:, 0 : gx_n * 8], xr1[...].reshape(gx_n * 8, 128))
    a_1 = got[0:8]
    a_2 = pltpu.roll(got[24:32], 128 - (h + 3), 1) + dot(
        jnp.concatenate([got[8:16], got[16:24]], axis=1), after[0:256]
    )
    msg, msg2, hs = [], [], []
    for way in range(2):
        msg.append(cols1[4 * way : 4 * way + 4] + outer(a_1[:, h + 1 + way : h + 2 + way], rv, 10, 128))
        row = outer(line(a_1, cv[16 + way : 17 + way, 0:128]), rv, 20, 128)
        row += outer(line(a_1, cv[12 + way : 13 + way, 0:128]), rv, 22, 128)
        row += outer(a_2[:, g + 1 + way : g + 2 + way], rv, 18, 128)
        msg2.append(cols2[4 * way : 4 * way + 4] + row)
        block = jnp.zeros((4, 128), jnp.float32)
        for i in range(2):
            at = h + g + 6 + 2 * i + way
            h_col = got[24:32, at : at + 1] + got[8 + 8 * i : 16 + 8 * i, h + 1 + way : h + 2 + way]
            for x_way in range(2):
                block += jnp.where(iota((4, 128), 1) == h + 1 + 2 * i + x_way, h_col[4 * x_way : 4 * x_way + 4], 0.0)
        hs.append(block)
    sent = jnp.concatenate(msg, axis=0) + pltpu.roll(jnp.concatenate(msg2, axis=0), h + 5, 1)
    sent += jnp.concatenate(hs, axis=0)
    ys1[...] = sent
    yr1[0] = sent
    send_same(y_peers, ys1, yr1, y_send.at[1], y_recv.at[1])
    down_turned = jnp.concatenate([col_255, col_255], axis=0).T[0:n0]
    is_last = iota((n0, 128), 1) == 127
    for d in range(DEPTH):
        out_v[d, 0] = w0[d, :, 0:128]
        out_v[d, 1] = w0[d, :, 128:256] + jnp.where(is_last, down_turned[:, d : d + 1], 0.0)
        for j in range(2):
            tail = iota((8, 128), 0) == 7
            fix = row_255[d : d + 1, 128 * j : 128 * j + 128]
            out_v[d, j, n0 - 8 : n0, :] = out_v[d, j, n0 - 8 : n0, :] + jnp.where(tail, fix, 0.0)
    base2, _ = local_level(2, h, base1, [detail(base1[d]) for d in range(DEPTH)])
    spread_out([w1[d] for d in range(DEPTH)], n, 256, 2, 2)
    beside = lambda value: jnp.concatenate([value[128 * i : 128 * i + 128] for i in range(3)], axis=1)
    nodes_1 = lambda value: jnp.where(lane <= h, value, 0.0)
    nodes_2 = lambda value: jnp.where(lane <= g, value, 0.0)
    other1 = jnp.concatenate([nodes_1(a_1), twice(cv, 10, 128)], axis=0)
    across = dot(a_1, beside(after))
    other2 = jnp.concatenate(
        [nodes_2(across[:, 256:384]), nodes_2(across[:, 0:128]), nodes_2(across[:, 128:256]), nodes_2(a_2)]
        + [twice(cv, row, 128) for row in (24, 20, 22, 18)],
        axis=0,
    )
    own = jnp.concatenate([twice(rv, row, 128) for row in (24, 20, 22, 18)], axis=0)
    row_after = beside(row_after)
    others = yr1.at[pl.ds(1, gy_n - 1)]
    pltpu.make_async_copy(others, others, y_recv.at[1]).wait()
    got = dot(col_table("join"), yr1[...].reshape(gy_n * 8, 128))
    down = dot(got[0:24], row_after)
    c_2 = nodes_2(pltpu.roll(got[24:32], 128 - (h + 5), 1) + down[8:16, 0:128] + down[16:24, 128:256])
    lhs = jnp.concatenate([own, down[0:8, 256:384], down[0:8, 0:128], down[0:8, 128:256], c_2], axis=0)
    lhs = jnp.concatenate([lhs, jnp.zeros_like(lhs)], axis=0).T[0 : padded_rows(g), 0:64]
    lhs1 = jnp.concatenate([twice(rv, 10, 128), nodes_1(got[0:8])], axis=0).T[0 : padded_rows(h)]
    details, last = [], []
    for d in range(DEPTH):
        last.append(base2[d] + dot(lhs, jnp.where(iota((64, 128), 0) % 4 == d, other2, 0.0)))
        nodes = base1[d] + dot(lhs1, jnp.where(iota((16, 128), 0) % 4 == d, other1, 0.0))
        details.append(detail(nodes))
    spread_out(details, h, 128, 4, 2)
    spread_out(last, g, 128, 8, 2)
    for d in range(DEPTH):
        out[d] = jnp.concatenate([out_v[d, j] for j in range(n0 // 128)], axis=1)

    for i, copy in enumerate(halos):
        copy.wait_send()
    pltpu.make_async_copy(xr0, xr0, x_send.at[0]).wait()
    pltpu.make_async_copy(yr0, yr0, y_send.at[0]).wait()
    others = xr1.at[pl.ds(1, gx_n - 1)]
    pltpu.make_async_copy(others, others, x_send.at[1]).wait()
    others = yr1.at[pl.ds(1, gy_n - 1)]
    pltpu.make_async_copy(others, others, y_send.at[1]).wait()


def even_rows(tall_v, value, rows_c):
    rows, lanes = value.shape
    half = rows // 2
    parts = []
    for j in range(lanes // 128):
        tall_v[j, 0:rows] = value[:, 128 * j : 128 * j + 128]
        part = tall_v[j, pl.ds(0, half, stride=2), :]
        parts.append(jnp.concatenate([part, jnp.zeros((rows_c - half, 128), jnp.float32)], axis=0))
    return jnp.concatenate(parts, axis=1)


def add_rows(ref, d, value, stride):
    place = pl.ds(0, value.shape[0], stride=stride)
    for j in range(ref.shape[1]):
        ref[d, j, place, :] = ref[d, j, place, :] + value[:, 128 * j : 128 * j + 128]


def shards(salinity):
    gx_n, gy_n = lax.axis_size("gx"), lax.axis_size("gy")
    _, nx, ny = salinity.shape
    n0 = nx
    (row_tab, row_places), (col_tab, col_places) = tables(nx * gx_n, ny * gy_n, gx_n, gy_n)
    vmem = lambda *shape: pltpu.VMEM(shape, jnp.float32)
    dma = lambda count: pltpu.SemaphoreType.DMA((count,))
    wide = padded_lanes(n0)
    second = vmem(DEPTH, padded_rows(n0 // 2), padded_lanes(n0 // 2))
    scratch = [vmem(DEPTH, n0 // 128, n0, 128), vmem(DEPTH, 2, n0, 128), second, vmem(DEPTH, n0, n0), second, vmem(2, padded_rows(n0), 128)]
    scratch += [vmem(*row_tab.shape[1:]), vmem(*col_tab.shape[1:])]
    scratch += [vmem(DEPTH, n0), vmem(DEPTH, n0), vmem(DEPTH, 128)] * 2
    scratch += [vmem(3, DEPTH, wide), vmem(gx_n - 1, DEPTH, wide)]
    scratch += [vmem(3, DEPTH + 1, n0 // 2), vmem(gy_n - 1, DEPTH + 1, n0 // 2)]
    scratch += [vmem(8, 128), vmem(gx_n, 8, 128), vmem(8, 128), vmem(gy_n, 8, 128)]
    scratch += [dma(4), dma(3), dma(3), dma(2), dma(2), dma(2), dma(2)]
    anywhere = pl.BlockSpec(memory_space=pl.ANY)
    out = pl.pallas_call(
        functools.partial(kernel, gx_n, gy_n, n0, row_places, col_places),
        out_shape=jax.ShapeDtypeStruct(salinity.shape, jnp.float32),
        in_specs=[anywhere] * 3,
        out_specs=pl.BlockSpec(memory_space=pltpu.VMEM),
        scratch_shapes=scratch,
        compiler_params=pltpu.CompilerParams(
            collective_id=0, has_side_effects=True, vmem_limit_bytes=VMEM_LIMIT
        ),
    )(salinity, row_tab, col_tab)
    return out


def solution(mesh):
    placed = P(None, "gx", "gy")
    return jax.shard_map(shards, mesh=mesh, in_specs=(placed,), out_specs=placed, check_vma=False)
```
